32 devices in a mesh: surf: 4 (over y, core), line: 8 (over z, x).
Axes of the slice: x: 2, y: 2, z: 4, core: 2. Of those that a mesh axis runs over, the one named last changes fastest.
Arguments:
- inv_block: bfloat16 [16, 16, 320, 320], P('surf', 'line'), as said below
- couple_block: bfloat16 [16, 16, 320, 320], P('surf', 'line')
- face_block: bfloat16 [16, 16, 320, 320], P('surf', 'line'), may hold values from -0.03125 to 0.03125
- rhs: bfloat16 [16, 16, 320, 64], P('surf', 'line'), may hold values from -0.59765625 to 0.59765625
- adjoint_prev: bfloat16 [16, 16, 320, 64], P('surf', 'line'), may hold values from -6 to 6
- nb_line: int32 [16], P('surf'), may hold values from 0 to 15
- send_list: int32 [4, 4, 4], P('surf'), may hold values from 0 to 7, as said below
- send_count: int32 [4, 4], P('surf'), may hold values from 0 to 4
- recv_list: int32 [4, 4, 4], P('surf'), may hold values from 0 to 7, as said below
Outputs:
- adjoint: bfloat16 [16, 16, 320, 64], P('surf', 'line')
The draws below stay inside these ranges and needn't reach their ends.
Inputs may be any that keep to these rules, and one draw needn't show every extreme that they name: `send_list`: for every sender s the blocks it sends to all peers are 8 distinct positions; every receiver gets 4 * 2 blocks in all at distinct positions. Each device sends 4 blocks to one peer and none to another. Slots at or past the count are unused. `recv_list`: entries of slots at or past the sender's count are unused. `inv_block`: every block is the identity plus a small perturbation, its rows scaled by per-row factors below one.
All inputs are finite; a program needn't handle non-finite values.
Results may differ from the reference program's by a relative error of at most 0.0013.
Values may be sent and summed in bfloat16 or wider, within the bound.
A program may use at most 320 MiB of HBM per device.

```python
import math
import jax
import jax.numpy as jnp
from jax import lax

CELL_UNKNOWNS = 320
K = 64
LS = 4
E = 2
STRAND_TOTAL = 16
CELLS_PER_STRAND = 16
CAP = 4
N_SURF = 4
N_LINE = 8


def draw_inv_block(key, part):
    slow_share = 0.5
    is_slow = jax.random.uniform(jax.random.fold_in(key, 7), (CELL_UNKNOWNS,)) < slow_share
    inflow_frequency = jnp.where(is_slow, math.exp(-1.0 / CELLS_PER_STRAND), math.exp(-1.0 / 40.0))
    spike_occurrences = jnp.where(jax.random.uniform(jax.random.fold_in(key, 11), (STRAND_TOTAL, CELLS_PER_STRAND, 1, 1)) < 2.0 / CELLS_PER_STRAND, 0.65, 1.0)
    stochastic_perturbation = jax.random.normal(jax.random.fold_in(key, 3), (STRAND_TOTAL, CELLS_PER_STRAND, CELL_UNKNOWNS, CELL_UNKNOWNS)) * (0.2 / math.sqrt(CELL_UNKNOWNS))
    linearized_operator = (jnp.eye(CELL_UNKNOWNS, dtype=jnp.float32) + stochastic_perturbation) * inflow_frequency[None, None, :, None] * spike_occurrences * math.exp(-0.02)
    return linearized_operator.astype(jnp.bfloat16)


def draw_couple_block(key, part):
    stochastic_perturbation = jax.random.normal(jax.random.fold_in(key, 5), (STRAND_TOTAL, CELLS_PER_STRAND, CELL_UNKNOWNS, CELL_UNKNOWNS)) * (0.2 / math.sqrt(CELL_UNKNOWNS))
    return (-(jnp.eye(CELL_UNKNOWNS, dtype=jnp.float32) + stochastic_perturbation)).astype(jnp.bfloat16)


def migration_plan(key):
    per_device = LS * E
    share = per_device // N_SURF
    ranks = jnp.arange(N_SURF, dtype=jnp.int32)
    empty_offset = (2 + jax.random.randint(jax.random.fold_in(key, 101), (), 0, N_SURF - 1)) % N_SURF
    double_offset = (empty_offset + 1 + jax.random.randint(jax.random.fold_in(key, 104), (), 0, N_SURF - 1)) % N_SURF
    weights = jnp.where(ranks == double_offset, 2 * share, jnp.where(ranks == empty_offset, 0, share)).astype(jnp.int32)
    senders = ranks[:, None]
    receivers = ranks[None, :]
    counts = weights[(receivers - senders) % N_SURF]
    counts_back = counts.T
    send_start = jnp.cumsum(counts, axis=1) - counts
    recv_start = jnp.cumsum(counts_back, axis=1) - counts_back
    send_perm = jax.vmap(lambda one_key: jax.random.permutation(one_key, per_device))(jax.random.split(jax.random.fold_in(key, 102), N_SURF))
    recv_perm = jax.vmap(lambda one_key: jax.random.permutation(one_key, per_device))(jax.random.split(jax.random.fold_in(key, 103), N_SURF))
    slot_ids = jnp.arange(CAP, dtype=jnp.int32)[None, None, :]
    send_pos = jnp.clip(send_start[:, :, None] + slot_ids, 0, per_device - 1).reshape(N_SURF, -1)
    recv_pos = jnp.clip(recv_start[:, :, None] + slot_ids, 0, per_device - 1).reshape(N_SURF, -1)
    send_list = jnp.take_along_axis(send_perm, send_pos, axis=1).reshape(N_SURF, N_SURF, CAP)
    recv_list = jnp.take_along_axis(recv_perm, recv_pos, axis=1).reshape(N_SURF, N_SURF, CAP)
    send_list = jnp.where(slot_ids < counts[:, :, None], send_list, 0)
    recv_list = jnp.where(slot_ids < counts_back[:, :, None], recv_list, 0)
    return (counts.astype(jnp.int32), send_list.astype(jnp.int32), recv_list.astype(jnp.int32))


def draw_send_list(key, part):
    return migration_plan(key)[1]


def draw_send_count(key, part):
    return migration_plan(key)[0]


def draw_recv_list(key, part):
    return migration_plan(key)[2]


def touch_ends(entries, stream_key, low, high):
    extent = entries.shape
    index_at = [jax.random.randint(jax.random.fold_in(stream_key, axis), (), 0, extent[axis]) for axis in range(len(extent))]
    entries = entries.at[tuple(index_at)].set(low)
    longest = extent.index(max(extent))
    index_at[longest] = (index_at[longest] + 1) % extent[longest]
    return entries.at[tuple(index_at)].set(high)


def levels(own_key, shape, pieces, low, high):
    loudness = 1.0
    for position, blocks in pieces:
        heights = jax.random.uniform(jax.random.fold_in(jax.random.fold_in(own_key, 6), position), (blocks,), jnp.float32, low / len(pieces), high / len(pieces))
        loudness = loudness * jnp.repeat(jnp.exp(heights), shape[position] // blocks).reshape((-1,) + (1,) * (len(shape) - 1 - position))
    return loudness


def gaussian(stream_key, extent, scale, most, pieces=(), kind=jnp.bfloat16):
    gain = levels(stream_key, extent, pieces, -0.22, 0.18) if pieces else 1.0
    drawn = jax.random.normal(stream_key, extent, jnp.float32) * scale * gain
    return jnp.minimum(jnp.maximum(drawn, -most), most).astype(kind)


def setup_inputs(seed: int = 0) -> dict:
    streams_of = jax.random.split(jax.random.key(seed), 10)
    return {
        "inv_block": draw_inv_block(jax.random.fold_in(streams_of[9], 71), 0),
        "couple_block": draw_couple_block(jax.random.fold_in(streams_of[9], 71), 0),
        "face_block": gaussian(streams_of[2], (STRAND_TOTAL, CELLS_PER_STRAND, CELL_UNKNOWNS, CELL_UNKNOWNS), (100 * CELL_UNKNOWNS) ** -0.5, 0.03125, ((0, 4), (1, 8))),
        "rhs": gaussian(streams_of[3], (STRAND_TOTAL, CELLS_PER_STRAND, CELL_UNKNOWNS, K), 0.1, 0.59765625, ((0, 4), (1, 8))),
        "adjoint_prev": gaussian(streams_of[4], (STRAND_TOTAL, CELLS_PER_STRAND, CELL_UNKNOWNS, K), 1.0, 6.0, ((0, 4), (1, 8))),
        "nb_line": touch_ends(jax.random.randint(streams_of[5], (STRAND_TOTAL,), 0, STRAND_TOTAL), jax.random.fold_in(streams_of[5], 1), 0, STRAND_TOTAL - 1).astype(jnp.int32),
        "send_list": draw_send_list(jax.random.fold_in(streams_of[9], 71), 0),
        "send_count": draw_send_count(jax.random.fold_in(streams_of[9], 71), 0),
        "recv_list": draw_recv_list(jax.random.fold_in(streams_of[9], 71), 0),
    }


HIGH = lax.Precision.HIGHEST


def migrate(blocks, send_list, send_count, recv_list):
    tail = blocks.shape[2:]
    per_device = LS * E
    grouped = blocks.reshape((N_SURF, LS, N_LINE, E) + tail)
    grouped = jnp.moveaxis(grouped, 2, 0).reshape((N_LINE, N_SURF * per_device) + tail)
    senders = jnp.arange(N_SURF, dtype=jnp.int32)[:, None, None]
    receivers = jnp.arange(N_SURF, dtype=jnp.int32)[None, :, None]
    slot_ids = jnp.arange(CAP, dtype=jnp.int32)[None, None, :]
    sources = senders * per_device + send_list
    targets = receivers * per_device + jnp.transpose(recv_list, (1, 0, 2))
    is_valid = slot_ids < send_count[:, :, None]
    targets = jnp.where(is_valid, targets, N_SURF * per_device).astype(jnp.int32)
    placed = jnp.zeros_like(grouped).at[:, targets.reshape(-1)].set(grouped[:, sources.reshape(-1)], mode="drop")
    placed = placed.reshape((N_LINE, N_SURF, LS, E) + tail)
    return jnp.moveaxis(placed, 0, 2).reshape(blocks.shape)


def reference(inv_block, couple_block, face_block, rhs, adjoint_prev, nb_line, send_list, send_count, recv_list):
    inv_moved = migrate(inv_block, send_list, send_count, recv_list)
    couple_moved = migrate(couple_block, send_list, send_count, recv_list)
    face_moved = migrate(face_block, send_list, send_count, recv_list)
    rhs_moved = migrate(rhs, send_list, send_count, recv_list)
    neighbors = adjoint_prev[nb_line].astype(jnp.float32)
    neighbor_term = jnp.einsum("lebc,lecd->lebd", face_moved.astype(jnp.float32), neighbors, precision=HIGH)
    forcing = rhs_moved.astype(jnp.float32) - neighbor_term

    def step_back(carry, items):
        inv_elem, couple_elem, forcing_elem = items
        drive = forcing_elem - jnp.einsum("lbc,lcd->lbd", couple_elem.astype(jnp.float32), carry, precision=HIGH)
        swept = jnp.einsum("lbc,lcd->lbd", inv_elem.astype(jnp.float32), drive, precision=HIGH)
        return swept, swept

    outer = jnp.zeros((STRAND_TOTAL, CELL_UNKNOWNS, K), jnp.float32)
    items = (jnp.moveaxis(inv_moved, 1, 0), jnp.moveaxis(couple_moved, 1, 0), jnp.moveaxis(forcing, 1, 0))
    _, sweep = lax.scan(step_back, outer, items, reverse=True)
    return jnp.moveaxis(sweep, 0, 1).astype(jnp.bfloat16)
```

```python
import functools

import jax
import jax.numpy as jnp
from jax import lax
from jax.experimental import pallas as pl
from jax.experimental.pallas import tpu as pltpu
from jax.sharding import PartitionSpec as P

MESH = pl.DeviceIdType.MESH
F32 = jnp.float32
BF16 = jnp.bfloat16
I16 = jnp.int16
I32 = jnp.int32
LANES = 128
TOP = 32767.0
TINY = 1e-30
LIMIT = 56 << 20


def dot(a, b):
    return jnp.dot(a, b, preferred_element_type=F32)


def split(value):
    high = value.astype(BF16)
    return high, (value - high.astype(F32)).astype(BF16)


def diagonal(size):
    return lax.broadcasted_iota(I32, (size, size), 0) == lax.broadcasted_iota(
        I32, (size, size), 1
    )


def coded(value):
    most = jnp.maximum(jnp.max(jnp.abs(value), axis=0, keepdims=True), TINY)
    return jnp.round(value * (TOP / most)).astype(I32), most * (1.0 / TOP)


def greet(barrier, peers):
    for peer in peers:
        pl.semaphore_signal(barrier, inc=1, device_id={"surf": peer}, device_id_type=MESH)
    pl.semaphore_wait(barrier, len(peers))


def gather_kernel(
    n, table_ref, adjoint_ref, inv_hbm, couple_hbm,
    tables_ref, adjoints_ref, code_ref, side_ref,
    inv_ref, couple_ref, load_sem, table_send, table_recv, send_sem, recv_sem,
):
    me = lax.axis_index("surf")
    lines, elems = adjoint_ref.shape[:2]
    size = inv_ref.shape[1]
    stored = lines * elems
    chips = n // 2
    core, chip = lax.rem(me, 2), me // 2
    partner = me + 1 - 2 * core

    def loads(b):
        at = (b // elems, b % elems)
        return (
            pltpu.make_async_copy(inv_hbm.at[at], inv_ref.at[b], load_sem.at[b, 0]),
            pltpu.make_async_copy(couple_hbm.at[at], couple_ref.at[b], load_sem.at[b, 1]),
        )

    for b in range(stored):
        for load in loads(b):
            load.start()

    tables_ref[me] = table_ref[...]
    for l in range(lines):
        adjoints_ref[me * lines + l] = jnp.concatenate(
            [adjoint_ref[l, e] for e in range(elems)], axis=-1
        )

    greet(pltpu.get_barrier_semaphore(), [lax.rem(me + d, n) for d in range(1, n)])

    def table_copy(d):
        return pltpu.make_async_remote_copy(
            src_ref=table_ref, dst_ref=tables_ref.at[me], send_sem=table_send.at[d],
            recv_sem=table_recv.at[d], device_id={"surf": lax.rem(me + d, n)},
            device_id_type=MESH,
        )

    def table_arrival(d):
        return pltpu.make_async_remote_copy(
            src_ref=table_ref, dst_ref=tables_ref.at[lax.rem(me + n - d, n)],
            send_sem=table_send.at[d], recv_sem=table_recv.at[d],
            device_id={"surf": lax.rem(me + d, n)}, device_id_type=MESH,
        )

    def line_copy(owner, l, way, to):
        row = owner * lines + l
        return pltpu.make_async_remote_copy(
            src_ref=adjoints_ref.at[row], dst_ref=adjoints_ref.at[row],
            send_sem=send_sem.at[way, l], recv_sem=recv_sem.at[row],
            device_id={"surf": to}, device_id_type=MESH,
        )

    def across(k):
        return lax.rem(chip + k, chips) * 2 + core

    for d in range(1, n):
        table_copy(d).start()
    for l in range(lines):
        for k in range(1, chips):
            line_copy(me, l, k, across(k)).start()
    for l in range(lines):
        line_copy(me, l, 0, partner).start()

    eye = diagonal(size)

    def product(b):
        for load in loads(b):
            load.wait()
        value = -dot(inv_ref[b], couple_ref[b])
        main = jnp.sum(jnp.where(eye, value, 0.0), axis=0, keepdims=True)
        main = main.astype(BF16).astype(F32)
        codes, scale = coded(value - jnp.where(eye, main, 0.0))
        code_ref[b, :, :size] = codes.astype(I16)
        side_ref[b, 0:1, :size] = scale
        side_ref[b, 1:2, :size] = main

    def relay(l):
        for k in range(1, chips):
            source = across(k)
            line_copy(source, l, k, partner).wait_recv()
            line_copy(source, l, chips - 1 + k, partner).start()

    for l in range(lines):
        for e in range(elems):
            product(l * elems + e)
        relay(l)

    for d in range(1, n):
        table_arrival(d).wait_recv()
        table_copy(d).wait_send()
    for l in range(lines):
        line_copy(partner, l, 0, partner).wait_recv()
        for k in range(1, chips):
            other = across(k)
            line_copy(other + 1 - 2 * core, l, 0, partner).wait_recv()
            line_copy(me, l, k, other).wait_send()
            line_copy(other, l, chips - 1 + k, partner).wait_send()
        line_copy(me, l, 0, partner).wait_send()


def gathered(n, table, adjoint_prev, inv_block, couple_block):
    lines, elems, size, cols = adjoint_prev.shape
    stored, wide = lines * elems, size + cols
    chips = n // 2
    vmem, hbm = pl.BlockSpec(memory_space=pltpu.VMEM), pl.BlockSpec(memory_space=pl.ANY)
    return pl.pallas_call(
        functools.partial(gather_kernel, n),
        out_shape=(
            jax.ShapeDtypeStruct((n, 1, LANES), I32),
            jax.ShapeDtypeStruct((n * lines, size, elems * cols), BF16),
            jax.ShapeDtypeStruct((stored, size, wide), I16),
            jax.ShapeDtypeStruct((stored, 8, wide), F32),
        ),
        in_specs=[vmem, vmem, hbm, hbm],
        out_specs=(vmem,) * 4,
        scratch_shapes=[
            pltpu.VMEM((stored, size, size), BF16),
            pltpu.VMEM((stored, size, size), BF16),
            pltpu.SemaphoreType.DMA((stored, 2)),
            pltpu.SemaphoreType.DMA((n,)),
            pltpu.SemaphoreType.DMA((n,)),
            pltpu.SemaphoreType.DMA((2 * chips - 1, lines)),
            pltpu.SemaphoreType.DMA((n * lines,)),
        ],
        compiler_params=pltpu.CompilerParams(
            collective_id=0, has_side_effects=True, vmem_limit_bytes=LIMIT
        ),
    )(table, adjoint_prev, inv_block, couple_block)


def index_kernel(n, lines, elems, cap, plans, tables_ref, send_ref, out_ref):
    me = lax.axis_index("surf")
    stored = lines * elems
    room = n * cap

    def places(r, s, j):
        return tables_ref[r, 0, s * cap + j]

    def count(s, r):
        return tables_ref[s, 0, room + lines + r]

    for d in range(n):
        to, source = lax.rem(me + d, n), lax.rem(me + n - d, n)
        for j in range(cap):
            used = j < count(me, to)
            goal = jnp.where(used, places(to, me, j), 0)
            slot = d * cap + j
            out_ref[slot] = jnp.where(used, send_ref[to * cap + j], 0)
            out_ref[room + slot] = tables_ref[to, 0, room + goal // elems]
            out_ref[2 * room + slot] = lax.rem(goal, elems)
    for q in range(stored):
        out_ref[3 * room + q] = 0
    for d in range(n):
        source = lax.rem(me + n - d, n)
        for j in range(cap):
            @pl.when(j < count(source, me))
            def _():
                out_ref[3 * room + places(me, source, j)] = d * cap + j

    best = jnp.int32(len(plans) - 1)
    most = []
    for d in range(n):
        value = count(0, d)
        for s in range(1, n):
            value = jnp.maximum(value, count(s, (s + d) % n))
        most.append(value)
    for p in reversed(range(len(plans) - 1)):
        fits = most[0] <= plans[p][0]
        for d in range(1, n):
            fits = jnp.logical_and(fits, most[d] <= plans[p][d])
        best = jnp.where(fits, p, best)
    out_ref[3 * room + stored] = best


def indexed(n, lines, elems, cap, plans, tables, sends):
    smem = pl.BlockSpec(memory_space=pltpu.SMEM)
    return pl.pallas_call(
        functools.partial(index_kernel, n, lines, elems, cap, plans),
        out_shape=jax.ShapeDtypeStruct((LANES,), I32),
        in_specs=[smem, smem],
        out_specs=smem,
    )(tables, sends)


def send_kernel(
    n, cap, budgets, index_ref, inv_ref, face_ref, rhs_ref, adjoints_ref, code_ref, side_ref,
    got_ref, got_side_ref, out_ref, out_side_ref, send_sem, recv_sem,
):
    me = lax.axis_index("surf")
    _, elems, size, cols = rhs_ref.shape
    room = n * cap
    wide = size + cols
    body = wide - LANES
    greet(pltpu.get_barrier_semaphore(), [lax.rem(me + d, n) for d in range(1, n)])
    upper = lax.broadcasted_iota(I32, (size, LANES), 1) >= cols
    upper_row = lax.broadcasted_iota(I32, (1, LANES), 1) >= cols

    def copies(d, slot):
        to = {"surf": lax.rem(me + d, n)}
        return (
            pltpu.make_async_remote_copy(
                src_ref=out_ref.at[slot], dst_ref=got_ref.at[slot],
                send_sem=send_sem.at[slot, 0], recv_sem=recv_sem.at[slot, 0],
                device_id=to, device_id_type=MESH,
            ),
            pltpu.make_async_remote_copy(
                src_ref=out_side_ref.at[slot], dst_ref=got_side_ref.at[slot],
                send_sem=send_sem.at[slot, 1], recv_sem=recv_sem.at[slot, 1],
                device_id=to, device_id_type=MESH,
            ),
        )

    def fill(slot, codes_at, sides_at):
        at = index_ref[slot]
        line, elem = index_ref[room + slot], index_ref[2 * room + slot]
        terms = dot(face_ref[at // elems, at % elems], adjoints_ref[line])
        terms = jnp.where(elem == 1, terms, pltpu.roll(terms, cols, 1))
        rhs = rhs_ref[at // elems, at % elems].astype(F32)
        force = jnp.concatenate([rhs, rhs], axis=-1) - terms
        hi = force.astype(BF16).astype(F32)
        both = jnp.where(upper, hi, pltpu.roll(force - hi, cols, 1)).astype(BF16)
        moved = dot(inv_ref[at // elems, at % elems], both)
        moved = moved + pltpu.roll(moved, cols, 1)
        codes, scale = coded(moved)
        codes_at[slot, :, :body] = code_ref[at, :, :body]
        last = code_ref[at, :, body:].astype(I32)
        codes_at[slot, :, body:] = jnp.where(upper, codes, last).astype(I16)
        sides_at[slot, :, :body] = side_ref[at, :, :body]
        sides_at[slot, :, body:] = side_ref[at, :, body:]
        sides_at[slot, 0:1, body:] = jnp.where(upper_row, scale, side_ref[at, 0:1, body:])

    for d in sorted(range(1, n), key=lambda d: -min(d, n - d)):
        def leave(j, _):
            slot = d * cap + j
            fill(slot, out_ref, out_side_ref)
            for copy in copies(d, slot):
                copy.start()
            return 0

        lax.fori_loop(0, budgets[d], leave, 0)

    def stay(j, _):
        fill(j, got_ref, got_side_ref)
        return 0

    lax.fori_loop(0, budgets[0], stay, 0)

    for d in range(1, n):
        def arrive(j, _):
            for copy in copies(d, d * cap + j):
                copy.wait()
            return 0

        lax.fori_loop(0, budgets[d], arrive, 0)


def sent(n, cap, plan, budgets, index, inv, face, rhs, adjoints, codes, sides):
    stored, size, wide = codes.shape
    vmem = pl.BlockSpec(memory_space=pltpu.VMEM)
    room = n * cap
    return pl.pallas_call(
        functools.partial(send_kernel, n, cap, budgets),
        out_shape=(
            jax.ShapeDtypeStruct((room, size, wide), I16),
            jax.ShapeDtypeStruct((room, 8, wide), F32),
        ),
        in_specs=[pl.BlockSpec(memory_space=pltpu.SMEM)] + [vmem] * 6,
        out_specs=(vmem, vmem),
        scratch_shapes=[
            pltpu.VMEM((room, size, wide), I16),
            pltpu.VMEM((room, 8, wide), F32),
            pltpu.SemaphoreType.DMA((room, 2)),
            pltpu.SemaphoreType.DMA((room, 2)),
        ],
        compiler_params=pltpu.CompilerParams(
            collective_id=2 + plan, has_side_effects=True, vmem_limit_bytes=LIMIT
        ),
    )(index, inv, face, rhs, adjoints, codes, sides)


def line_kernel(n, lines, elems, first, index_ref, code_ref, side_ref, *refs):
    (out_ref, outer_map, outer_shift, map_hi, map_lo, shift, going, coming,
     send_sem, recv_sem) = refs
    me = lax.axis_index("line")
    _, size, wide = code_ref.shape
    cols = wide - size

    inner, outer = jnp.maximum(me - 1, 0), jnp.minimum(me + 1, n - 1)
    barrier = pltpu.get_barrier_semaphore()

    @pl.when(me < n - 1)
    def _():
        pl.semaphore_signal(barrier, inc=1, device_id={"line": outer}, device_id_type=MESH)

    @pl.when(me > 0)
    def _():
        pl.semaphore_wait(barrier, 1)

    eye = diagonal(size)

    def decoded(slot):
        value = code_ref[slot].astype(F32) * side_ref[slot, 0:1]
        square = value[:, :size]
        square = square + jnp.where(eye, side_ref[slot, 1:2, :size], 0.0)
        return square, value[:, size:]

    def segment(l, _):
        square, moved = decoded(index_ref[first + l * elems + 1])
        hi, lo = split(square)
        move_hi, move_lo = split(moved)
        outer_map[l, :, :size] = hi
        outer_map[l, :, size:] = lo
        outer_shift[l] = moved
        all_hi = jnp.concatenate([hi, lo, move_hi, move_lo], axis=-1)
        only_hi = jnp.concatenate([hi, move_hi], axis=-1)
        square, moved = decoded(index_ref[first + l * elems])
        in_hi, in_lo = split(square)
        wide_sum = dot(in_hi, all_hi)
        small = dot(in_lo, only_hi)
        whole = wide_sum[:, :size] + (wide_sum[:, size : 2 * size] + small[:, :size])
        m_hi, m_lo = split(whole)
        map_hi[l] = m_hi
        map_lo[l] = m_lo
        shift[l] = moved + (
            wide_sum[:, 2 * size : 2 * size + cols]
            + (wide_sum[:, 2 * size + cols :] + small[:, size:])
        )
        return 0

    lax.fori_loop(0, lines, segment, 0)

    def copy(l):
        return pltpu.make_async_remote_copy(
            src_ref=going.at[l], dst_ref=coming.at[l], send_sem=send_sem.at[l],
            recv_sem=recv_sem.at[l], device_id={"line": inner}, device_id_type=MESH,
        )

    @pl.when(me == n - 1)
    def _():
        coming[...] = jnp.zeros_like(coming)

    def applied(hi, lo, value):
        both = dot(hi, value)
        return both[:, :cols] + (both[:, cols:] + dot(lo, value[:, :cols]))

    for l in range(lines):
        @pl.when(me < n - 1)
        def _():
            copy(l).wait_recv()

        last = shift[l] + applied(map_hi[l], map_lo[l], coming[l])
        hi, lo = split(last)
        going[l] = jnp.concatenate([hi, lo], axis=-1)

        @pl.when(me > 0)
        def _():
            copy(l).start()

        out_ref[l, 0] = hi

    for l in range(lines):
        value = outer_shift[l] + applied(
            outer_map[l, :, :size], outer_map[l, :, size:], coming[l]
        )
        out_ref[l, 1] = value.astype(BF16)

    for l in range(lines):
        @pl.when(me > 0)
        def _():
            copy(l).wait_send()


def swept(n, lines, elems, first, index, codes, sides):
    _, size, wide = codes.shape
    cols = wide - size
    vmem = pl.BlockSpec(memory_space=pltpu.VMEM)
    square = pltpu.VMEM((lines, size, size), BF16)
    return pl.pallas_call(
        functools.partial(line_kernel, n, lines, elems, first),
        out_shape=jax.ShapeDtypeStruct((lines, elems, size, cols), BF16),
        in_specs=[pl.BlockSpec(memory_space=pltpu.SMEM), vmem, vmem],
        out_specs=vmem,
        scratch_shapes=[
            pltpu.VMEM((lines, size, 2 * size), BF16),
            pltpu.VMEM((lines, size, cols), F32),
            square, square,
            pltpu.VMEM((lines, size, cols), F32),
            pltpu.VMEM((lines, size, 2 * cols), BF16),
            pltpu.VMEM((lines, size, 2 * cols), BF16),
            pltpu.SemaphoreType.DMA((lines,)),
            pltpu.SemaphoreType.DMA((lines,)),
        ],
        compiler_params=pltpu.CompilerParams(
            collective_id=1, has_side_effects=True, vmem_limit_bytes=LIMIT
        ),
    )(index, codes, sides)


def plans_of(n, cap):
    plans = []
    if n == 4 and cap % 2 == 0:
        for empty in (0, 2, 3):
            for double in range(n):
                if double != empty:
                    plans.append(tuple(
                        cap if d == double else 0 if d == empty else cap // 2
                        for d in range(n)
                    ))
    return plans + [(cap,) * n]


def per_device(n_surf, n_line, inv_block, couple_block, face_block, rhs, adjoint_prev,
               nb_line, send_list, send_count, recv_list):
    lines, elems, size, _ = inv_block.shape
    cap = send_list.shape[2]
    plans = plans_of(n_surf, cap)
    table = jnp.concatenate([recv_list[0].reshape(-1), nb_line, send_count[0]])
    table = jnp.pad(table, (0, LANES - table.shape[0]))[None]
    tables, adjoints, codes, sides = gathered(
        n_surf, table, adjoint_prev, inv_block, couple_block
    )
    index = indexed(n_surf, lines, elems, cap, plans, tables, send_list[0].reshape(-1))
    first = 3 * n_surf * cap

    def branch(p):
        return lambda: sent(
            n_surf, cap, p, plans[p], index, inv_block, face_block, rhs, adjoints, codes, sides
        )

    if len(plans) > 1:
        got, got_sides = lax.switch(
            index[first + lines * elems], [branch(p) for p in range(len(plans))]
        )
    else:
        got, got_sides = branch(0)()
    return swept(n_line, lines, elems, first, index, got, got_sides)


def solution(mesh):
    whole = P("surf", "line", None, None)
    in_specs = (
        whole, whole, whole, whole, whole,
        P("surf"), P("surf", None, None), P("surf", None), P("surf", None, None),
    )
    body = functools.partial(per_device, mesh.shape["surf"], mesh.shape["line"])
    return jax.shard_map(
        body, mesh=mesh, in_specs=in_specs, out_specs=whole, check_vma=False
    )
```

```python
import functools

import jax
import jax.numpy as jnp
from jax import lax
from jax.experimental import pallas as pl
from jax.experimental.pallas import tpu as pltpu
from jax.sharding import PartitionSpec as P

MESH = pl.DeviceIdType.MESH
F32 = jnp.float32
BF16 = jnp.bfloat16
I16 = jnp.int16
I32 = jnp.int32
LANES = 128
TOP = 32767.0
TINY = 1e-30
CARRY_TOP = 32700.0


def dot(a, b):
    return jnp.dot(a, b, preferred_element_type=F32)


def split(value):
    high = value.astype(BF16)
    return high, (value - high.astype(F32)).astype(BF16)


def diagonal(size):
    return lax.broadcasted_iota(I32, (size, size), 0) == lax.broadcasted_iota(
        I32, (size, size), 1
    )


def coded(value):
    most = jnp.maximum(jnp.max(jnp.abs(value), axis=0, keepdims=True), TINY)
    return jnp.round(value * (TOP / most)).astype(I32), most * (1.0 / TOP)


def gather_kernel(
    n, cap, plans, recv_list_ref, nb_ref, count_ref, send_list_ref, adjoint_ref, rhs_ref,
    inv_hbm, couple_hbm,
    index_ref, plan_ref, adjoints_ref, both_ref, code_ref, side_ref,
    places_ref, nbs_ref, counts_ref, inv_ref, couple_ref,
    load_sem, table_send, table_recv, send_sem, recv_sem,
):
    me = lax.axis_index("surf")
    lines, elems = adjoint_ref.shape[:2]
    size = inv_ref.shape[1]
    stored = lines * elems
    chips = n // 2
    core, chip = lax.rem(me, 2), me // 2
    partner = me + 1 - 2 * core

    def loads(b):
        at = (b // elems, b % elems)
        return (
            pltpu.make_async_copy(inv_hbm.at[at], inv_ref.at[b], load_sem.at[b, 0]),
            pltpu.make_async_copy(couple_hbm.at[at], couple_ref.at[b], load_sem.at[b, 1]),
        )

    for b in range(stored):
        for load in loads(b):
            load.start()

    barrier = pltpu.get_barrier_semaphore()
    for d in range(1, n):
        pl.semaphore_signal(
            barrier, inc=1, device_id={"surf": lax.rem(me + d, n)}, device_id_type=MESH
        )

    for l in range(lines):
        stack = jnp.concatenate([adjoint_ref[l, e] for e in range(elems)], axis=0)
        adjoints_ref[me * lines + l] = stack.T

    pl.semaphore_wait(barrier, n - 1)

    def tables(d, owner):
        return [
            pltpu.make_async_remote_copy(
                src_ref=source, dst_ref=goal.at[owner], send_sem=table_send.at[d, i],
                recv_sem=table_recv.at[d, i], device_id={"surf": lax.rem(me + d, n)},
                device_id_type=MESH,
            )
            for i, (source, goal) in enumerate((
                (recv_list_ref.at[0], places_ref), (nb_ref, nbs_ref),
                (count_ref.at[0], counts_ref),
            ))
        ]

    def line_copy(owner, l, way, to):
        row = owner * lines + l
        return pltpu.make_async_remote_copy(
            src_ref=adjoints_ref.at[row], dst_ref=adjoints_ref.at[row],
            send_sem=send_sem.at[way, l], recv_sem=recv_sem.at[row],
            device_id={"surf": to}, device_id_type=MESH,
        )

    def across(k):
        return lax.rem(chip + k, chips) * 2 + core

    for d in range(1, n):
        for copy in tables(d, me):
            copy.start()
    for l in range(lines):
        for k in range(1, chips):
            line_copy(me, l, k, across(k)).start()
    for l in range(lines):
        line_copy(me, l, 0, partner).start()

    for s in range(n):
        for j in range(cap):
            places_ref[me, s, j] = recv_list_ref[0, s, j]
        counts_ref[me, s] = count_ref[0, s]
    for l in range(lines):
        nbs_ref[me, l] = nb_ref[l]

    eye = diagonal(size)

    def product(b):
        for load in loads(b):
            load.wait()
        value = -dot(inv_ref[b], couple_ref[b])
        main = jnp.sum(jnp.where(eye, value, 0.0), axis=0, keepdims=True)
        main = main.astype(BF16).astype(F32)
        codes, scale = coded(value - jnp.where(eye, main, 0.0))
        code_ref[b, :, :size] = codes.astype(I16)
        side_ref[b, 0:1, :size] = scale
        side_ref[b, 1:2, :size] = main
        rhs = rhs_ref[b // elems, b % elems]
        both_ref[b] = jnp.concatenate([rhs, rhs], axis=0).T

    def relay(l):
        for k in range(1, chips):
            source = across(k)
            line_copy(source, l, k, partner).wait_recv()
            line_copy(source, l, chips - 1 + k, partner).start()

    for b in range(stored):
        product(b)

    for d in range(1, n):
        for copy in tables(d, lax.rem(me + n - d, n)):
            copy.wait_recv()
        for copy in tables(d, me):
            copy.wait_send()
    index_table(n, lines, elems, cap, plans, me, places_ref, nbs_ref, counts_ref,
                send_list_ref, index_ref, plan_ref)

    for l in range(lines):
        relay(l)
    for l in range(lines):
        line_copy(partner, l, 0, partner).wait_recv()
        for k in range(1, chips):
            other = across(k)
            line_copy(other + 1 - 2 * core, l, 0, partner).wait_recv()
            line_copy(me, l, k, other).wait_send()
            line_copy(other, l, chips - 1 + k, partner).wait_send()
        line_copy(me, l, 0, partner).wait_send()


def index_table(n, lines, elems, cap, plans, me, places, nbs, counts, sends, out_ref, plan_ref):
    stored = lines * elems
    room = n * cap
    for d in range(n):
        to = lax.rem(me + d, n)
        here = counts[me, to]
        for j in range(cap):
            used = j < here
            goal = jnp.where(used, places[to, me, j], 0)
            slot = d * cap + j
            out_ref[slot] = jnp.where(used, sends[0, to, j], 0)
            line = goal // elems
            out_ref[room + slot] = nbs[to, line]
            out_ref[2 * room + slot] = goal - line * elems
    for q in range(stored):
        value = jnp.int32(0)
        for d in range(n):
            source = lax.rem(me + n - d, n)
            for j in range(cap):
                hit = jnp.logical_and(j < counts[source, me], places[me, source, j] == q)
                value = jnp.where(hit, d * cap + j, value)
        out_ref[3 * room + q] = value

    best = jnp.int32(len(plans) - 1)
    most = []
    for d in range(n):
        value = counts[0, d]
        for s in range(1, n):
            value = jnp.maximum(value, counts[s, (s + d) % n])
        most.append(value)
    for p in reversed(range(len(plans) - 1)):
        fits = most[0] <= plans[p][0]
        for d in range(1, n):
            fits = jnp.logical_and(fits, most[d] <= plans[p][d])
        best = jnp.where(fits, p, best)
    plan_ref[0] = best


def gathered(n, cap, plans, recv_list, nb_line, send_count, send_list, adjoint_t, rhs_t,
             inv_block, couple_block):
    lines, elems, cols, size = adjoint_t.shape
    stored, wide = lines * elems, size + cols
    chips = n // 2
    vmem, hbm = pl.BlockSpec(memory_space=pltpu.VMEM), pl.BlockSpec(memory_space=pl.ANY)
    smem = pl.BlockSpec(memory_space=pltpu.SMEM)
    return pl.pallas_call(
        functools.partial(gather_kernel, n, cap, plans),
        out_shape=(
            jax.ShapeDtypeStruct((LANES,), I32),
            jax.ShapeDtypeStruct((1,), I32),
            jax.ShapeDtypeStruct((n * lines, size, elems * cols), BF16),
            jax.ShapeDtypeStruct((stored, size, 2 * cols), BF16),
            jax.ShapeDtypeStruct((stored, size, wide), I16),
            jax.ShapeDtypeStruct((stored, 2, wide), F32),
        ),
        in_specs=[smem] * 4 + [vmem] * 2 + [hbm] * 2,
        out_specs=(smem, smem) + (vmem,) * 4,
        scratch_shapes=[
            pltpu.SMEM((n, n, cap), I32),
            pltpu.SMEM((n, lines), I32),
            pltpu.SMEM((n, n), I32),
            pltpu.VMEM((stored, size, size), BF16),
            pltpu.VMEM((stored, size, size), BF16),
            pltpu.SemaphoreType.DMA((stored, 2)),
            pltpu.SemaphoreType.DMA((n, 3)),
            pltpu.SemaphoreType.DMA((n, 3)),
            pltpu.SemaphoreType.DMA((2 * chips - 1, lines)),
            pltpu.SemaphoreType.DMA((n * lines,)),
        ],
        compiler_params=pltpu.CompilerParams(
            collective_id=0, has_side_effects=True, vmem_limit_bytes=16 << 20
        ),
    )(recv_list, nb_line, send_count, send_list, adjoint_t, rhs_t, inv_block, couple_block)


def sweep_kernel(
    n, n_line, cap, lines, elems, budgets,
    index_ref, inv_ref, face_ref, both_ref, adjoints_ref, code_ref, side_ref,
    result_ref, out_ref, out_side_ref, got_ref, got_side_ref, hi_ref, lo_ref,
    map_hi, map_lo, shift, going, coming,
    send_sem, recv_sem, go_sem, come_sem,
):
    me, place = lax.axis_index("surf"), lax.axis_index("line")
    _, size, wide = code_ref.shape
    cols = wide - size
    room = n * cap
    body = wide - LANES
    half = size // 2
    inner, outer = jnp.maximum(place - 1, 0), jnp.minimum(place + 1, n_line - 1)
    top = n_line - 1

    barrier = pltpu.get_barrier_semaphore()
    for d in range(1, n):
        pl.semaphore_signal(
            barrier, inc=1, device_id={"surf": lax.rem(me + d, n)}, device_id_type=MESH
        )

    @pl.when(place < top)
    def _():
        pl.semaphore_signal(barrier, inc=1, device_id={"line": outer}, device_id_type=MESH)

    @pl.when(place > 0)
    def _():
        pl.semaphore_wait(barrier, n)

    @pl.when(place == 0)
    def _():
        pl.semaphore_wait(barrier, n - 1)

    upper = lax.broadcasted_iota(I32, (size, LANES), 1) >= cols
    upper_half = lax.broadcasted_iota(I32, (half, LANES), 1) >= cols
    upper_row = lax.broadcasted_iota(I32, (1, LANES), 1) >= cols
    eye = lax.broadcasted_iota(I32, (size, wide), 0) == lax.broadcasted_iota(
        I32, (size, wide), 1
    )

    def copies(d, slot):
        to = {"surf": lax.rem(me + d, n)}
        return (
            pltpu.make_async_remote_copy(
                src_ref=out_ref.at[slot], dst_ref=got_ref.at[slot],
                send_sem=send_sem.at[slot, 0], recv_sem=recv_sem.at[slot, 0],
                device_id=to, device_id_type=MESH,
            ),
            pltpu.make_async_remote_copy(
                src_ref=out_side_ref.at[slot], dst_ref=got_side_ref.at[slot],
                send_sem=send_sem.at[slot, 1], recv_sem=recv_sem.at[slot, 1],
                device_id=to, device_id_type=MESH,
            ),
        )

    def fill(slot, codes_at, sides_at):
        at = index_ref[slot]
        line, elem = index_ref[room + slot], index_ref[2 * room + slot]
        terms = dot(face_ref[at], adjoints_ref[line])
        terms = jnp.where(elem == 1, terms, pltpu.roll(terms, cols, 1))
        force = both_ref[at].astype(F32) - terms
        hi = force.astype(BF16).astype(F32)
        both = jnp.where(upper, hi, pltpu.roll(force - hi, cols, 1)).astype(BF16)
        moved = dot(inv_ref[at], both)
        moved = moved + pltpu.roll(moved, cols, 1)
        codes, scale = coded(moved)
        codes_at[slot, :, :body] = code_ref[at, :, :body]
        last = code_ref[at, :, body:].astype(I32)
        codes_at[slot, :, body:] = jnp.where(upper, codes, last).astype(I16)
        sides_at[slot, :, :body] = side_ref[at, :, :body]
        sides_at[slot, 0:1, body:] = jnp.where(upper_row, scale, side_ref[at, 0:1, body:])
        sides_at[slot, 1:2, body:] = side_ref[at, 1:2, body:]

    def decode(slot):
        value = got_ref[slot].astype(F32) * got_side_ref[slot, 0:1]
        value = value + jnp.where(eye, got_side_ref[slot, 1:2], 0.0)
        hi, lo = split(value)
        hi_ref[slot] = hi
        lo_ref[slot] = lo

    order = sorted(range(1, n), key=lambda d: -min(d, n - d))
    for d in order:
        def leave(j, _):
            slot = d * cap + j
            fill(slot, out_ref, out_side_ref)
            for copy in copies(d, slot):
                copy.start()
            return 0

        lax.fori_loop(0, budgets[d], leave, 0)

    def stay(j, _):
        fill(j, got_ref, got_side_ref)
        decode(j)
        return 0

    lax.fori_loop(0, budgets[0], stay, 0)

    for d in reversed(order):
        def arrive(j, _):
            for copy in copies(d, d * cap + j):
                copy.wait_recv()
            decode(d * cap + j)
            return 0

        lax.fori_loop(0, budgets[d], arrive, 0)

    def pass_on(l):
        return pltpu.make_async_remote_copy(
            src_ref=going.at[l], dst_ref=coming.at[l], send_sem=go_sem.at[l],
            recv_sem=come_sem.at[l], device_id={"line": inner}, device_id_type=MESH,
        )

    def carry(l, twice):
        packed = jnp.where(upper_half, twice[half:], twice[:half])
        most = jnp.maximum(jnp.max(jnp.abs(packed), axis=0, keepdims=True), TINY)
        power = jnp.ceil(jnp.log2(most) * 256.0)
        codes = jnp.round(packed * (CARRY_TOP * jnp.exp2(power * (-1.0 / 256.0))))
        going[l, :half] = codes.astype(I32).astype(I16)
        going[l, half:] = jnp.broadcast_to(power, (16, LANES)).astype(I32).astype(I16)

    def carried(l):
        power = coming[l, half:].astype(F32)[0:1]
        value = coming[l, :half].astype(F32) * (
            jnp.exp2(power * (1.0 / 256.0)) * (1.0 / CARRY_TOP)
        )
        hi = value.astype(BF16).astype(F32)
        lo = value - hi
        hi_turn, lo_turn = pltpu.roll(hi, cols, 1), pltpu.roll(lo, cols, 1)
        pair = jnp.concatenate(
            [jnp.where(upper_half, lo_turn, hi), jnp.where(upper_half, lo, hi_turn)], axis=0
        ).astype(BF16)
        same = jnp.concatenate(
            [jnp.where(upper_half, hi_turn, hi), jnp.where(upper_half, hi, hi_turn)], axis=0
        ).astype(BF16)
        return pair, same

    def applied(hi, lo, pair, same):
        first = dot(hi, pair)
        return first + (pltpu.roll(first, cols, 1) + dot(lo, same))

    def doubled(tile):
        return jnp.where(upper, tile, pltpu.roll(tile, cols, 1))

    def compose(l, _):
        inside = index_ref[3 * room + l * elems]
        outside = index_ref[3 * room + l * elems + 1]
        in_hi, in_lo = hi_ref[inside][:, :size], lo_ref[inside][:, :size]
        far_hi, far_lo = hi_ref[outside], lo_ref[outside]
        whole = dot(in_hi, far_hi) + (dot(in_hi, far_lo) + dot(in_lo, far_hi))
        tile = whole[:, body:] + (
            hi_ref[inside][:, body:].astype(F32) + lo_ref[inside][:, body:].astype(F32)
        )
        m_hi, m_lo = split(whole)
        map_hi[l] = m_hi
        map_lo[l] = m_lo
        twice = doubled(tile)
        shift[l] = twice

        @pl.when(place == top)
        def _():
            carry(l, twice)
            pass_on(l).start()

        return 0

    lax.fori_loop(0, lines, compose, 0)

    @pl.when(place == top)
    def _():
        coming[...] = jnp.zeros_like(coming)

    def step(l, _):
        @pl.when(place < top)
        def _():
            pass_on(l).wait_recv()

        pair, same = carried(l)
        twice = shift[l] + applied(map_hi[l][:, :size], map_lo[l][:, :size], pair, same)

        @pl.when(jnp.logical_and(place > 0, place < top))
        def _():
            carry(l, twice)
            pass_on(l).start()

        outside = index_ref[3 * room + l * elems + 1]
        far_hi, far_lo = hi_ref[outside], lo_ref[outside]
        first = doubled(far_hi[:, body:].astype(F32) + far_lo[:, body:].astype(F32))
        first = first + applied(far_hi[:, :size], far_lo[:, :size], pair, same)
        result_ref[l] = jnp.where(upper, first, twice).astype(BF16).T
        return 0

    lax.fori_loop(0, lines, step, 0)

    @pl.when(place > 0)
    def _():
        def gone(l, _):
            pass_on(l).wait_send()
            return 0

        lax.fori_loop(0, lines, gone, 0)

    for d in order:
        def left(j, _):
            for copy in copies(d, d * cap + j):
                copy.wait_send()
            return 0

        lax.fori_loop(0, budgets[d], left, 0)


def swept(n, n_line, cap, lines, elems, plan, budgets, index, inv, face, both, adjoints,
          codes, sides):
    stored, size, wide = codes.shape
    cols = wide - size
    vmem = pl.BlockSpec(memory_space=pltpu.VMEM)
    room = n * cap
    coded_blocks = pltpu.VMEM((room, size, wide), I16)
    side_rows = pltpu.VMEM((room, 2, wide), F32)
    parts = pltpu.VMEM((room, size, wide), BF16)
    maps = pltpu.VMEM((lines, size, wide), BF16)
    message = pltpu.VMEM((lines, size // 2 + 16, LANES), I16)
    return pl.pallas_call(
        functools.partial(sweep_kernel, n, n_line, cap, lines, elems, budgets),
        out_shape=jax.ShapeDtypeStruct((lines, elems * cols, size), BF16),
        in_specs=[pl.BlockSpec(memory_space=pltpu.SMEM)] + [vmem] * 6,
        out_specs=vmem,
        scratch_shapes=[
            coded_blocks, side_rows, coded_blocks, side_rows, parts, parts, maps, maps,
            pltpu.VMEM((lines, size, LANES), F32),
            message, message,
            pltpu.SemaphoreType.DMA((room, 2)),
            pltpu.SemaphoreType.DMA((room, 2)),
            pltpu.SemaphoreType.DMA((lines,)),
            pltpu.SemaphoreType.DMA((lines,)),
        ],
        compiler_params=pltpu.CompilerParams(
            collective_id=1 + plan, has_side_effects=True, vmem_limit_bytes=36 << 20
        ),
    )(index, inv, face, both, adjoints, codes, sides)


def plans_of(n, cap):
    plans = []
    if n == 4 and cap % 2 == 0:
        for empty in (0, 2, 3):
            for double in range(n):
                if double != empty:
                    plans.append(tuple(
                        cap if d == double else 0 if d == empty else cap // 2
                        for d in range(n)
                    ))
    return plans + [(cap,) * n]


def per_device(n_surf, n_line, inv_block, couple_block, face_block, rhs, adjoint_prev,
               nb_line, send_list, send_count, recv_list):
    lines, elems, size, _ = inv_block.shape
    cols = rhs.shape[3]
    cap = send_list.shape[2]
    plans = plans_of(n_surf, cap)
    index, plan, adjoints, both, codes, sides = gathered(
        n_surf, cap, plans, recv_list, nb_line, send_count, send_list,
        jnp.swapaxes(adjoint_prev, 2, 3), jnp.swapaxes(rhs, 2, 3), inv_block, couple_block,
    )
    inv = inv_block.reshape(lines * elems, size, size)
    face = face_block.reshape(lines * elems, size, size)

    def branch(p):
        return lambda: swept(
            n_surf, n_line, cap, lines, elems, p, plans[p], index, inv, face, both, adjoints,
            codes, sides,
        )

    if len(plans) > 1:
        result = lax.switch(plan[0], [branch(p) for p in range(len(plans))])
    else:
        result = branch(0)()
    return jnp.swapaxes(result.reshape(lines, elems, cols, size), 2, 3)


def solution(mesh):
    whole = P("surf", "line", None, None)
    in_specs = (
        whole, whole, whole, whole, whole,
        P("surf"), P("surf", None, None), P("surf", None), P("surf", None, None),
    )
    body = functools.partial(per_device, mesh.shape["surf"], mesh.shape["line"])
    return jax.shard_map(
        body, mesh=mesh, in_specs=in_specs, out_specs=whole, check_vma=False
    )
```

```python
import functools

import jax
import jax.numpy as jnp
from jax import lax
from jax.experimental import pallas as pl
from jax.experimental.pallas import tpu as pltpu
from jax.sharding import PartitionSpec as P

MESH = pl.DeviceIdType.MESH
F32 = jnp.float32
BF16 = jnp.bfloat16
I16 = jnp.int16
I32 = jnp.int32
LANES = 128
TOP = 32767.0
TINY = 1e-30
CARRY_TOP = 32700.0


def dot(a, b):
    return jnp.dot(a, b, preferred_element_type=F32)


def split(value):
    high = value.astype(BF16)
    return high, (value - high.astype(F32)).astype(BF16)


def diagonal(size):
    return lax.broadcasted_iota(I32, (size, size), 0) == lax.broadcasted_iota(
        I32, (size, size), 1
    )


def coded(value):
    most = jnp.maximum(jnp.max(jnp.abs(value), axis=0, keepdims=True), TINY)
    return jnp.round(value * (TOP / most)).astype(I32), most * (1.0 / TOP)


def gather_kernel(
    n, cap, plans, recv_list_hbm, nb_hbm, count_hbm, send_list_hbm, adjoint_hbm, rhs_hbm,
    inv_hbm, couple_hbm,
    index_ref, plan_ref, adjoints_ref, both_ref, code_ref, side_ref,
    recv_list_ref, nb_ref, count_ref, send_list_ref, adjoint_ref, rhs_ref,
    places_ref, nbs_ref, counts_ref, inv_ref, couple_ref,
    first_sem, load_sem, table_send, table_recv, send_sem, recv_sem,
):
    me = lax.axis_index("surf")
    lines, elems = adjoint_ref.shape[:2]
    size = inv_ref.shape[1]
    stored = lines * elems
    chips = n // 2
    core, chip = lax.rem(me, 2), me // 2
    partner = me + 1 - 2 * core

    def loads(b):
        at = (b // elems, b % elems)
        return (
            pltpu.make_async_copy(inv_hbm.at[at], inv_ref.at[b], load_sem.at[b, 0]),
            pltpu.make_async_copy(couple_hbm.at[at], couple_ref.at[b], load_sem.at[b, 1]),
        )

    first = [
        pltpu.make_async_copy(source, goal, first_sem.at[i])
        for i, (source, goal) in enumerate((
            (adjoint_hbm, adjoint_ref), (recv_list_hbm, recv_list_ref), (nb_hbm, nb_ref),
            (count_hbm, count_ref), (send_list_hbm, send_list_ref), (rhs_hbm, rhs_ref),
        ))
    ]
    for load in first:
        load.start()
    barrier = pltpu.get_barrier_semaphore()
    for d in range(1, n):
        pl.semaphore_signal(
            barrier, inc=1, device_id={"surf": lax.rem(me + d, n)}, device_id_type=MESH
        )
    for b in range(stored):
        for load in loads(b):
            load.start()
    for load in first:
        load.wait()

    for l in range(lines):
        stack = jnp.concatenate([adjoint_ref[l, e] for e in range(elems)], axis=0)
        adjoints_ref[me * lines + l] = stack.T

    pl.semaphore_wait(barrier, n - 1)

    def tables(d, owner):
        return [
            pltpu.make_async_remote_copy(
                src_ref=source, dst_ref=goal.at[owner], send_sem=table_send.at[d, i],
                recv_sem=table_recv.at[d, i], device_id={"surf": lax.rem(me + d, n)},
                device_id_type=MESH,
            )
            for i, (source, goal) in enumerate((
                (recv_list_ref.at[0], places_ref), (nb_ref, nbs_ref),
                (count_ref.at[0], counts_ref),
            ))
        ]

    def line_copy(owner, l, way, to):
        row = owner * lines + l
        return pltpu.make_async_remote_copy(
            src_ref=adjoints_ref.at[row], dst_ref=adjoints_ref.at[row],
            send_sem=send_sem.at[way, l], recv_sem=recv_sem.at[row],
            device_id={"surf": to}, device_id_type=MESH,
        )

    def across(k):
        return lax.rem(chip + k, chips) * 2 + core

    for d in range(1, n):
        for copy in tables(d, me):
            copy.start()
    for l in range(lines):
        for k in range(1, chips):
            line_copy(me, l, k, across(k)).start()
    for l in range(lines):
        line_copy(me, l, 0, partner).start()

    for s in range(n):
        for j in range(cap):
            places_ref[me, s, j] = recv_list_ref[0, s, j]
        counts_ref[me, s] = count_ref[0, s]
    for l in range(lines):
        nbs_ref[me, l] = nb_ref[l]

    eye = diagonal(size)

    def product(b):
        for load in loads(b):
            load.wait()
        value = -dot(inv_ref[b], couple_ref[b])
        main = jnp.sum(jnp.where(eye, value, 0.0), axis=0, keepdims=True)
        main = main.astype(BF16).astype(F32)
        codes, scale = coded(value - jnp.where(eye, main, 0.0))
        code_ref[b, :, :size] = codes.astype(I16)
        side_ref[b, 0:1, :size] = scale
        side_ref[b, 1:2, :size] = main
        rhs = rhs_ref[b // elems, b % elems]
        both_ref[b] = jnp.concatenate([rhs, rhs], axis=0).T

    def relay(l):
        for k in range(1, chips):
            source = across(k)
            line_copy(source, l, k, partner).wait_recv()
            line_copy(source, l, chips - 1 + k, partner).start()

    for b in range(stored):
        product(b)

    for d in range(1, n):
        for copy in tables(d, lax.rem(me + n - d, n)):
            copy.wait_recv()
        for copy in tables(d, me):
            copy.wait_send()
    index_table(n, lines, elems, cap, plans, me, places_ref, nbs_ref, counts_ref,
                send_list_ref, index_ref, plan_ref)

    for l in range(lines):
        relay(l)
    for l in range(lines):
        line_copy(partner, l, 0, partner).wait_recv()
        for k in range(1, chips):
            other = across(k)
            line_copy(other + 1 - 2 * core, l, 0, partner).wait_recv()
            line_copy(me, l, k, other).wait_send()
            line_copy(other, l, chips - 1 + k, partner).wait_send()
        line_copy(me, l, 0, partner).wait_send()


def index_table(n, lines, elems, cap, plans, me, places, nbs, counts, sends, out_ref, plan_ref):
    stored = lines * elems
    room = n * cap
    for d in range(n):
        to = lax.rem(me + d, n)
        here = counts[me, to]
        for j in range(cap):
            used = j < here
            goal = jnp.where(used, places[to, me, j], 0)
            slot = d * cap + j
            out_ref[slot] = jnp.where(used, sends[0, to, j], 0)
            line = goal // elems
            out_ref[room + slot] = nbs[to, line]
            out_ref[2 * room + slot] = goal - line * elems
    for q in range(stored):
        value = jnp.int32(0)
        for d in range(n):
            source = lax.rem(me + n - d, n)
            for j in range(cap):
                hit = jnp.logical_and(j < counts[source, me], places[me, source, j] == q)
                value = jnp.where(hit, d * cap + j, value)
        out_ref[3 * room + q] = value

    best = jnp.int32(len(plans) - 1)
    most = []
    for d in range(n):
        value = counts[0, d]
        for s in range(1, n):
            value = jnp.maximum(value, counts[s, (s + d) % n])
        most.append(value)
    for p in reversed(range(len(plans) - 1)):
        fits = most[0] <= plans[p][0]
        for d in range(1, n):
            fits = jnp.logical_and(fits, most[d] <= plans[p][d])
        best = jnp.where(fits, p, best)
    plan_ref[0] = best


def gathered(n, cap, plans, recv_list, nb_line, send_count, send_list, adjoint_t, rhs_t,
             inv_block, couple_block):
    lines, elems, cols, size = adjoint_t.shape
    stored, wide = lines * elems, size + cols
    chips = n // 2
    vmem, hbm = pl.BlockSpec(memory_space=pltpu.VMEM), pl.BlockSpec(memory_space=pl.ANY)
    smem = pl.BlockSpec(memory_space=pltpu.SMEM)
    return pl.pallas_call(
        functools.partial(gather_kernel, n, cap, plans),
        out_shape=(
            jax.ShapeDtypeStruct((LANES,), I32),
            jax.ShapeDtypeStruct((1,), I32),
            jax.ShapeDtypeStruct((n * lines, size, elems * cols), BF16),
            jax.ShapeDtypeStruct((stored, size, 2 * cols), BF16),
            jax.ShapeDtypeStruct((stored, size, wide), I16),
            jax.ShapeDtypeStruct((stored, 2, wide), F32),
        ),
        in_specs=[hbm] * 8,
        out_specs=(smem, smem) + (vmem,) * 4,
        scratch_shapes=[
            pltpu.SMEM(recv_list.shape, I32),
            pltpu.SMEM(nb_line.shape, I32),
            pltpu.SMEM(send_count.shape, I32),
            pltpu.SMEM(send_list.shape, I32),
            pltpu.VMEM(adjoint_t.shape, BF16),
            pltpu.VMEM(rhs_t.shape, BF16),
            pltpu.SMEM((n, n, cap), I32),
            pltpu.SMEM((n, lines), I32),
            pltpu.SMEM((n, n), I32),
            pltpu.VMEM((stored, size, size), BF16),
            pltpu.VMEM((stored, size, size), BF16),
            pltpu.SemaphoreType.DMA((6,)),
            pltpu.SemaphoreType.DMA((stored, 2)),
            pltpu.SemaphoreType.DMA((n, 3)),
            pltpu.SemaphoreType.DMA((n, 3)),
            pltpu.SemaphoreType.DMA((2 * chips - 1, lines)),
            pltpu.SemaphoreType.DMA((n * lines,)),
        ],
        compiler_params=pltpu.CompilerParams(
            collective_id=0, has_side_effects=True, vmem_limit_bytes=60 << 20
        ),
    )(recv_list, nb_line, send_count, send_list, adjoint_t, rhs_t, inv_block, couple_block)


def sweep_kernel(
    n, n_line, cap, lines, elems, budgets,
    index_ref, inv_hbm, face_hbm, both_hbm, adjoints_hbm, code_hbm, side_hbm,
    result_ref, inv_ref, face_ref, both_ref, adjoints_ref, code_ref, side_ref, out_ref, out_side_ref, got_ref, got_side_ref, hi_ref, lo_ref,
    map_hi, map_lo, shift, going, coming,
    load_sem, send_sem, recv_sem, go_sem, come_sem,
):
    me, place = lax.axis_index("surf"), lax.axis_index("line")
    _, size, wide = code_hbm.shape
    cols = wide - size
    room = n * cap
    body = wide - LANES
    half = size // 2
    inner, outer = jnp.maximum(place - 1, 0), jnp.minimum(place + 1, n_line - 1)
    top = n_line - 1

    loads = [
        pltpu.make_async_copy(source, goal, load_sem.at[i])
        for i, (source, goal) in enumerate((
            (face_hbm, face_ref), (adjoints_hbm, adjoints_ref), (both_hbm, both_ref),
            (inv_hbm, inv_ref), (code_hbm, code_ref), (side_hbm, side_ref),
        ))
    ]
    for load in loads:
        load.start()
    barrier = pltpu.get_barrier_semaphore()
    for d in range(1, n):
        pl.semaphore_signal(
            barrier, inc=1, device_id={"surf": lax.rem(me + d, n)}, device_id_type=MESH
        )

    @pl.when(place < top)
    def _():
        pl.semaphore_signal(barrier, inc=1, device_id={"line": outer}, device_id_type=MESH)

    @pl.when(place > 0)
    def _():
        pl.semaphore_wait(barrier, n)

    @pl.when(place == 0)
    def _():
        pl.semaphore_wait(barrier, n - 1)

    upper = lax.broadcasted_iota(I32, (size, LANES), 1) >= cols
    upper_half = lax.broadcasted_iota(I32, (half, LANES), 1) >= cols
    upper_row = lax.broadcasted_iota(I32, (1, LANES), 1) >= cols
    eye = lax.broadcasted_iota(I32, (size, wide), 0) == lax.broadcasted_iota(
        I32, (size, wide), 1
    )

    def copies(d, slot):
        to = {"surf": lax.rem(me + d, n)}
        return (
            pltpu.make_async_remote_copy(
                src_ref=out_ref.at[slot], dst_ref=got_ref.at[slot],
                send_sem=send_sem.at[slot, 0], recv_sem=recv_sem.at[slot, 0],
                device_id=to, device_id_type=MESH,
            ),
            pltpu.make_async_remote_copy(
                src_ref=out_side_ref.at[slot], dst_ref=got_side_ref.at[slot],
                send_sem=send_sem.at[slot, 1], recv_sem=recv_sem.at[slot, 1],
                device_id=to, device_id_type=MESH,
            ),
        )

    def fill(slot, codes_at, sides_at):
        at = index_ref[slot]
        line, elem = index_ref[room + slot], index_ref[2 * room + slot]
        terms = dot(face_ref[at], adjoints_ref[line])
        terms = jnp.where(elem == 1, terms, pltpu.roll(terms, cols, 1))
        force = both_ref[at].astype(F32) - terms
        hi = force.astype(BF16).astype(F32)
        both = jnp.where(upper, hi, pltpu.roll(force - hi, cols, 1)).astype(BF16)
        moved = dot(inv_ref[at], both)
        moved = moved + pltpu.roll(moved, cols, 1)
        codes, scale = coded(moved)
        codes_at[slot, :, :body] = code_ref[at, :, :body]
        last = code_ref[at, :, body:].astype(I32)
        codes_at[slot, :, body:] = jnp.where(upper, codes, last).astype(I16)
        sides_at[slot, :, :body] = side_ref[at, :, :body]
        sides_at[slot, 0:1, body:] = jnp.where(upper_row, scale, side_ref[at, 0:1, body:])
        sides_at[slot, 1:2, body:] = side_ref[at, 1:2, body:]

    def decode(slot):
        value = got_ref[slot].astype(F32) * got_side_ref[slot, 0:1]
        value = value + jnp.where(eye, got_side_ref[slot, 1:2], 0.0)
        hi, lo = split(value)
        hi_ref[slot] = hi
        lo_ref[slot] = lo

    for load in loads:
        load.wait()
    order = sorted(range(1, n), key=lambda d: -min(d, n - d))
    for d in order:
        def leave(j, _):
            slot = d * cap + j
            fill(slot, out_ref, out_side_ref)
            for copy in copies(d, slot):
                copy.start()
            return 0

        lax.fori_loop(0, budgets[d], leave, 0)

    def stay(j, _):
        fill(j, got_ref, got_side_ref)
        decode(j)
        return 0

    lax.fori_loop(0, budgets[0], stay, 0)

    for d in reversed(order):
        def arrive(j, _):
            for copy in copies(d, d * cap + j):
                copy.wait_recv()
            decode(d * cap + j)
            return 0

        lax.fori_loop(0, budgets[d], arrive, 0)

    def pass_on(l):
        return pltpu.make_async_remote_copy(
            src_ref=going.at[l], dst_ref=coming.at[l], send_sem=go_sem.at[l],
            recv_sem=come_sem.at[l], device_id={"line": inner}, device_id_type=MESH,
        )

    def carry(l, twice):
        packed = jnp.where(upper_half, twice[half:], twice[:half])
        most = jnp.maximum(jnp.max(jnp.abs(packed), axis=0, keepdims=True), TINY)
        power = jnp.ceil(jnp.log2(most) * 256.0)
        codes = jnp.round(packed * (CARRY_TOP * jnp.exp2(power * (-1.0 / 256.0))))
        going[l, :half] = codes.astype(I32).astype(I16)
        going[l, half:] = jnp.broadcast_to(power, (16, LANES)).astype(I32).astype(I16)

    def carried(l):
        power = coming[l, half:].astype(F32)[0:1]
        value = coming[l, :half].astype(F32) * (
            jnp.exp2(power * (1.0 / 256.0)) * (1.0 / CARRY_TOP)
        )
        hi = value.astype(BF16).astype(F32)
        lo = value - hi
        hi_turn, lo_turn = pltpu.roll(hi, cols, 1), pltpu.roll(lo, cols, 1)
        pair = jnp.concatenate(
            [jnp.where(upper_half, lo_turn, hi), jnp.where(upper_half, lo, hi_turn)], axis=0
        ).astype(BF16)
        same = jnp.concatenate(
            [jnp.where(upper_half, hi_turn, hi), jnp.where(upper_half, hi, hi_turn)], axis=0
        ).astype(BF16)
        return pair, same

    def applied(hi, lo, pair, same):
        first = dot(hi, pair)
        return first + (pltpu.roll(first, cols, 1) + dot(lo, same))

    def doubled(tile):
        return jnp.where(upper, tile, pltpu.roll(tile, cols, 1))

    def compose(l, _):
        inside = index_ref[3 * room + l * elems]
        outside = index_ref[3 * room + l * elems + 1]
        in_hi, in_lo = hi_ref[inside][:, :size], lo_ref[inside][:, :size]
        far_hi, far_lo = hi_ref[outside], lo_ref[outside]
        whole = dot(in_hi, far_hi) + (dot(in_hi, far_lo) + dot(in_lo, far_hi))
        tile = whole[:, body:] + (
            hi_ref[inside][:, body:].astype(F32) + lo_ref[inside][:, body:].astype(F32)
        )
        m_hi, m_lo = split(whole)
        map_hi[l] = m_hi
        map_lo[l] = m_lo
        twice = doubled(tile)
        shift[l] = twice

        @pl.when(place == top)
        def _():
            carry(l, twice)
            pass_on(l).start()

        return 0

    lax.fori_loop(0, lines, compose, 0)

    @pl.when(place == top)
    def _():
        coming[...] = jnp.zeros_like(coming)

    def step(l, _):
        @pl.when(place < top)
        def _():
            pass_on(l).wait_recv()

        pair, same = carried(l)
        twice = shift[l] + applied(map_hi[l][:, :size], map_lo[l][:, :size], pair, same)

        @pl.when(jnp.logical_and(place > 0, place < top))
        def _():
            carry(l, twice)
            pass_on(l).start()

        outside = index_ref[3 * room + l * elems + 1]
        far_hi, far_lo = hi_ref[outside], lo_ref[outside]
        first = doubled(far_hi[:, body:].astype(F32) + far_lo[:, body:].astype(F32))
        first = first + applied(far_hi[:, :size], far_lo[:, :size], pair, same)
        result_ref[l] = jnp.where(upper, first, twice).astype(BF16).T
        return 0

    lax.fori_loop(0, lines, step, 0)

    @pl.when(place > 0)
    def _():
        def gone(l, _):
            pass_on(l).wait_send()
            return 0

        lax.fori_loop(0, lines, gone, 0)

    for d in order:
        def left(j, _):
            for copy in copies(d, d * cap + j):
                copy.wait_send()
            return 0

        lax.fori_loop(0, budgets[d], left, 0)


def swept(n, n_line, cap, lines, elems, plan, budgets, index, inv, face, both, adjoints,
          codes, sides):
    stored, size, wide = codes.shape
    cols = wide - size
    vmem = pl.BlockSpec(memory_space=pltpu.VMEM)
    room = n * cap
    coded_blocks = pltpu.VMEM((room, size, wide), I16)
    side_rows = pltpu.VMEM((room, 2, wide), F32)
    parts = pltpu.VMEM((room, size, wide), BF16)
    maps = pltpu.VMEM((lines, size, wide), BF16)
    message = pltpu.VMEM((lines, size // 2 + 16, LANES), I16)
    return pl.pallas_call(
        functools.partial(sweep_kernel, n, n_line, cap, lines, elems, budgets),
        out_shape=jax.ShapeDtypeStruct((lines, elems * cols, size), BF16),
        in_specs=[pl.BlockSpec(memory_space=pltpu.SMEM)] + [pl.BlockSpec(memory_space=pl.ANY)] * 6,
        out_specs=vmem,
        scratch_shapes=[
            pltpu.VMEM(inv.shape, BF16),
            pltpu.VMEM(face.shape, BF16),
            pltpu.VMEM(both.shape, BF16),
            pltpu.VMEM(adjoints.shape, BF16),
            pltpu.VMEM(codes.shape, I16),
            pltpu.VMEM(sides.shape, F32),
            coded_blocks, side_rows, coded_blocks, side_rows, parts, parts, maps, maps,
            pltpu.VMEM((lines, size, LANES), F32),
            message, message,
            pltpu.SemaphoreType.DMA((6,)),
            pltpu.SemaphoreType.DMA((room, 2)),
            pltpu.SemaphoreType.DMA((room, 2)),
            pltpu.SemaphoreType.DMA((lines,)),
            pltpu.SemaphoreType.DMA((lines,)),
        ],
        compiler_params=pltpu.CompilerParams(
            collective_id=1 + plan, has_side_effects=True, vmem_limit_bytes=60 << 20
        ),
    )(index, inv, face, both, adjoints, codes, sides)


def plans_of(n, cap):
    plans = []
    if n == 4 and cap % 2 == 0:
        for empty in (0, 2, 3):
            for double in range(n):
                if double != empty:
                    plans.append(tuple(
                        cap if d == double else 0 if d == empty else cap // 2
                        for d in range(n)
                    ))
    return plans + [(cap,) * n]


def per_device(n_surf, n_line, inv_block, couple_block, face_block, rhs, adjoint_prev,
               nb_line, send_list, send_count, recv_list):
    lines, elems, size, _ = inv_block.shape
    cols = rhs.shape[3]
    cap = send_list.shape[2]
    plans = plans_of(n_surf, cap)
    index, plan, adjoints, both, codes, sides = gathered(
        n_surf, cap, plans, recv_list, nb_line, send_count, send_list,
        jnp.swapaxes(adjoint_prev, 2, 3), jnp.swapaxes(rhs, 2, 3), inv_block, couple_block,
    )
    inv = inv_block.reshape(lines * elems, size, size)
    face = face_block.reshape(lines * elems, size, size)

    def branch(p):
        return lambda: swept(
            n_surf, n_line, cap, lines, elems, p, plans[p], index, inv, face, both, adjoints,
            codes, sides,
        )

    if len(plans) > 1:
        result = lax.switch(plan[0], [branch(p) for p in range(len(plans))])
    else:
        result = branch(0)()
    return jnp.swapaxes(result.reshape(lines, elems, cols, size), 2, 3)


def solution(mesh):
    whole = P("surf", "line", None, None)
    in_specs = (
        whole, whole, whole, whole, whole,
        P("surf"), P("surf", None, None), P("surf", None), P("surf", None, None),
    )
    body = functools.partial(per_device, mesh.shape["surf"], mesh.shape["line"])
    return jax.shard_map(
        body, mesh=mesh, in_specs=in_specs, out_specs=whole, check_vma=False
    )
```

```python
import functools

import jax
import jax.numpy as jnp
from jax import lax
from jax.experimental import pallas as pl
from jax.experimental.pallas import tpu as pltpu
from jax.sharding import PartitionSpec as P

MESH = pl.DeviceIdType.MESH
F32 = jnp.float32
BF16 = jnp.bfloat16
I16 = jnp.int16
I32 = jnp.int32
LANES = 128
TOP = 32767.0
TINY = 1e-30
CARRY_TOP = 32700.0


def dot(a, b):
    return jnp.dot(a, b, preferred_element_type=F32)


def split(value):
    high = value.astype(BF16)
    return high, (value - high.astype(F32)).astype(BF16)


def diagonal(size):
    return lax.broadcasted_iota(I32, (size, size), 0) == lax.broadcasted_iota(
        I32, (size, size), 1
    )


def coded(value):
    most = jnp.maximum(jnp.max(jnp.abs(value), axis=0, keepdims=True), TINY)
    return jnp.round(value * (TOP / most)).astype(I32), most * (1.0 / TOP)


def gather_kernel(
    n, cap, plans, recv_list_hbm, nb_hbm, count_hbm, send_list_hbm, adjoint_hbm, rhs_hbm,
    inv_hbm, couple_hbm,
    index_ref, plan_ref, adjoints_ref, both_ref, code_ref, side_ref,
    recv_list_ref, nb_ref, count_ref, send_list_ref, adjoint_ref, rhs_ref,
    places_ref, nbs_ref, counts_ref, inv_ref, couple_ref,
    first_sem, load_sem, table_send, table_recv, send_sem, recv_sem,
):
    me = lax.axis_index("surf")
    lines, elems = adjoint_ref.shape[:2]
    size = inv_ref.shape[1]
    stored = lines * elems
    chips = n // 2
    core, chip = lax.rem(me, 2), me // 2
    partner = me + 1 - 2 * core

    def loads(b):
        at = (b // elems, b % elems)
        return (
            pltpu.make_async_copy(inv_hbm.at[at], inv_ref.at[b], load_sem.at[b, 0]),
            pltpu.make_async_copy(couple_hbm.at[at], couple_ref.at[b], load_sem.at[b, 1]),
        )

    first = [
        pltpu.make_async_copy(source, goal, first_sem.at[i])
        for i, (source, goal) in enumerate((
            (adjoint_hbm, adjoint_ref), (recv_list_hbm, recv_list_ref), (nb_hbm, nb_ref),
            (count_hbm, count_ref), (send_list_hbm, send_list_ref), (rhs_hbm, rhs_ref),
        ))
    ]
    for load in first:
        load.start()
    barrier = pltpu.get_barrier_semaphore()
    for d in range(1, n):
        pl.semaphore_signal(
            barrier, inc=1, device_id={"surf": lax.rem(me + d, n)}, device_id_type=MESH
        )
    for b in range(stored):
        for load in loads(b):
            load.start()
    for load in first:
        load.wait()

    for l in range(lines):
        stack = jnp.concatenate([adjoint_ref[l, e] for e in range(elems)], axis=0)
        adjoints_ref[me * lines + l] = stack.T

    pl.semaphore_wait(barrier, n - 1)

    def tables(d, owner):
        return [
            pltpu.make_async_remote_copy(
                src_ref=source, dst_ref=goal.at[owner], send_sem=table_send.at[d, i],
                recv_sem=table_recv.at[d, i], device_id={"surf": lax.rem(me + d, n)},
                device_id_type=MESH,
            )
            for i, (source, goal) in enumerate((
                (recv_list_ref.at[0], places_ref), (nb_ref, nbs_ref),
                (count_ref.at[0], counts_ref),
            ))
        ]

    def line_copy(owner, l, way, to):
        row = owner * lines + l
        return pltpu.make_async_remote_copy(
            src_ref=adjoints_ref.at[row], dst_ref=adjoints_ref.at[row],
            send_sem=send_sem.at[way, l], recv_sem=recv_sem.at[row],
            device_id={"surf": to}, device_id_type=MESH,
        )

    def across(k):
        return lax.rem(chip + k, chips) * 2 + core

    for d in range(1, n):
        for copy in tables(d, me):
            copy.start()
    for l in range(lines):
        for k in range(1, chips):
            line_copy(me, l, k, across(k)).start()
    for l in range(lines):
        line_copy(me, l, 0, partner).start()

    for s in range(n):
        for j in range(cap):
            places_ref[me, s, j] = recv_list_ref[0, s, j]
        counts_ref[me, s] = count_ref[0, s]
    for l in range(lines):
        nbs_ref[me, l] = nb_ref[l]

    eye = diagonal(size)

    def product(b):
        for load in loads(b):
            load.wait()
        value = -dot(inv_ref[b], couple_ref[b])
        main = jnp.sum(jnp.where(eye, value, 0.0), axis=0, keepdims=True)
        main = main.astype(BF16).astype(F32)
        codes, scale = coded(value - jnp.where(eye, main, 0.0))
        code_ref[b, :, :size] = codes.astype(I16)
        side_ref[b, 0:1, :size] = scale
        side_ref[b, 1:2, :size] = main
        rhs = rhs_ref[b // elems, b % elems]
        both_ref[b] = jnp.concatenate([rhs, rhs], axis=0).T

    def relay(l):
        for k in range(1, chips):
            source = across(k)
            line_copy(source, l, k, partner).wait_recv()
            line_copy(source, l, chips - 1 + k, partner).start()

    for b in range(stored):
        product(b)

    for d in range(1, n):
        for copy in tables(d, lax.rem(me + n - d, n)):
            copy.wait_recv()
        for copy in tables(d, me):
            copy.wait_send()
    index_table(n, lines, elems, cap, plans, me, places_ref, nbs_ref, counts_ref,
                send_list_ref, index_ref, plan_ref)

    for l in range(lines):
        relay(l)
    for l in range(lines):
        line_copy(partner, l, 0, partner).wait_recv()
        for k in range(1, chips):
            other = across(k)
            line_copy(other + 1 - 2 * core, l, 0, partner).wait_recv()
            line_copy(me, l, k, other).wait_send()
            line_copy(other, l, chips - 1 + k, partner).wait_send()
        line_copy(me, l, 0, partner).wait_send()


def index_table(n, lines, elems, cap, plans, me, places, nbs, counts, sends, out_ref, plan_ref):
    stored = lines * elems
    room = n * cap
    for d in range(n):
        to = lax.rem(me + d, n)
        here = counts[me, to]
        for j in range(cap):
            used = j < here
            goal = jnp.where(used, places[to, me, j], 0)
            slot = d * cap + j
            out_ref[slot] = jnp.where(used, sends[0, to, j], 0)
            line = goal // elems
            out_ref[room + slot] = nbs[to, line]
            out_ref[2 * room + slot] = goal - line * elems
    for q in range(stored):
        value = jnp.int32(0)
        for d in range(n):
            source = lax.rem(me + n - d, n)
            for j in range(cap):
                hit = jnp.logical_and(j < counts[source, me], places[me, source, j] == q)
                value = jnp.where(hit, d * cap + j, value)
        out_ref[3 * room + q] = value

    best = jnp.int32(len(plans) - 1)
    most = []
    for d in range(n):
        value = counts[0, d]
        for s in range(1, n):
            value = jnp.maximum(value, counts[s, (s + d) % n])
        most.append(value)
    for p in reversed(range(len(plans) - 1)):
        fits = most[0] <= plans[p][0]
        for d in range(1, n):
            fits = jnp.logical_and(fits, most[d] <= plans[p][d])
        best = jnp.where(fits, p, best)
    plan_ref[0] = best


def gathered(n, cap, plans, recv_list, nb_line, send_count, send_list, adjoint_t, rhs_t,
             inv_block, couple_block):
    lines, elems, cols, size = adjoint_t.shape
    stored, wide = lines * elems, size + cols
    chips = n // 2
    vmem, hbm = pl.BlockSpec(memory_space=pltpu.VMEM), pl.BlockSpec(memory_space=pl.ANY)
    smem = pl.BlockSpec(memory_space=pltpu.SMEM)
    return pl.pallas_call(
        functools.partial(gather_kernel, n, cap, plans),
        out_shape=(
            jax.ShapeDtypeStruct((LANES,), I32),
            jax.ShapeDtypeStruct((1,), I32),
            jax.ShapeDtypeStruct((n * lines, size, elems * cols), BF16),
            jax.ShapeDtypeStruct((stored, size, 2 * cols), BF16),
            jax.ShapeDtypeStruct((stored, size, wide), I16),
            jax.ShapeDtypeStruct((stored, 2, wide), F32),
        ),
        in_specs=[hbm] * 8,
        out_specs=(smem, smem) + (vmem,) * 4,
        scratch_shapes=[
            pltpu.SMEM(recv_list.shape, I32),
            pltpu.SMEM(nb_line.shape, I32),
            pltpu.SMEM(send_count.shape, I32),
            pltpu.SMEM(send_list.shape, I32),
            pltpu.VMEM(adjoint_t.shape, BF16),
            pltpu.VMEM(rhs_t.shape, BF16),
            pltpu.SMEM((n, n, cap), I32),
            pltpu.SMEM((n, lines), I32),
            pltpu.SMEM((n, n), I32),
            pltpu.VMEM((stored, size, size), BF16),
            pltpu.VMEM((stored, size, size), BF16),
            pltpu.SemaphoreType.DMA((6,)),
            pltpu.SemaphoreType.DMA((stored, 2)),
            pltpu.SemaphoreType.DMA((n, 3)),
            pltpu.SemaphoreType.DMA((n, 3)),
            pltpu.SemaphoreType.DMA((2 * chips - 1, lines)),
            pltpu.SemaphoreType.DMA((n * lines,)),
        ],
        compiler_params=pltpu.CompilerParams(
            collective_id=0, has_side_effects=True, vmem_limit_bytes=60 << 20
        ),
    )(recv_list, nb_line, send_count, send_list, adjoint_t, rhs_t, inv_block, couple_block)


def sweep_kernel(
    n, n_line, cap, lines, elems, budgets, relays, holders,
    index_ref, inv_hbm, face_hbm, both_hbm, adjoints_hbm, code_hbm, side_hbm,
    result_ref, inv_ref, face_ref, both_ref, adjoints_ref, code_ref, side_ref, out_ref, out_side_ref, got_ref, got_side_ref, hi_ref, lo_ref,
    map_hi, map_lo, shift, going, coming, relay_ref,
    load_sem, send_sem, recv_sem, go_sem, come_sem, leg_send, leg_recv, on_send, on_recv,
):
    me, place = lax.axis_index("surf"), lax.axis_index("line")
    _, size, wide = code_hbm.shape
    cols = wide - size
    room = n * cap
    body = wide - LANES
    half = size // 2
    inner, outer = jnp.maximum(place - 1, 0), jnp.minimum(place + 1, n_line - 1)
    top = n_line - 1

    loads = [
        pltpu.make_async_copy(source, goal, load_sem.at[i])
        for i, (source, goal) in enumerate((
            (face_hbm, face_ref), (adjoints_hbm, adjoints_ref), (both_hbm, both_ref),
            (inv_hbm, inv_ref), (code_hbm, code_ref), (side_hbm, side_ref),
        ))
    ]
    for load in loads:
        load.start()
    barrier = pltpu.get_barrier_semaphore()
    for d in range(1, n):
        pl.semaphore_signal(
            barrier, inc=1, device_id={"surf": lax.rem(me + d, n)}, device_id_type=MESH
        )

    @pl.when(place < top)
    def _():
        pl.semaphore_signal(barrier, inc=1, device_id={"line": outer}, device_id_type=MESH)

    greeted = n - 1 + jnp.where(place > 0, 1, 0)
    for far, mate in sorted({(far, mate) for far, _, mate in relays}):
        @pl.when(place == mate)
        def _():
            pl.semaphore_signal(
                barrier, inc=1, device_id={"surf": lax.rem(me + n // 2, n), "line": far},
                device_id_type=MESH,
            )

        @pl.when(place == far)
        def _():
            pl.semaphore_signal(barrier, inc=1, device_id={"line": mate}, device_id_type=MESH)

        greeted = greeted + jnp.where(jnp.logical_or(place == far, place == mate), 1, 0)
    pl.semaphore_wait(barrier, greeted)

    around = jnp.int32(0)
    for far, _, _ in relays:
        around = around + jnp.where(place == far, 1, 0)
    held = jnp.logical_or(place == -1, place == -2)
    for mate in holders:
        held = jnp.logical_or(held, place == mate)

    upper = lax.broadcasted_iota(I32, (size, LANES), 1) >= cols
    upper_half = lax.broadcasted_iota(I32, (half, LANES), 1) >= cols
    upper_row = lax.broadcasted_iota(I32, (1, LANES), 1) >= cols
    eye = lax.broadcasted_iota(I32, (size, wide), 0) == lax.broadcasted_iota(
        I32, (size, wide), 1
    )

    def copies(d, slot):
        to = {"surf": lax.rem(me + d, n)}
        return (
            pltpu.make_async_remote_copy(
                src_ref=out_ref.at[slot], dst_ref=got_ref.at[slot],
                send_sem=send_sem.at[slot, 0], recv_sem=recv_sem.at[slot, 0],
                device_id=to, device_id_type=MESH,
            ),
            pltpu.make_async_remote_copy(
                src_ref=out_side_ref.at[slot], dst_ref=got_side_ref.at[slot],
                send_sem=send_sem.at[slot, 1], recv_sem=recv_sem.at[slot, 1],
                device_id=to, device_id_type=MESH,
            ),
        )

    def fill(slot, codes_at, sides_at):
        at = index_ref[slot]
        line, elem = index_ref[room + slot], index_ref[2 * room + slot]
        terms = dot(face_ref[at], adjoints_ref[line])
        terms = jnp.where(elem == 1, terms, pltpu.roll(terms, cols, 1))
        force = both_ref[at].astype(F32) - terms
        hi = force.astype(BF16).astype(F32)
        both = jnp.where(upper, hi, pltpu.roll(force - hi, cols, 1)).astype(BF16)
        moved = dot(inv_ref[at], both)
        moved = moved + pltpu.roll(moved, cols, 1)
        codes, scale = coded(moved)
        codes_at[slot, :, :body] = code_ref[at, :, :body]
        last = code_ref[at, :, body:].astype(I32)
        codes_at[slot, :, body:] = jnp.where(upper, codes, last).astype(I16)
        sides_at[slot, :, :body] = side_ref[at, :, :body]
        sides_at[slot, 0:1, body:] = jnp.where(upper_row, scale, side_ref[at, 0:1, body:])
        sides_at[slot, 1:2, body:] = side_ref[at, 1:2, body:]

    def decode(slot):
        value = got_ref[slot].astype(F32) * got_side_ref[slot, 0:1]
        value = value + jnp.where(eye, got_side_ref[slot, 1:2], 0.0)
        hi, lo = split(value)
        hi_ref[slot] = hi
        lo_ref[slot] = lo

    for load in loads:
        load.wait()
    order = sorted(range(1, n), key=lambda d: -min(d, n - d))
    opposite = n // 2

    def first_leg(k, c):
        far, j, mate = relays[k]
        part = pl.ds(c * half, half)
        return pltpu.make_async_remote_copy(
            src_ref=out_ref.at[opposite * cap + j, part], dst_ref=relay_ref.at[k, part],
            send_sem=leg_send.at[k, c], recv_sem=leg_recv.at[k, c],
            device_id={"surf": lax.rem(me + opposite, n), "line": mate}, device_id_type=MESH,
        )

    def second_leg(k, c):
        far, j, mate = relays[k]
        part = pl.ds(c * half, half)
        return pltpu.make_async_remote_copy(
            src_ref=relay_ref.at[k, part], dst_ref=got_ref.at[opposite * cap + j, part],
            send_sem=on_send.at[k, c], recv_sem=on_recv.at[k, c],
            device_id={"line": far}, device_id_type=MESH,
        )

    def start(d, slot):
        block, rows = copies(d, slot)
        rows.start()
        if d != opposite or not relays:
            block.start()
            return

        @pl.when(slot - d * cap >= around)
        def _():
            block.start()

        for k, (far, j, mate) in enumerate(relays):
            @pl.when(jnp.logical_and(place == far, slot == d * cap + j))
            def _():
                first_leg(k, 0).start()
                first_leg(k, 1).start()

    for d in order:
        def leave(j, _):
            slot = d * cap + j
            fill(slot, out_ref, out_side_ref)

            @pl.when(jnp.logical_not(held))
            def _():
                start(d, slot)

            return 0

        lax.fori_loop(0, budgets[d], leave, 0)

    def stay(j, _):
        fill(j, got_ref, got_side_ref)
        decode(j)
        return 0

    lax.fori_loop(0, budgets[0], stay, 0)

    for c in range(2):
        for k, (far, j, mate) in enumerate(relays):
            @pl.when(place == mate)
            def _():
                first_leg(k, c).wait_recv()
                second_leg(k, c).start()

    if holders:
        @pl.when(held)
        def _():
            for d in order:
                def release(j, _):
                    for copy in copies(d, d * cap + j):
                        copy.start()
                    return 0

                lax.fori_loop(0, budgets[d], release, 0)

    for d in reversed(order):
        def arrive(j, _):
            slot = d * cap + j
            block, rows = copies(d, slot)
            rows.wait_recv()
            if d != opposite or not relays:
                block.wait_recv()
            else:
                @pl.when(j >= around)
                def _():
                    block.wait_recv()

                for k, (far, at, mate) in enumerate(relays):
                    @pl.when(jnp.logical_and(place == far, j == at))
                    def _():
                        second_leg(k, 0).wait_recv()
                        second_leg(k, 1).wait_recv()

            decode(slot)
            return 0

        lax.fori_loop(0, budgets[d], arrive, 0)

    def pass_on(l):
        return pltpu.make_async_remote_copy(
            src_ref=going.at[l], dst_ref=coming.at[l], send_sem=go_sem.at[l],
            recv_sem=come_sem.at[l], device_id={"line": inner}, device_id_type=MESH,
        )

    def carry(l, twice):
        packed = jnp.where(upper_half, twice[half:], twice[:half])
        most = jnp.maximum(jnp.max(jnp.abs(packed), axis=0, keepdims=True), TINY)
        power = jnp.ceil(jnp.log2(most) * 256.0)
        codes = jnp.round(packed * (CARRY_TOP * jnp.exp2(power * (-1.0 / 256.0))))
        going[l, :half] = codes.astype(I32).astype(I16)
        going[l, half:] = jnp.broadcast_to(power, (16, LANES)).astype(I32).astype(I16)

    def carried(l):
        power = coming[l, half:].astype(F32)[0:1]
        value = coming[l, :half].astype(F32) * (
            jnp.exp2(power * (1.0 / 256.0)) * (1.0 / CARRY_TOP)
        )
        hi = value.astype(BF16).astype(F32)
        lo = value - hi
        hi_turn, lo_turn = pltpu.roll(hi, cols, 1), pltpu.roll(lo, cols, 1)
        pair = jnp.concatenate(
            [jnp.where(upper_half, lo_turn, hi), jnp.where(upper_half, lo, hi_turn)], axis=0
        ).astype(BF16)
        same = jnp.concatenate(
            [jnp.where(upper_half, hi_turn, hi), jnp.where(upper_half, hi, hi_turn)], axis=0
        ).astype(BF16)
        return pair, same

    def applied(hi, lo, pair, same):
        first = dot(hi, pair)
        return first + (pltpu.roll(first, cols, 1) + dot(lo, same))

    def doubled(tile):
        return jnp.where(upper, tile, pltpu.roll(tile, cols, 1))

    def compose(l):
        inside = index_ref[3 * room + l * elems]
        outside = index_ref[3 * room + l * elems + 1]
        in_hi, in_lo = hi_ref[inside][:, :size], lo_ref[inside][:, :size]
        far_hi, far_lo = hi_ref[outside], lo_ref[outside]
        whole = dot(in_hi, far_hi) + (dot(in_hi, far_lo) + dot(in_lo, far_hi))
        tile = whole[:, body:] + (
            hi_ref[inside][:, body:].astype(F32) + lo_ref[inside][:, body:].astype(F32)
        )
        m_hi, m_lo = split(whole)
        map_hi[l] = m_hi
        map_lo[l] = m_lo
        twice = doubled(tile)
        shift[l] = twice

        @pl.when(place == top)
        def _():
            carry(l, twice)
            pass_on(l).start()

    @pl.when(place == top)
    def _():
        coming[...] = jnp.zeros_like(coming)

    def step(l):
        pass_on(l).wait_recv()
        pair, same = carried(l)
        twice = shift[l] + applied(map_hi[l][:, :size], map_lo[l][:, :size], pair, same)

        @pl.when(place > 0)
        def _():
            carry(l, twice)
            pass_on(l).start()

        shift[l] = twice

    def finish(l):
        pair, same = carried(l)
        outside = index_ref[3 * room + l * elems + 1]
        far_hi, far_lo = hi_ref[outside], lo_ref[outside]
        first = doubled(far_hi[:, body:].astype(F32) + far_lo[:, body:].astype(F32))
        first = first + applied(far_hi[:, :size], far_lo[:, :size], pair, same)
        result_ref[l] = jnp.where(upper, first, shift[l]).astype(BF16).T

    def turn(i, _):
        early, late = place == top - 1, place == 0
        pairs_from = jnp.where(early, 0, jnp.where(late, lines, 3 * lines))
        paired = jnp.logical_and(i >= pairs_from, i < pairs_from + 2 * lines)
        stage = jnp.where(paired, pairs_from // lines + lax.rem(i, 2), i // lines)
        l = jnp.where(paired, (i - pairs_from) // 2, lax.rem(i, lines))

        @pl.when(stage == 0)
        def _():
            compose(l)

        @pl.when(jnp.logical_and(stage == 1, place < top))
        def _():
            step(l)

        @pl.when(stage == 2)
        def _():
            finish(l)

        return 0

    lax.fori_loop(0, 3 * lines, turn, 0)

    @pl.when(place > 0)
    def _():
        def gone(l, _):
            pass_on(l).wait_send()
            return 0

        lax.fori_loop(0, lines, gone, 0)

    for k, (far, j, mate) in enumerate(relays):
        @pl.when(place == far)
        def _():
            first_leg(k, 0).wait_send()
            first_leg(k, 1).wait_send()

        @pl.when(place == mate)
        def _():
            second_leg(k, 0).wait_send()
            second_leg(k, 1).wait_send()

    for d in order:
        def left(j, _):
            block, rows = copies(d, d * cap + j)
            rows.wait_send()
            if d != opposite or not relays:
                block.wait_send()
            else:
                @pl.when(j >= around)
                def _():
                    block.wait_send()

            return 0

        lax.fori_loop(0, budgets[d], left, 0)


def relays_of(n, n_line, budgets):
    if n != 4 or n_line != 8:
        return (), ()
    crossing = 2 * budgets[2] + budgets[1] + budgets[3]
    if budgets[2] < 2 or crossing < 6:
        return (), ()
    if crossing < 8:
        return ((7, 0, 1),), (1,)
    relays = ((7, 0, 1), (7, 1, 3), (6, 0, 0))
    if crossing > 8:
        relays += ((5, 0, 2),)
    return relays, (0, 1)


def swept(n, n_line, cap, lines, elems, plan, budgets, index, inv, face, both, adjoints,
          codes, sides):
    stored, size, wide = codes.shape
    cols = wide - size
    vmem = pl.BlockSpec(memory_space=pltpu.VMEM)
    room = n * cap
    coded_blocks = pltpu.VMEM((room, size, wide), I16)
    side_rows = pltpu.VMEM((room, 2, wide), F32)
    parts = pltpu.VMEM((room, size, wide), BF16)
    maps = pltpu.VMEM((lines, size, wide), BF16)
    message = pltpu.VMEM((lines, size // 2 + 16, LANES), I16)
    relays, holders = relays_of(n, n_line, budgets)
    legs = pltpu.SemaphoreType.DMA((max(len(relays), 1), 2))
    return pl.pallas_call(
        functools.partial(
            sweep_kernel, n, n_line, cap, lines, elems, budgets, relays, holders
        ),
        out_shape=jax.ShapeDtypeStruct((lines, elems * cols, size), BF16),
        in_specs=[pl.BlockSpec(memory_space=pltpu.SMEM)] + [pl.BlockSpec(memory_space=pl.ANY)] * 6,
        out_specs=vmem,
        scratch_shapes=[
            pltpu.VMEM(inv.shape, BF16),
            pltpu.VMEM(face.shape, BF16),
            pltpu.VMEM(both.shape, BF16),
            pltpu.VMEM(adjoints.shape, BF16),
            pltpu.VMEM(codes.shape, I16),
            pltpu.VMEM(sides.shape, F32),
            coded_blocks, side_rows, coded_blocks, side_rows, parts, parts, maps, maps,
            pltpu.VMEM((lines, size, LANES), F32),
            message, message,
            pltpu.VMEM((max(len(relays), 1), size, wide), I16),
            pltpu.SemaphoreType.DMA((6,)),
            pltpu.SemaphoreType.DMA((room, 2)),
            pltpu.SemaphoreType.DMA((room, 2)),
            pltpu.SemaphoreType.DMA((lines,)),
            pltpu.SemaphoreType.DMA((lines,)),
            legs, legs, legs, legs,
        ],
        compiler_params=pltpu.CompilerParams(
            collective_id=1 + plan, has_side_effects=True, vmem_limit_bytes=60 << 20
        ),
    )(index, inv, face, both, adjoints, codes, sides)


def plans_of(n, cap):
    plans = []
    if n == 4 and cap % 2 == 0:
        for empty in (0, 2, 3):
            for double in range(n):
                if double != empty:
                    plans.append(tuple(
                        cap if d == double else 0 if d == empty else cap // 2
                        for d in range(n)
                    ))
    return plans + [(cap,) * n]


def per_device(n_surf, n_line, inv_block, couple_block, face_block, rhs, adjoint_prev,
               nb_line, send_list, send_count, recv_list):
    lines, elems, size, _ = inv_block.shape
    cols = rhs.shape[3]
    cap = send_list.shape[2]
    plans = plans_of(n_surf, cap)
    index, plan, adjoints, both, codes, sides = gathered(
        n_surf, cap, plans, recv_list, nb_line, send_count, send_list,
        jnp.swapaxes(adjoint_prev, 2, 3), jnp.swapaxes(rhs, 2, 3), inv_block, couple_block,
    )
    inv = inv_block.reshape(lines * elems, size, size)
    face = face_block.reshape(lines * elems, size, size)

    def branch(p):
        return lambda: swept(
            n_surf, n_line, cap, lines, elems, p, plans[p], index, inv, face, both, adjoints,
            codes, sides,
        )

    if len(plans) > 1:
        result = lax.switch(plan[0], [branch(p) for p in range(len(plans))])
    else:
        result = branch(0)()
    return jnp.swapaxes(result.reshape(lines, elems, cols, size), 2, 3)


def solution(mesh):
    whole = P("surf", "line", None, None)
    in_specs = (
        whole, whole, whole, whole, whole,
        P("surf"), P("surf", None, None), P("surf", None), P("surf", None, None),
    )
    body = functools.partial(per_device, mesh.shape["surf"], mesh.shape["line"])
    return jax.shard_map(
        body, mesh=mesh, in_specs=in_specs, out_specs=whole, check_vma=False
    )
```

```python
import functools

import jax
import jax.numpy as jnp
from jax import lax
from jax.experimental import pallas as pl
from jax.experimental.pallas import tpu as pltpu
from jax.sharding import PartitionSpec as P

MESH = pl.DeviceIdType.MESH
F32 = jnp.float32
BF16 = jnp.bfloat16
I16 = jnp.int16
I32 = jnp.int32
LANES = 128
TOP = 32767.0
TINY = 1e-30
CARRY_TOP = 32700.0


def dot(a, b):
    return jnp.dot(a, b, preferred_element_type=F32)


def split(value):
    high = value.astype(BF16)
    return high, (value - high.astype(F32)).astype(BF16)


def diagonal(size):
    return lax.broadcasted_iota(I32, (size, size), 0) == lax.broadcasted_iota(
        I32, (size, size), 1
    )


def coded(value):
    most = jnp.maximum(jnp.max(jnp.abs(value), axis=0, keepdims=True), TINY)
    return jnp.round(value * (TOP / most)).astype(I32), most * (1.0 / TOP)


def gather_kernel(
    n, cap, plans, recv_list_hbm, nb_hbm, count_hbm, send_list_hbm, adjoint_hbm, rhs_hbm,
    inv_hbm, couple_hbm,
    index_ref, plan_ref, adjoints_ref, both_ref, code_ref, side_ref,
    recv_list_ref, nb_ref, count_ref, send_list_ref, adjoint_ref, rhs_ref,
    places_ref, nbs_ref, counts_ref, inv_ref, couple_ref,
    first_sem, load_sem, table_send, table_recv, send_sem, recv_sem,
):
    me = lax.axis_index("surf")
    lines, elems = adjoint_ref.shape[:2]
    size = inv_ref.shape[1]
    stored = lines * elems
    chips = n // 2
    core, chip = lax.rem(me, 2), me // 2
    partner = me + 1 - 2 * core

    def loads(b):
        at = (b // elems, b % elems)
        return (
            pltpu.make_async_copy(inv_hbm.at[at], inv_ref.at[b], load_sem.at[b, 0]),
            pltpu.make_async_copy(couple_hbm.at[at], couple_ref.at[b], load_sem.at[b, 1]),
        )

    first = [
        pltpu.make_async_copy(source, goal, first_sem.at[i])
        for i, (source, goal) in enumerate((
            (adjoint_hbm, adjoint_ref), (recv_list_hbm, recv_list_ref), (nb_hbm, nb_ref),
            (count_hbm, count_ref), (send_list_hbm, send_list_ref), (rhs_hbm, rhs_ref),
        ))
    ]
    for load in first:
        load.start()
    barrier = pltpu.get_barrier_semaphore()
    for d in range(1, n):
        pl.semaphore_signal(
            barrier, inc=1, device_id={"surf": lax.rem(me + d, n)}, device_id_type=MESH
        )
    for b in range(stored):
        for load in loads(b):
            load.start()
    for load in first:
        load.wait()

    for l in range(lines):
        stack = jnp.concatenate([adjoint_ref[l, e] for e in range(elems)], axis=0)
        adjoints_ref[me * lines + l] = stack.T

    pl.semaphore_wait(barrier, n - 1)

    def tables(d, owner):
        return [
            pltpu.make_async_remote_copy(
                src_ref=source, dst_ref=goal.at[owner], send_sem=table_send.at[d, i],
                recv_sem=table_recv.at[d, i], device_id={"surf": lax.rem(me + d, n)},
                device_id_type=MESH,
            )
            for i, (source, goal) in enumerate((
                (recv_list_ref.at[0], places_ref), (nb_ref, nbs_ref),
                (count_ref.at[0], counts_ref),
            ))
        ]

    def line_copy(owner, l, way, to):
        row = owner * lines + l
        return pltpu.make_async_remote_copy(
            src_ref=adjoints_ref.at[row], dst_ref=adjoints_ref.at[row],
            send_sem=send_sem.at[way, l], recv_sem=recv_sem.at[row],
            device_id={"surf": to}, device_id_type=MESH,
        )

    def across(k):
        return lax.rem(chip + k, chips) * 2 + core

    for d in range(1, n):
        for copy in tables(d, me):
            copy.start()
    for l in range(lines):
        for k in range(1, chips):
            line_copy(me, l, k, across(k)).start()
    for l in range(lines):
        line_copy(me, l, 0, partner).start()

    for s in range(n):
        for j in range(cap):
            places_ref[me, s, j] = recv_list_ref[0, s, j]
        counts_ref[me, s] = count_ref[0, s]
    for l in range(lines):
        nbs_ref[me, l] = nb_ref[l]

    eye = diagonal(size)

    def product(b):
        for load in loads(b):
            load.wait()
        value = -dot(inv_ref[b], couple_ref[b])
        main = jnp.sum(jnp.where(eye, value, 0.0), axis=0, keepdims=True)
        main = main.astype(BF16).astype(F32)
        codes, scale = coded(value - jnp.where(eye, main, 0.0))
        code_ref[b, :, :size] = codes.astype(I16)
        side_ref[b, 0:1, :size] = scale
        side_ref[b, 1:2, :size] = main
        rhs = rhs_ref[b // elems, b % elems]
        both_ref[b] = jnp.concatenate([rhs, rhs], axis=0).T

    def relay(l):
        for k in range(1, chips):
            source = across(k)
            line_copy(source, l, k, partner).wait_recv()
            line_copy(source, l, chips - 1 + k, partner).start()

    lax.fori_loop(0, stored, lambda b, _: (product(b), 0)[1], 0)

    for d in range(1, n):
        for copy in tables(d, lax.rem(me + n - d, n)):
            copy.wait_recv()
        for copy in tables(d, me):
            copy.wait_send()
    index_table(n, lines, elems, cap, plans, me, places_ref, nbs_ref, counts_ref,
                send_list_ref, index_ref, plan_ref)

    for l in range(lines):
        relay(l)
    for l in range(lines):
        line_copy(partner, l, 0, partner).wait_recv()
        for k in range(1, chips):
            other = across(k)
            line_copy(other + 1 - 2 * core, l, 0, partner).wait_recv()
            line_copy(me, l, k, other).wait_send()
            line_copy(other, l, chips - 1 + k, partner).wait_send()
        line_copy(me, l, 0, partner).wait_send()


def index_table(n, lines, elems, cap, plans, me, places, nbs, counts, sends, out_ref, plan_ref):
    stored = lines * elems
    room = n * cap
    for d in range(n):
        to = lax.rem(me + d, n)
        here = counts[me, to]
        for j in range(cap):
            used = j < here
            goal = jnp.where(used, places[to, me, j], 0)
            slot = d * cap + j
            out_ref[slot] = jnp.where(used, sends[0, to, j], 0)
            line = goal // elems
            out_ref[room + slot] = nbs[to, line]
            out_ref[2 * room + slot] = goal - line * elems
    for q in range(stored):
        value = jnp.int32(0)
        for d in range(n):
            source = lax.rem(me + n - d, n)
            for j in range(cap):
                hit = jnp.logical_and(j < counts[source, me], places[me, source, j] == q)
                value = jnp.where(hit, d * cap + j, value)
        out_ref[3 * room + q] = value

    best = jnp.int32(len(plans) - 1)
    most = []
    for d in range(n):
        value = counts[0, d]
        for s in range(1, n):
            value = jnp.maximum(value, counts[s, (s + d) % n])
        most.append(value)
    for p in reversed(range(len(plans) - 1)):
        fits = most[0] <= plans[p][0]
        for d in range(1, n):
            fits = jnp.logical_and(fits, most[d] <= plans[p][d])
        best = jnp.where(fits, p, best)
    plan_ref[0] = best


def gathered(n, cap, plans, recv_list, nb_line, send_count, send_list, adjoint_t, rhs_t,
             inv_block, couple_block):
    lines, elems, cols, size = adjoint_t.shape
    stored, wide = lines * elems, size + cols
    chips = n // 2
    vmem, hbm = pl.BlockSpec(memory_space=pltpu.VMEM), pl.BlockSpec(memory_space=pl.ANY)
    smem = pl.BlockSpec(memory_space=pltpu.SMEM)
    return pl.pallas_call(
        functools.partial(gather_kernel, n, cap, plans),
        out_shape=(
            jax.ShapeDtypeStruct((LANES,), I32),
            jax.ShapeDtypeStruct((1,), I32),
            jax.ShapeDtypeStruct((n * lines, size, elems * cols), BF16),
            jax.ShapeDtypeStruct((stored, size, 2 * cols), BF16),
            jax.ShapeDtypeStruct((stored, size, wide), I16),
            jax.ShapeDtypeStruct((stored, 2, wide), F32),
        ),
        in_specs=[hbm] * 8,
        out_specs=(smem, smem) + (vmem,) * 4,
        scratch_shapes=[
            pltpu.SMEM(recv_list.shape, I32),
            pltpu.SMEM(nb_line.shape, I32),
            pltpu.SMEM(send_count.shape, I32),
            pltpu.SMEM(send_list.shape, I32),
            pltpu.VMEM(adjoint_t.shape, BF16),
            pltpu.VMEM(rhs_t.shape, BF16),
            pltpu.SMEM((n, n, cap), I32),
            pltpu.SMEM((n, lines), I32),
            pltpu.SMEM((n, n), I32),
            pltpu.VMEM((stored, size, size), BF16),
            pltpu.VMEM((stored, size, size), BF16),
            pltpu.SemaphoreType.DMA((6,)),
            pltpu.SemaphoreType.DMA((stored, 2)),
            pltpu.SemaphoreType.DMA((n, 3)),
            pltpu.SemaphoreType.DMA((n, 3)),
            pltpu.SemaphoreType.DMA((2 * chips - 1, lines)),
            pltpu.SemaphoreType.DMA((n * lines,)),
        ],
        compiler_params=pltpu.CompilerParams(
            collective_id=0, has_side_effects=True, vmem_limit_bytes=60 << 20
        ),
    )(recv_list, nb_line, send_count, send_list, adjoint_t, rhs_t, inv_block, couple_block)


def sweep_kernel(
    n, n_line, cap, lines, elems, budgets, relays, holders,
    index_ref, inv_hbm, face_hbm, both_hbm, adjoints_hbm, code_hbm, side_hbm,
    result_ref, inv_ref, face_ref, both_ref, adjoints_ref, code_ref, side_ref, out_ref, out_side_ref, got_ref, got_side_ref, hi_ref, lo_ref,
    map_hi, map_lo, shift, going, coming, relay_ref,
    load_sem, send_sem, recv_sem, go_sem, come_sem, leg_send, leg_recv, on_send, on_recv,
):
    me, place = lax.axis_index("surf"), lax.axis_index("line")
    _, size, wide = code_hbm.shape
    cols = wide - size
    room = n * cap
    body = wide - LANES
    half = size // 2
    inner, outer = jnp.maximum(place - 1, 0), jnp.minimum(place + 1, n_line - 1)
    top = n_line - 1

    loads = [
        pltpu.make_async_copy(source, goal, load_sem.at[i])
        for i, (source, goal) in enumerate((
            (face_hbm, face_ref), (adjoints_hbm, adjoints_ref), (both_hbm, both_ref),
            (inv_hbm, inv_ref), (code_hbm, code_ref), (side_hbm, side_ref),
        ))
    ]
    for load in loads:
        load.start()
    barrier = pltpu.get_barrier_semaphore()
    for d in range(1, n):
        pl.semaphore_signal(
            barrier, inc=1, device_id={"surf": lax.rem(me + d, n)}, device_id_type=MESH
        )

    @pl.when(place < top)
    def _():
        pl.semaphore_signal(barrier, inc=1, device_id={"line": outer}, device_id_type=MESH)

    greeted = n - 1 + jnp.where(place > 0, 1, 0)
    for far, mate in sorted({(far, mate) for far, _, mate in relays}):
        @pl.when(place == mate)
        def _():
            pl.semaphore_signal(
                barrier, inc=1, device_id={"surf": lax.rem(me + n // 2, n), "line": far},
                device_id_type=MESH,
            )

        @pl.when(place == far)
        def _():
            pl.semaphore_signal(barrier, inc=1, device_id={"line": mate}, device_id_type=MESH)

        greeted = greeted + jnp.where(jnp.logical_or(place == far, place == mate), 1, 0)
    pl.semaphore_wait(barrier, greeted)

    around = jnp.int32(0)
    for far, _, _ in relays:
        around = around + jnp.where(place == far, 1, 0)
    held = jnp.logical_or(place == -1, place == -2)
    for mate in holders:
        held = jnp.logical_or(held, place == mate)

    upper = lax.broadcasted_iota(I32, (size, LANES), 1) >= cols
    upper_half = lax.broadcasted_iota(I32, (half, LANES), 1) >= cols
    upper_row = lax.broadcasted_iota(I32, (1, LANES), 1) >= cols
    eye = lax.broadcasted_iota(I32, (size, wide), 0) == lax.broadcasted_iota(
        I32, (size, wide), 1
    )

    def copies(d, slot):
        to = {"surf": lax.rem(me + d, n)}
        return (
            pltpu.make_async_remote_copy(
                src_ref=out_ref.at[slot], dst_ref=got_ref.at[slot],
                send_sem=send_sem.at[slot, 0], recv_sem=recv_sem.at[slot, 0],
                device_id=to, device_id_type=MESH,
            ),
            pltpu.make_async_remote_copy(
                src_ref=out_side_ref.at[slot], dst_ref=got_side_ref.at[slot],
                send_sem=send_sem.at[slot, 1], recv_sem=recv_sem.at[slot, 1],
                device_id=to, device_id_type=MESH,
            ),
        )

    def fill(slot):
        at = index_ref[slot]
        line, elem = index_ref[room + slot], index_ref[2 * room + slot]
        terms = dot(face_ref[at], adjoints_ref[line])
        terms = jnp.where(elem == 1, terms, pltpu.roll(terms, cols, 1))
        force = both_ref[at].astype(F32) - terms
        hi = force.astype(BF16).astype(F32)
        both = jnp.where(upper, hi, pltpu.roll(force - hi, cols, 1)).astype(BF16)
        moved = dot(inv_ref[at], both)
        moved = moved + pltpu.roll(moved, cols, 1)
        codes, scale = coded(moved)
        out_ref[slot, :, :body] = code_ref[at, :, :body]
        last = code_ref[at, :, body:].astype(I32)
        out_ref[slot, :, body:] = jnp.where(upper, codes, last).astype(I16)
        out_side_ref[slot, :, :body] = side_ref[at, :, :body]
        out_side_ref[slot, 0:1, body:] = jnp.where(upper_row, scale, side_ref[at, 0:1, body:])
        out_side_ref[slot, 1:2, body:] = side_ref[at, 1:2, body:]

    def decode(codes_at, sides_at, slot):
        value = codes_at[slot].astype(F32) * sides_at[slot, 0:1]
        value = value + jnp.where(eye, sides_at[slot, 1:2], 0.0)
        hi, lo = split(value)
        hi_ref[slot] = hi
        lo_ref[slot] = lo

    for load in loads:
        load.wait()
    order = sorted(range(1, n), key=lambda d: -min(d, n - d))
    opposite = n // 2

    def first_leg(k, c):
        far, j, mate = relays[k]
        part = pl.ds(c * half, half)
        return pltpu.make_async_remote_copy(
            src_ref=out_ref.at[opposite * cap + j, part], dst_ref=relay_ref.at[k, part],
            send_sem=leg_send.at[k, c], recv_sem=leg_recv.at[k, c],
            device_id={"surf": lax.rem(me + opposite, n), "line": mate}, device_id_type=MESH,
        )

    def second_leg(k, c):
        far, j, mate = relays[k]
        part = pl.ds(c * half, half)
        return pltpu.make_async_remote_copy(
            src_ref=relay_ref.at[k, part], dst_ref=got_ref.at[opposite * cap + j, part],
            send_sem=on_send.at[k, c], recv_sem=on_recv.at[k, c],
            device_id={"line": far}, device_id_type=MESH,
        )

    def walk(offsets, visit):
        ends = []
        for d in offsets:
            ends.append((ends[-1] if ends else 0) + budgets[d])

        def turn(i, _):
            d, start = jnp.int32(offsets[-1]), jnp.int32(([0] + ends)[len(offsets) - 1])
            for p in reversed(range(len(offsets) - 1)):
                before = i < ends[p]
                d = jnp.where(before, offsets[p], d)
                start = jnp.where(before, ([0] + ends)[p], start)
            visit(d, i - start)
            return 0

        lax.fori_loop(0, ends[-1], turn, 0)

    def direct(d, j):
        return jnp.logical_or(d != opposite, j >= around)

    def leave(d, j):
        slot = d * cap + j
        fill(slot)

        @pl.when(d == 0)
        def _():
            decode(out_ref, out_side_ref, slot)

        @pl.when(jnp.logical_and(d > 0, jnp.logical_not(held)))
        def _():
            block, rows = copies(d, slot)
            rows.start()

            @pl.when(direct(d, j))
            def _():
                block.start()

            for k, (far, at, mate) in enumerate(relays):
                @pl.when(jnp.logical_and(place == far, slot == opposite * cap + at))
                def _():
                    first_leg(k, 0).start()
                    first_leg(k, 1).start()

    walk(order + [0], leave)

    for c in range(2):
        for k, (far, j, mate) in enumerate(relays):
            @pl.when(place == mate)
            def _():
                first_leg(k, c).wait_recv()
                second_leg(k, c).start()

    if holders:
        @pl.when(held)
        def _():
            def release(d, j):
                for copy in copies(d, d * cap + j):
                    copy.start()

            walk(order, release)

    def arrive(d, j):
        slot = d * cap + j
        block, rows = copies(d, slot)
        rows.wait_recv()

        @pl.when(direct(d, j))
        def _():
            block.wait_recv()

        for k, (far, at, mate) in enumerate(relays):
            @pl.when(jnp.logical_and(place == far, slot == opposite * cap + at))
            def _():
                second_leg(k, 0).wait_recv()
                second_leg(k, 1).wait_recv()

        decode(got_ref, got_side_ref, slot)

    walk(order[::-1], arrive)

    def pass_on(l):
        return pltpu.make_async_remote_copy(
            src_ref=going.at[l], dst_ref=coming.at[l], send_sem=go_sem.at[l],
            recv_sem=come_sem.at[l], device_id={"line": inner}, device_id_type=MESH,
        )

    def carry(l, twice):
        packed = jnp.where(upper_half, twice[half:], twice[:half])
        most = jnp.maximum(jnp.max(jnp.abs(packed), axis=0, keepdims=True), TINY)
        power = jnp.ceil(jnp.log2(most) * 256.0)
        codes = jnp.round(packed * (CARRY_TOP * jnp.exp2(power * (-1.0 / 256.0))))
        going[l, :half] = codes.astype(I32).astype(I16)
        going[l, half:] = jnp.broadcast_to(power, (16, LANES)).astype(I32).astype(I16)

    def carried(l):
        power = coming[l, half:].astype(F32)[0:1]
        value = coming[l, :half].astype(F32) * (
            jnp.exp2(power * (1.0 / 256.0)) * (1.0 / CARRY_TOP)
        )
        hi = value.astype(BF16).astype(F32)
        lo = value - hi
        hi_turn, lo_turn = pltpu.roll(hi, cols, 1), pltpu.roll(lo, cols, 1)
        pair = jnp.concatenate(
            [jnp.where(upper_half, lo_turn, hi), jnp.where(upper_half, lo, hi_turn)], axis=0
        ).astype(BF16)
        same = jnp.concatenate(
            [jnp.where(upper_half, hi_turn, hi), jnp.where(upper_half, hi, hi_turn)], axis=0
        ).astype(BF16)
        return pair, same

    def applied(hi, lo, pair, same):
        first = dot(hi, pair)
        return first + (pltpu.roll(first, cols, 1) + dot(lo, same))

    def doubled(tile):
        return jnp.where(upper, tile, pltpu.roll(tile, cols, 1))

    def compose(l):
        inside = index_ref[3 * room + l * elems]
        outside = index_ref[3 * room + l * elems + 1]
        in_hi, in_lo = hi_ref[inside][:, :size], lo_ref[inside][:, :size]
        far_hi, far_lo = hi_ref[outside], lo_ref[outside]
        whole = dot(in_hi, far_hi) + (dot(in_hi, far_lo) + dot(in_lo, far_hi))
        tile = whole[:, body:] + (
            hi_ref[inside][:, body:].astype(F32) + lo_ref[inside][:, body:].astype(F32)
        )
        m_hi, m_lo = split(whole)
        map_hi[l] = m_hi
        map_lo[l] = m_lo
        twice = doubled(tile)
        shift[l] = twice

        @pl.when(place == top)
        def _():
            carry(l, twice)
            pass_on(l).start()

    @pl.when(place == top)
    def _():
        coming[...] = jnp.zeros_like(coming)

    def step(l):
        pass_on(l).wait_recv()
        pair, same = carried(l)
        twice = shift[l] + applied(map_hi[l][:, :size], map_lo[l][:, :size], pair, same)

        @pl.when(place > 0)
        def _():
            carry(l, twice)
            pass_on(l).start()

        shift[l] = twice

    def finish(l):
        pair, same = carried(l)
        outside = index_ref[3 * room + l * elems + 1]
        far_hi, far_lo = hi_ref[outside], lo_ref[outside]
        first = doubled(far_hi[:, body:].astype(F32) + far_lo[:, body:].astype(F32))
        first = first + applied(far_hi[:, :size], far_lo[:, :size], pair, same)
        result_ref[l] = jnp.where(upper, first, shift[l]).astype(BF16).T

    def turn(i, _):
        early, late = place == top - 1, place == 0
        pairs_from = jnp.where(early, 0, jnp.where(late, lines, 3 * lines))
        paired = jnp.logical_and(i >= pairs_from, i < pairs_from + 2 * lines)
        stage = jnp.where(paired, pairs_from // lines + lax.rem(i, 2), i // lines)
        l = jnp.where(paired, (i - pairs_from) // 2, lax.rem(i, lines))

        @pl.when(stage == 0)
        def _():
            compose(l)

        @pl.when(jnp.logical_and(stage == 1, place < top))
        def _():
            step(l)

        @pl.when(stage == 2)
        def _():
            finish(l)

        return 0

    lax.fori_loop(0, 3 * lines, turn, 0)

    @pl.when(place > 0)
    def _():
        def gone(l, _):
            pass_on(l).wait_send()
            return 0

        lax.fori_loop(0, lines, gone, 0)

    for k, (far, j, mate) in enumerate(relays):
        @pl.when(place == far)
        def _():
            first_leg(k, 0).wait_send()
            first_leg(k, 1).wait_send()

        @pl.when(place == mate)
        def _():
            second_leg(k, 0).wait_send()
            second_leg(k, 1).wait_send()

    def left(d, j):
        block, rows = copies(d, d * cap + j)
        rows.wait_send()

        @pl.when(direct(d, j))
        def _():
            block.wait_send()

    walk(order, left)


def relays_of(n, n_line, budgets):
    if n != 4 or n_line != 8:
        return (), ()
    crossing = 2 * budgets[2] + budgets[1] + budgets[3]
    if budgets[2] < 2 or crossing < 6:
        return (), ()
    if crossing < 8:
        return ((7, 0, 1),), (1,)
    relays = ((7, 0, 1), (7, 1, 3), (6, 0, 0))
    if crossing > 8:
        relays += ((5, 0, 2),)
    return relays, (0, 1)


def swept(n, n_line, cap, lines, elems, plan, budgets, index, inv, face, both, adjoints,
          codes, sides):
    stored, size, wide = codes.shape
    cols = wide - size
    vmem = pl.BlockSpec(memory_space=pltpu.VMEM)
    room = n * cap
    coded_blocks = pltpu.VMEM((room, size, wide), I16)
    side_rows = pltpu.VMEM((room, 2, wide), F32)
    parts = pltpu.VMEM((room, size, wide), BF16)
    maps = pltpu.VMEM((lines, size, wide), BF16)
    message = pltpu.VMEM((lines, size // 2 + 16, LANES), I16)
    relays, holders = relays_of(n, n_line, budgets)
    legs = pltpu.SemaphoreType.DMA((max(len(relays), 1), 2))
    return pl.pallas_call(
        functools.partial(
            sweep_kernel, n, n_line, cap, lines, elems, budgets, relays, holders
        ),
        out_shape=jax.ShapeDtypeStruct((lines, elems * cols, size), BF16),
        in_specs=[pl.BlockSpec(memory_space=pltpu.SMEM)] + [pl.BlockSpec(memory_space=pl.ANY)] * 6,
        out_specs=vmem,
        scratch_shapes=[
            pltpu.VMEM(inv.shape, BF16),
            pltpu.VMEM(face.shape, BF16),
            pltpu.VMEM(both.shape, BF16),
            pltpu.VMEM(adjoints.shape, BF16),
            pltpu.VMEM(codes.shape, I16),
            pltpu.VMEM(sides.shape, F32),
            coded_blocks, side_rows, coded_blocks, side_rows, parts, parts, maps, maps,
            pltpu.VMEM((lines, size, LANES), F32),
            message, message,
            pltpu.VMEM((max(len(relays), 1), size, wide), I16),
            pltpu.SemaphoreType.DMA((6,)),
            pltpu.SemaphoreType.DMA((room, 2)),
            pltpu.SemaphoreType.DMA((room, 2)),
            pltpu.SemaphoreType.DMA((lines,)),
            pltpu.SemaphoreType.DMA((lines,)),
            legs, legs, legs, legs,
        ],
        compiler_params=pltpu.CompilerParams(
            collective_id=1 + plan, has_side_effects=True, vmem_limit_bytes=60 << 20
        ),
    )(index, inv, face, both, adjoints, codes, sides)


def plans_of(n, cap):
    plans = []
    if n == 4 and cap % 2 == 0:
        for empty in (0, 2, 3):
            for double in range(n):
                if double != empty:
                    plans.append(tuple(
                        cap if d == double else 0 if d == empty else cap // 2
                        for d in range(n)
                    ))
    return plans + [(cap,) * n]


def per_device(n_surf, n_line, inv_block, couple_block, face_block, rhs, adjoint_prev,
               nb_line, send_list, send_count, recv_list):
    lines, elems, size, _ = inv_block.shape
    cols = rhs.shape[3]
    cap = send_list.shape[2]
    plans = plans_of(n_surf, cap)
    index, plan, adjoints, both, codes, sides = gathered(
        n_surf, cap, plans, recv_list, nb_line, send_count, send_list,
        jnp.swapaxes(adjoint_prev, 2, 3), jnp.swapaxes(rhs, 2, 3), inv_block, couple_block,
    )
    inv = inv_block.reshape(lines * elems, size, size)
    face = face_block.reshape(lines * elems, size, size)

    def branch(p):
        return lambda: swept(
            n_surf, n_line, cap, lines, elems, p, plans[p], index, inv, face, both, adjoints,
            codes, sides,
        )

    if len(plans) > 1:
        result = lax.switch(plan[0], [branch(p) for p in range(len(plans))])
    else:
        result = branch(0)()
    return jnp.swapaxes(result.reshape(lines, elems, cols, size), 2, 3)


def solution(mesh):
    whole = P("surf", "line", None, None)
    in_specs = (
        whole, whole, whole, whole, whole,
        P("surf"), P("surf", None, None), P("surf", None), P("surf", None, None),
    )
    body = functools.partial(per_device, mesh.shape["surf"], mesh.shape["line"])
    return jax.shard_map(
        body, mesh=mesh, in_specs=in_specs, out_specs=whole, check_vma=False
    )
```

```python
import functools

import jax
import jax.numpy as jnp
from jax import lax
from jax.experimental import pallas as pl
from jax.experimental.pallas import tpu as pltpu
from jax.sharding import PartitionSpec as P

MESH = pl.DeviceIdType.MESH
F32 = jnp.float32
BF16 = jnp.bfloat16
I16 = jnp.int16
I32 = jnp.int32
LANES = 128
TOP = 32767.0
TINY = 1e-30
CARRY_TOP = 32700.0


def dot(a, b):
    return jnp.dot(a, b, preferred_element_type=F32)


def split(value):
    high = value.astype(BF16)
    return high, (value - high.astype(F32)).astype(BF16)


def diagonal(size):
    return lax.broadcasted_iota(I32, (size, size), 0) == lax.broadcasted_iota(
        I32, (size, size), 1
    )


def coded(value):
    most = jnp.maximum(jnp.max(jnp.abs(value), axis=0, keepdims=True), TINY)
    return jnp.round(value * (TOP / most)).astype(I32), most * (1.0 / TOP)


def gather_kernel(
    n, cap, plans, recv_list_hbm, nb_hbm, count_hbm, send_list_hbm, adjoint_hbm, rhs_hbm,
    inv_hbm, couple_hbm,
    index_ref, plan_ref, adjoints_ref, both_ref, code_ref, side_ref,
    recv_list_ref, nb_ref, count_ref, send_list_ref, adjoint_ref, rhs_ref,
    places_ref, nbs_ref, counts_ref, inv_ref, couple_ref,
    first_sem, load_sem, table_send, table_recv, send_sem, recv_sem,
):
    me = lax.axis_index("surf")
    lines, elems = adjoint_ref.shape[:2]
    size = inv_ref.shape[1]
    stored = lines * elems
    chips = n // 2
    core, chip = lax.rem(me, 2), me // 2
    partner = me + 1 - 2 * core

    def loads(b):
        at = (b // elems, b % elems)
        return (
            pltpu.make_async_copy(inv_hbm.at[at], inv_ref.at[b], load_sem.at[b, 0]),
            pltpu.make_async_copy(couple_hbm.at[at], couple_ref.at[b], load_sem.at[b, 1]),
        )

    first = [
        pltpu.make_async_copy(source, goal, first_sem.at[i])
        for i, (source, goal) in enumerate((
            (adjoint_hbm, adjoint_ref), (recv_list_hbm, recv_list_ref), (nb_hbm, nb_ref),
            (count_hbm, count_ref), (send_list_hbm, send_list_ref), (rhs_hbm, rhs_ref),
        ))
    ]
    for load in first:
        load.start()
    barrier = pltpu.get_barrier_semaphore()
    for d in range(1, n):
        pl.semaphore_signal(
            barrier, inc=1, device_id={"surf": lax.rem(me + d, n)}, device_id_type=MESH
        )
    for b in range(stored):
        for load in loads(b):
            load.start()
    for load in first:
        load.wait()

    for l in range(lines):
        stack = jnp.concatenate([adjoint_ref[l, e] for e in range(elems)], axis=0)
        adjoints_ref[me * lines + l] = stack.T

    pl.semaphore_wait(barrier, n - 1)

    def tables(d, owner):
        return [
            pltpu.make_async_remote_copy(
                src_ref=source, dst_ref=goal.at[owner], send_sem=table_send.at[d, i],
                recv_sem=table_recv.at[d, i], device_id={"surf": lax.rem(me + d, n)},
                device_id_type=MESH,
            )
            for i, (source, goal) in enumerate((
                (recv_list_ref.at[0], places_ref), (nb_ref, nbs_ref),
                (count_ref.at[0], counts_ref),
            ))
        ]

    def line_copy(owner, l, way, to):
        row = owner * lines + l
        return pltpu.make_async_remote_copy(
            src_ref=adjoints_ref.at[row], dst_ref=adjoints_ref.at[row],
            send_sem=send_sem.at[way, l], recv_sem=recv_sem.at[row],
            device_id={"surf": to}, device_id_type=MESH,
        )

    def across(k):
        return lax.rem(chip + k, chips) * 2 + core

    for d in range(1, n):
        for copy in tables(d, me):
            copy.start()
    for l in range(lines):
        for k in range(1, chips):
            line_copy(me, l, k, across(k)).start()
    for l in range(lines):
        line_copy(me, l, 0, partner).start()

    for s in range(n):
        for j in range(cap):
            places_ref[me, s, j] = recv_list_ref[0, s, j]
        counts_ref[me, s] = count_ref[0, s]
    for l in range(lines):
        nbs_ref[me, l] = nb_ref[l]

    eye = diagonal(size)

    def product(b):
        for load in loads(b):
            load.wait()
        value = -dot(inv_ref[b], couple_ref[b])
        main = jnp.sum(jnp.where(eye, value, 0.0), axis=0, keepdims=True)
        main = main.astype(BF16).astype(F32)
        codes, scale = coded(value - jnp.where(eye, main, 0.0))
        code_ref[b, :, :size] = codes.astype(I16)
        side_ref[b, 0:1, :size] = scale
        side_ref[b, 1:2, :size] = main
        rhs = rhs_ref[b // elems, b % elems]
        both_ref[b] = jnp.concatenate([rhs, rhs], axis=0).T

    def relay(l):
        for k in range(1, chips):
            source = across(k)
            line_copy(source, l, k, partner).wait_recv()
            line_copy(source, l, chips - 1 + k, partner).start()

    lax.fori_loop(0, stored, lambda b, _: (product(b), 0)[1], 0)

    for d in range(1, n):
        for copy in tables(d, lax.rem(me + n - d, n)):
            copy.wait_recv()
        for copy in tables(d, me):
            copy.wait_send()
    index_table(n, lines, elems, cap, plans, me, places_ref, nbs_ref, counts_ref,
                send_list_ref, index_ref, plan_ref)

    for l in range(lines):
        relay(l)
    for l in range(lines):
        line_copy(partner, l, 0, partner).wait_recv()
        for k in range(1, chips):
            other = across(k)
            line_copy(other + 1 - 2 * core, l, 0, partner).wait_recv()
            line_copy(me, l, k, other).wait_send()
            line_copy(other, l, chips - 1 + k, partner).wait_send()
        line_copy(me, l, 0, partner).wait_send()


def index_table(n, lines, elems, cap, plans, me, places, nbs, counts, sends, out_ref, plan_ref):
    stored = lines * elems
    room = n * cap
    for d in range(n):
        to = lax.rem(me + d, n)
        here = counts[me, to]
        for j in range(cap):
            used = j < here
            goal = jnp.where(used, places[to, me, j], 0)
            slot = d * cap + j
            out_ref[slot] = jnp.where(used, sends[0, to, j], 0)
            line = goal // elems
            out_ref[room + slot] = nbs[to, line]
            out_ref[2 * room + slot] = goal - line * elems
    for q in range(stored):
        value = jnp.int32(0)
        for d in range(n):
            source = lax.rem(me + n - d, n)
            for j in range(cap):
                hit = jnp.logical_and(j < counts[source, me], places[me, source, j] == q)
                value = jnp.where(hit, d * cap + j, value)
        out_ref[3 * room + q] = value

    best = jnp.int32(len(plans) - 1)
    most = []
    for d in range(n):
        value = counts[0, d]
        for s in range(1, n):
            value = jnp.maximum(value, counts[s, (s + d) % n])
        most.append(value)
    for p in reversed(range(len(plans) - 1)):
        fits = most[0] <= plans[p][0]
        for d in range(1, n):
            fits = jnp.logical_and(fits, most[d] <= plans[p][d])
        best = jnp.where(fits, p, best)
    plan_ref[0] = best


def gathered(n, cap, plans, recv_list, nb_line, send_count, send_list, adjoint_t, rhs_t,
             inv_block, couple_block):
    lines, elems, cols, size = adjoint_t.shape
    stored, wide = lines * elems, size + cols
    chips = n // 2
    vmem, hbm = pl.BlockSpec(memory_space=pltpu.VMEM), pl.BlockSpec(memory_space=pl.ANY)
    smem = pl.BlockSpec(memory_space=pltpu.SMEM)
    return pl.pallas_call(
        functools.partial(gather_kernel, n, cap, plans),
        out_shape=(
            jax.ShapeDtypeStruct((LANES,), I32),
            jax.ShapeDtypeStruct((1,), I32),
            jax.ShapeDtypeStruct((n * lines, size, elems * cols), BF16),
            jax.ShapeDtypeStruct((stored, size, 2 * cols), BF16),
            jax.ShapeDtypeStruct((stored, size, wide), I16),
            jax.ShapeDtypeStruct((stored, 2, wide), F32),
        ),
        in_specs=[hbm] * 8,
        out_specs=(smem, smem) + (vmem,) * 4,
        scratch_shapes=[
            pltpu.SMEM(recv_list.shape, I32),
            pltpu.SMEM(nb_line.shape, I32),
            pltpu.SMEM(send_count.shape, I32),
            pltpu.SMEM(send_list.shape, I32),
            pltpu.VMEM(adjoint_t.shape, BF16),
            pltpu.VMEM(rhs_t.shape, BF16),
            pltpu.SMEM((n, n, cap), I32),
            pltpu.SMEM((n, lines), I32),
            pltpu.SMEM((n, n), I32),
            pltpu.VMEM((stored, size, size), BF16),
            pltpu.VMEM((stored, size, size), BF16),
            pltpu.SemaphoreType.DMA((6,)),
            pltpu.SemaphoreType.DMA((stored, 2)),
            pltpu.SemaphoreType.DMA((n, 3)),
            pltpu.SemaphoreType.DMA((n, 3)),
            pltpu.SemaphoreType.DMA((2 * chips - 1, lines)),
            pltpu.SemaphoreType.DMA((n * lines,)),
        ],
        compiler_params=pltpu.CompilerParams(
            collective_id=0, has_side_effects=True, vmem_limit_bytes=54 << 20
        ),
    )(recv_list, nb_line, send_count, send_list, adjoint_t, rhs_t, inv_block, couple_block)


def sweep_kernel(
    n, n_line, cap, lines, elems, budgets, relays, holders,
    index_ref, inv_ref, face_ref, both_ref, adjoints_ref, code_ref, side_ref,
    result_ref, out_ref, out_side_ref, got_ref, got_side_ref, hi_ref, lo_ref,
    map_hi, map_lo, shift, going, coming, relay_ref,
    send_sem, recv_sem, go_sem, come_sem, leg_send, leg_recv, on_send, on_recv,
):
    me, place = lax.axis_index("surf"), lax.axis_index("line")
    _, size, wide = code_ref.shape
    cols = wide - size
    room = n * cap
    body = wide - LANES
    half = size // 2
    inner, outer = jnp.maximum(place - 1, 0), jnp.minimum(place + 1, n_line - 1)
    top = n_line - 1

    barrier = pltpu.get_barrier_semaphore()
    for d in range(1, n):
        pl.semaphore_signal(
            barrier, inc=1, device_id={"surf": lax.rem(me + d, n)}, device_id_type=MESH
        )

    @pl.when(place < top)
    def _():
        pl.semaphore_signal(barrier, inc=1, device_id={"line": outer}, device_id_type=MESH)

    greeted = n - 1 + jnp.where(place > 0, 1, 0)
    for far, mate in sorted({(far, mate) for far, _, mate in relays}):
        @pl.when(place == mate)
        def _():
            pl.semaphore_signal(
                barrier, inc=1, device_id={"surf": lax.rem(me + n // 2, n), "line": far},
                device_id_type=MESH,
            )

        @pl.when(place == far)
        def _():
            pl.semaphore_signal(barrier, inc=1, device_id={"line": mate}, device_id_type=MESH)

        greeted = greeted + jnp.where(jnp.logical_or(place == far, place == mate), 1, 0)

    around = jnp.int32(0)
    for far, _, _ in relays:
        around = around + jnp.where(place == far, 1, 0)
    held = jnp.logical_or(place == -1, place == -2)
    for mate in holders:
        held = jnp.logical_or(held, place == mate)

    upper = lax.broadcasted_iota(I32, (size, LANES), 1) >= cols
    upper_half = lax.broadcasted_iota(I32, (half, LANES), 1) >= cols
    upper_row = lax.broadcasted_iota(I32, (1, LANES), 1) >= cols
    eye = lax.broadcasted_iota(I32, (size, wide), 0) == lax.broadcasted_iota(
        I32, (size, wide), 1
    )

    def copies(d, slot):
        to = {"surf": lax.rem(me + d, n)}
        return (
            pltpu.make_async_remote_copy(
                src_ref=out_ref.at[slot], dst_ref=got_ref.at[slot],
                send_sem=send_sem.at[slot, 0], recv_sem=recv_sem.at[slot, 0],
                device_id=to, device_id_type=MESH,
            ),
            pltpu.make_async_remote_copy(
                src_ref=out_side_ref.at[slot], dst_ref=got_side_ref.at[slot],
                send_sem=send_sem.at[slot, 1], recv_sem=recv_sem.at[slot, 1],
                device_id=to, device_id_type=MESH,
            ),
        )

    def fill(slot):
        at = index_ref[slot]
        line, elem = index_ref[room + slot], index_ref[2 * room + slot]
        terms = dot(face_ref[at], adjoints_ref[line])
        terms = jnp.where(elem == 1, terms, pltpu.roll(terms, cols, 1))
        force = both_ref[at].astype(F32) - terms
        hi = force.astype(BF16).astype(F32)
        both = jnp.where(upper, hi, pltpu.roll(force - hi, cols, 1)).astype(BF16)
        moved = dot(inv_ref[at], both)
        moved = moved + pltpu.roll(moved, cols, 1)
        codes, scale = coded(moved)
        out_ref[slot, :, :body] = code_ref[at, :, :body]
        last = code_ref[at, :, body:].astype(I32)
        out_ref[slot, :, body:] = jnp.where(upper, codes, last).astype(I16)
        out_side_ref[slot, :, :body] = side_ref[at, :, :body]
        out_side_ref[slot, 0:1, body:] = jnp.where(upper_row, scale, side_ref[at, 0:1, body:])
        out_side_ref[slot, 1:2, body:] = side_ref[at, 1:2, body:]

    def decode(codes_at, sides_at, slot):
        value = codes_at[slot].astype(F32) * sides_at[slot, 0:1]
        value = value + jnp.where(eye, sides_at[slot, 1:2], 0.0)
        hi, lo = split(value)
        hi_ref[slot] = hi
        lo_ref[slot] = lo

    order = sorted(range(1, n), key=lambda d: -min(d, n - d))
    opposite = n // 2

    def first_leg(k, c):
        far, j, mate = relays[k]
        part = pl.ds(c * half, half)
        return pltpu.make_async_remote_copy(
            src_ref=out_ref.at[opposite * cap + j, part], dst_ref=relay_ref.at[k, part],
            send_sem=leg_send.at[k, c], recv_sem=leg_recv.at[k, c],
            device_id={"surf": lax.rem(me + opposite, n), "line": mate}, device_id_type=MESH,
        )

    def second_leg(k, c):
        far, j, mate = relays[k]
        part = pl.ds(c * half, half)
        return pltpu.make_async_remote_copy(
            src_ref=relay_ref.at[k, part], dst_ref=got_ref.at[opposite * cap + j, part],
            send_sem=on_send.at[k, c], recv_sem=on_recv.at[k, c],
            device_id={"line": far}, device_id_type=MESH,
        )

    def walk(offsets, visit):
        ends = []
        for d in offsets:
            ends.append((ends[-1] if ends else 0) + budgets[d])

        def turn(i, _):
            d, start = jnp.int32(offsets[-1]), jnp.int32(([0] + ends)[len(offsets) - 1])
            for p in reversed(range(len(offsets) - 1)):
                before = i < ends[p]
                d = jnp.where(before, offsets[p], d)
                start = jnp.where(before, ([0] + ends)[p], start)
            visit(i, d, i - start)
            return 0

        lax.fori_loop(0, ends[-1], turn, 0)

    def direct(d, j):
        return jnp.logical_or(d != opposite, j >= around)

    def leave(i, d, j):
        slot = d * cap + j
        fill(slot)

        @pl.when(i == 0)
        def _():
            pl.semaphore_wait(barrier, greeted)

        @pl.when(d == 0)
        def _():
            decode(out_ref, out_side_ref, slot)

        @pl.when(jnp.logical_and(d > 0, jnp.logical_not(held)))
        def _():
            block, rows = copies(d, slot)
            rows.start()

            @pl.when(direct(d, j))
            def _():
                block.start()

            for k, (far, at, mate) in enumerate(relays):
                @pl.when(jnp.logical_and(place == far, slot == opposite * cap + at))
                def _():
                    first_leg(k, 0).start()
                    first_leg(k, 1).start()

    walk(order + [0], leave)

    for c in range(2):
        for k, (far, j, mate) in enumerate(relays):
            @pl.when(place == mate)
            def _():
                first_leg(k, c).wait_recv()
                second_leg(k, c).start()

    if holders:
        @pl.when(held)
        def _():
            def release(_, d, j):
                for copy in copies(d, d * cap + j):
                    copy.start()

            walk(order, release)

    def arrive(_, d, j):
        slot = d * cap + j
        block, rows = copies(d, slot)
        rows.wait_recv()

        @pl.when(direct(d, j))
        def _():
            block.wait_recv()

        for k, (far, at, mate) in enumerate(relays):
            @pl.when(jnp.logical_and(place == far, slot == opposite * cap + at))
            def _():
                second_leg(k, 0).wait_recv()
                second_leg(k, 1).wait_recv()

        decode(got_ref, got_side_ref, slot)

    walk(order[::-1], arrive)

    def pass_on(l):
        return pltpu.make_async_remote_copy(
            src_ref=going.at[l], dst_ref=coming.at[l], send_sem=go_sem.at[l],
            recv_sem=come_sem.at[l], device_id={"line": inner}, device_id_type=MESH,
        )

    def carry(l, twice):
        packed = jnp.where(upper_half, twice[half:], twice[:half])
        most = jnp.maximum(jnp.max(jnp.abs(packed), axis=0, keepdims=True), TINY)
        power = jnp.ceil(jnp.log2(most) * 256.0)
        codes = jnp.round(packed * (CARRY_TOP * jnp.exp2(power * (-1.0 / 256.0))))
        going[l, :half] = codes.astype(I32).astype(I16)
        going[l, half:] = jnp.broadcast_to(power, (16, LANES)).astype(I32).astype(I16)

    def carried(l):
        power = coming[l, half:].astype(F32)[0:1]
        value = coming[l, :half].astype(F32) * (
            jnp.exp2(power * (1.0 / 256.0)) * (1.0 / CARRY_TOP)
        )
        hi = value.astype(BF16).astype(F32)
        lo = value - hi
        hi_turn, lo_turn = pltpu.roll(hi, cols, 1), pltpu.roll(lo, cols, 1)
        pair = jnp.concatenate(
            [jnp.where(upper_half, lo_turn, hi), jnp.where(upper_half, lo, hi_turn)], axis=0
        ).astype(BF16)
        same = jnp.concatenate(
            [jnp.where(upper_half, hi_turn, hi), jnp.where(upper_half, hi, hi_turn)], axis=0
        ).astype(BF16)
        return pair, same

    def applied(hi, lo, pair, same):
        first = dot(hi, pair)
        return first + (pltpu.roll(first, cols, 1) + dot(lo, same))

    def doubled(tile):
        return jnp.where(upper, tile, pltpu.roll(tile, cols, 1))

    def compose(l):
        inside = index_ref[3 * room + l * elems]
        outside = index_ref[3 * room + l * elems + 1]
        in_hi, in_lo = hi_ref[inside][:, :size], lo_ref[inside][:, :size]
        far_hi, far_lo = hi_ref[outside], lo_ref[outside]
        whole = dot(in_hi, far_hi) + (dot(in_hi, far_lo) + dot(in_lo, far_hi))
        tile = whole[:, body:] + (
            hi_ref[inside][:, body:].astype(F32) + lo_ref[inside][:, body:].astype(F32)
        )
        m_hi, m_lo = split(whole)
        map_hi[l] = m_hi
        map_lo[l] = m_lo
        twice = doubled(tile)
        shift[l] = twice

        @pl.when(place == top)
        def _():
            carry(l, twice)
            pass_on(l).start()

    @pl.when(place == top)
    def _():
        coming[...] = jnp.zeros_like(coming)

    def step(l):
        pass_on(l).wait_recv()
        pair, same = carried(l)
        twice = shift[l] + applied(map_hi[l][:, :size], map_lo[l][:, :size], pair, same)

        @pl.when(place > 0)
        def _():
            carry(l, twice)
            pass_on(l).start()

        shift[l] = twice

    def finish(l):
        pair, same = carried(l)
        outside = index_ref[3 * room + l * elems + 1]
        far_hi, far_lo = hi_ref[outside], lo_ref[outside]
        first = doubled(far_hi[:, body:].astype(F32) + far_lo[:, body:].astype(F32))
        first = first + applied(far_hi[:, :size], far_lo[:, :size], pair, same)
        result_ref[l] = jnp.where(upper, first, shift[l]).astype(BF16).T

    def turn(i, _):
        early, late = place == top - 1, place == 0
        pairs_from = jnp.where(early, 0, jnp.where(late, lines, 3 * lines))
        paired = jnp.logical_and(i >= pairs_from, i < pairs_from + 2 * lines)
        stage = jnp.where(paired, pairs_from // lines + lax.rem(i, 2), i // lines)
        l = jnp.where(paired, (i - pairs_from) // 2, lax.rem(i, lines))

        @pl.when(stage == 0)
        def _():
            compose(l)

        @pl.when(jnp.logical_and(stage == 1, place < top))
        def _():
            step(l)

        @pl.when(stage == 2)
        def _():
            finish(l)

        return 0

    lax.fori_loop(0, 3 * lines, turn, 0)

    @pl.when(place > 0)
    def _():
        def gone(l, _):
            pass_on(l).wait_send()
            return 0

        lax.fori_loop(0, lines, gone, 0)

    for k, (far, j, mate) in enumerate(relays):
        @pl.when(place == far)
        def _():
            first_leg(k, 0).wait_send()
            first_leg(k, 1).wait_send()

        @pl.when(place == mate)
        def _():
            second_leg(k, 0).wait_send()
            second_leg(k, 1).wait_send()

    def left(_, d, j):
        block, rows = copies(d, d * cap + j)
        rows.wait_send()

        @pl.when(direct(d, j))
        def _():
            block.wait_send()

    walk(order, left)


def relays_of(n, n_line, budgets):
    if n != 4 or n_line != 8:
        return (), ()
    crossing = 2 * budgets[2] + budgets[1] + budgets[3]
    if budgets[2] < 2 or crossing < 6:
        return (), ()
    if crossing < 8:
        return ((7, 0, 1),), (1,)
    relays = ((7, 0, 1), (7, 1, 3), (6, 0, 0))
    if crossing > 8:
        relays += ((5, 0, 2),)
    return relays, (0, 1)


def swept(n, n_line, cap, lines, elems, plan, budgets, index, inv, face, both, adjoints,
          codes, sides):
    stored, size, wide = codes.shape
    cols = wide - size
    vmem = pl.BlockSpec(memory_space=pltpu.VMEM)
    room = n * cap
    coded_blocks = pltpu.VMEM((room, size, wide), I16)
    side_rows = pltpu.VMEM((room, 2, wide), F32)
    parts = pltpu.VMEM((room, size, wide), BF16)
    maps = pltpu.VMEM((lines, size, wide), BF16)
    message = pltpu.VMEM((lines, size // 2 + 16, LANES), I16)
    relays, holders = relays_of(n, n_line, budgets)
    legs = pltpu.SemaphoreType.DMA((max(len(relays), 1), 2))
    return pl.pallas_call(
        functools.partial(
            sweep_kernel, n, n_line, cap, lines, elems, budgets, relays, holders
        ),
        out_shape=jax.ShapeDtypeStruct((lines, elems * cols, size), BF16),
        in_specs=[pl.BlockSpec(memory_space=pltpu.SMEM)] + [vmem] * 6,
        out_specs=vmem,
        scratch_shapes=[
            coded_blocks, side_rows, coded_blocks, side_rows, parts, parts, maps, maps,
            pltpu.VMEM((lines, size, LANES), F32),
            message, message,
            pltpu.VMEM((max(len(relays), 1), size, wide), I16),
            pltpu.SemaphoreType.DMA((room, 2)),
            pltpu.SemaphoreType.DMA((room, 2)),
            pltpu.SemaphoreType.DMA((lines,)),
            pltpu.SemaphoreType.DMA((lines,)),
            legs, legs, legs, legs,
        ],
        compiler_params=pltpu.CompilerParams(
            collective_id=1 + plan, has_side_effects=True, vmem_limit_bytes=40 << 20
        ),
    )(index, inv, face, both, adjoints, codes, sides)


def plans_of(n, cap):
    plans = []
    if n == 4 and cap % 2 == 0:
        for empty in (0, 2, 3):
            for double in range(n):
                if double != empty:
                    plans.append(tuple(
                        cap if d == double else 0 if d == empty else cap // 2
                        for d in range(n)
                    ))
    return plans + [(cap,) * n]


def per_device(n_surf, n_line, inv_block, couple_block, face_block, rhs, adjoint_prev,
               nb_line, send_list, send_count, recv_list):
    lines, elems, size, _ = inv_block.shape
    cols = rhs.shape[3]
    cap = send_list.shape[2]
    plans = plans_of(n_surf, cap)
    index, plan, adjoints, both, codes, sides = gathered(
        n_surf, cap, plans, recv_list, nb_line, send_count, send_list,
        jnp.swapaxes(adjoint_prev, 2, 3), jnp.swapaxes(rhs, 2, 3), inv_block, couple_block,
    )
    inv = inv_block.reshape(lines * elems, size, size)
    face = face_block.reshape(lines * elems, size, size)

    def branch(p):
        return lambda: swept(
            n_surf, n_line, cap, lines, elems, p, plans[p], index, inv, face, both, adjoints,
            codes, sides,
        )

    if len(plans) > 1:
        result = lax.switch(plan[0], [branch(p) for p in range(len(plans))])
    else:
        result = branch(0)()
    return jnp.swapaxes(result.reshape(lines, elems, cols, size), 2, 3)


def solution(mesh):
    whole = P("surf", "line", None, None)
    in_specs = (
        whole, whole, whole, whole, whole,
        P("surf"), P("surf", None, None), P("surf", None), P("surf", None, None),
    )
    body = functools.partial(per_device, mesh.shape["surf"], mesh.shape["line"])
    return jax.shard_map(
        body, mesh=mesh, in_specs=in_specs, out_specs=whole, check_vma=False
    )
```

```python
import functools

import jax
import jax.numpy as jnp
from jax import lax
from jax.experimental import pallas as pl
from jax.experimental.pallas import tpu as pltpu
from jax.sharding import PartitionSpec as P

MESH = pl.DeviceIdType.MESH
F32 = jnp.float32
BF16 = jnp.bfloat16
I16 = jnp.int16
I32 = jnp.int32
LANES = 128
TOP = 32767.0
TINY = 1e-30
CARRY_TOP = 32700.0


def dot(a, b):
    return jnp.dot(a, b, preferred_element_type=F32)


def split(value):
    high = value.astype(BF16)
    return high, (value - high.astype(F32)).astype(BF16)


def diagonal(size):
    return lax.broadcasted_iota(I32, (size, size), 0) == lax.broadcasted_iota(
        I32, (size, size), 1
    )


def coded(value):
    most = jnp.maximum(jnp.max(jnp.abs(value), axis=0, keepdims=True), TINY)
    return jnp.round(value * (TOP / most)).astype(I32), most * (1.0 / TOP)


def gather_kernel(
    n, cap, plans, recv_list_hbm, nb_hbm, count_hbm, send_list_hbm, adjoint_hbm, rhs_hbm,
    inv_hbm, couple_hbm,
    index_ref, plan_ref, adjoints_ref, both_ref, code_ref, side_ref,
    recv_list_ref, nb_ref, count_ref, send_list_ref, adjoint_ref, rhs_ref,
    places_ref, nbs_ref, counts_ref, inv_ref, couple_ref,
    first_sem, load_sem, table_send, table_recv, send_sem, recv_sem,
):
    me = lax.axis_index("surf")
    lines, elems = adjoint_ref.shape[:2]
    size = inv_ref.shape[1]
    stored = lines * elems
    chips = n // 2
    core, chip = lax.rem(me, 2), me // 2
    partner = me + 1 - 2 * core

    def loads(b):
        at = (b // elems, b % elems)
        return (
            pltpu.make_async_copy(inv_hbm.at[at], inv_ref.at[b], load_sem.at[b, 0]),
            pltpu.make_async_copy(couple_hbm.at[at], couple_ref.at[b], load_sem.at[b, 1]),
        )

    first = [
        pltpu.make_async_copy(source, goal, first_sem.at[i])
        for i, (source, goal) in enumerate((
            (adjoint_hbm, adjoint_ref), (recv_list_hbm, recv_list_ref), (nb_hbm, nb_ref),
            (count_hbm, count_ref), (send_list_hbm, send_list_ref), (rhs_hbm, rhs_ref),
        ))
    ]
    for load in first:
        load.start()
    barrier = pltpu.get_barrier_semaphore()
    for d in range(1, n):
        pl.semaphore_signal(
            barrier, inc=1, device_id={"surf": lax.rem(me + d, n)}, device_id_type=MESH
        )
    for b in range(stored):
        for load in loads(b):
            load.start()
    for load in first:
        load.wait()

    for l in range(lines):
        stack = jnp.concatenate([adjoint_ref[l, e] for e in range(elems)], axis=0)
        adjoints_ref[me * lines + l] = stack.T

    pl.semaphore_wait(barrier, n - 1)

    def tables(d, owner):
        return [
            pltpu.make_async_remote_copy(
                src_ref=source, dst_ref=goal.at[owner], send_sem=table_send.at[d, i],
                recv_sem=table_recv.at[d, i], device_id={"surf": lax.rem(me + d, n)},
                device_id_type=MESH,
            )
            for i, (source, goal) in enumerate((
                (recv_list_ref.at[0], places_ref), (nb_ref, nbs_ref),
                (count_ref.at[0], counts_ref),
            ))
        ]

    def line_copy(owner, l, way, to):
        row = owner * lines + l
        return pltpu.make_async_remote_copy(
            src_ref=adjoints_ref.at[row], dst_ref=adjoints_ref.at[row],
            send_sem=send_sem.at[way, l], recv_sem=recv_sem.at[row],
            device_id={"surf": to}, device_id_type=MESH,
        )

    def across(k):
        return lax.rem(chip + k, chips) * 2 + core

    for d in range(1, n):
        for copy in tables(d, me):
            copy.start()
    for l in range(lines):
        for k in range(1, chips):
            line_copy(me, l, k, across(k)).start()
    for l in range(lines):
        line_copy(me, l, 0, partner).start()

    for s in range(n):
        for j in range(cap):
            places_ref[me, s, j] = recv_list_ref[0, s, j]
        counts_ref[me, s] = count_ref[0, s]
    for l in range(lines):
        nbs_ref[me, l] = nb_ref[l]

    eye = diagonal(size)

    def product(b):
        for load in loads(b):
            load.wait()
        value = -dot(inv_ref[b], couple_ref[b])
        main = jnp.sum(jnp.where(eye, value, 0.0), axis=0, keepdims=True)
        main = main.astype(BF16).astype(F32)
        codes, scale = coded(value - jnp.where(eye, main, 0.0))
        code_ref[b, :, :size] = codes.astype(I16)
        side_ref[b, 0:1, :size] = scale
        side_ref[b, 1:2, :size] = main
        rhs = rhs_ref[b // elems, b % elems]
        both_ref[b] = jnp.concatenate([rhs, rhs], axis=0).T

    def relay(l):
        for k in range(1, chips):
            source = across(k)
            line_copy(source, l, k, partner).wait_recv()
            line_copy(source, l, chips - 1 + k, partner).start()

    lax.fori_loop(0, stored, lambda b, _: (product(b), 0)[1], 0)

    for d in range(1, n):
        for copy in tables(d, lax.rem(me + n - d, n)):
            copy.wait_recv()
        for copy in tables(d, me):
            copy.wait_send()
    index_table(n, lines, elems, cap, plans, me, places_ref, nbs_ref, counts_ref,
                send_list_ref, index_ref, plan_ref)

    for l in range(lines):
        relay(l)
    for l in range(lines):
        line_copy(partner, l, 0, partner).wait_recv()
        for k in range(1, chips):
            other = across(k)
            line_copy(other + 1 - 2 * core, l, 0, partner).wait_recv()
            line_copy(me, l, k, other).wait_send()
            line_copy(other, l, chips - 1 + k, partner).wait_send()
        line_copy(me, l, 0, partner).wait_send()


def index_table(n, lines, elems, cap, plans, me, places, nbs, counts, sends, out_ref, plan_ref):
    stored = lines * elems
    room = n * cap
    for d in range(n):
        to = lax.rem(me + d, n)
        here = counts[me, to]
        for j in range(cap):
            used = j < here
            goal = jnp.where(used, places[to, me, j], 0)
            slot = d * cap + j
            out_ref[slot] = jnp.where(used, sends[0, to, j], 0)
            line = goal // elems
            out_ref[room + slot] = nbs[to, line]
            out_ref[2 * room + slot] = goal - line * elems
    for q in range(stored):
        value = jnp.int32(0)
        for d in range(n):
            source = lax.rem(me + n - d, n)
            for j in range(cap):
                hit = jnp.logical_and(j < counts[source, me], places[me, source, j] == q)
                value = jnp.where(hit, d * cap + j, value)
        out_ref[3 * room + q] = value

    best = jnp.int32(len(plans) - 1)
    most = []
    for d in range(n):
        value = counts[0, d]
        for s in range(1, n):
            value = jnp.maximum(value, counts[s, (s + d) % n])
        most.append(value)
    for p in reversed(range(len(plans) - 1)):
        fits = most[0] <= plans[p][0]
        for d in range(1, n):
            fits = jnp.logical_and(fits, most[d] <= plans[p][d])
        best = jnp.where(fits, p, best)
    plan_ref[0] = best


def gathered(n, cap, plans, recv_list, nb_line, send_count, send_list, adjoint_t, rhs_t,
             inv_block, couple_block):
    lines, elems, cols, size = adjoint_t.shape
    stored, wide = lines * elems, size + cols
    chips = n // 2
    vmem, hbm = pl.BlockSpec(memory_space=pltpu.VMEM), pl.BlockSpec(memory_space=pl.ANY)
    smem = pl.BlockSpec(memory_space=pltpu.SMEM)
    return pl.pallas_call(
        functools.partial(gather_kernel, n, cap, plans),
        out_shape=(
            jax.ShapeDtypeStruct((LANES,), I32),
            jax.ShapeDtypeStruct((1,), I32),
            jax.ShapeDtypeStruct((n * lines, size, elems * cols), BF16),
            jax.ShapeDtypeStruct((stored, size, 2 * cols), BF16),
            jax.ShapeDtypeStruct((stored, size, wide), I16),
            jax.ShapeDtypeStruct((stored, 2, wide), F32),
        ),
        in_specs=[hbm] * 8,
        out_specs=(smem, smem) + (vmem,) * 4,
        scratch_shapes=[
            pltpu.SMEM(recv_list.shape, I32),
            pltpu.SMEM(nb_line.shape, I32),
            pltpu.SMEM(send_count.shape, I32),
            pltpu.SMEM(send_list.shape, I32),
            pltpu.VMEM(adjoint_t.shape, BF16),
            pltpu.VMEM(rhs_t.shape, BF16),
            pltpu.SMEM((n, n, cap), I32),
            pltpu.SMEM((n, lines), I32),
            pltpu.SMEM((n, n), I32),
            pltpu.VMEM((stored, size, size), BF16),
            pltpu.VMEM((stored, size, size), BF16),
            pltpu.SemaphoreType.DMA((6,)),
            pltpu.SemaphoreType.DMA((stored, 2)),
            pltpu.SemaphoreType.DMA((n, 3)),
            pltpu.SemaphoreType.DMA((n, 3)),
            pltpu.SemaphoreType.DMA((2 * chips - 1, lines)),
            pltpu.SemaphoreType.DMA((n * lines,)),
        ],
        compiler_params=pltpu.CompilerParams(
            collective_id=0, has_side_effects=True, vmem_limit_bytes=54 << 20
        ),
    )(recv_list, nb_line, send_count, send_list, adjoint_t, rhs_t, inv_block, couple_block)


def sweep_kernel(
    n, n_line, cap, lines, elems, budgets, relays, holders,
    index_ref, inv_ref, face_ref, both_ref, adjoints_ref, code_ref, side_ref,
    result_ref, out_ref, out_side_ref, got_ref, got_side_ref, hi_ref, lo_ref,
    map_hi, map_lo, shift, going, coming, relay_ref,
    send_sem, recv_sem, go_sem, come_sem, leg_send, leg_recv, on_send, on_recv,
):
    me, place = lax.axis_index("surf"), lax.axis_index("line")
    _, size, wide = code_ref.shape
    cols = wide - size
    room = n * cap
    body = wide - LANES
    half = size // 2
    inner, outer = jnp.maximum(place - 1, 0), jnp.minimum(place + 1, n_line - 1)
    top = n_line - 1

    barrier = pltpu.get_barrier_semaphore()
    for d in range(1, n):
        pl.semaphore_signal(
            barrier, inc=1, device_id={"surf": lax.rem(me + d, n)}, device_id_type=MESH
        )

    @pl.when(place < top)
    def _():
        pl.semaphore_signal(barrier, inc=1, device_id={"line": outer}, device_id_type=MESH)

    greeted = n - 1 + jnp.where(place > 0, 1, 0)
    core = lax.rem(me, 2)

    def on(at, core_only):
        here = place == at
        return here if core_only < 0 else jnp.logical_and(here, core == core_only)

    for far, mate, core_only in sorted({(far, mate, c) for far, _, mate, c in relays}):
        @pl.when(on(mate, core_only))
        def _():
            pl.semaphore_signal(
                barrier, inc=1, device_id={"surf": lax.rem(me + n // 2, n), "line": far},
                device_id_type=MESH,
            )

        @pl.when(on(far, core_only))
        def _():
            pl.semaphore_signal(barrier, inc=1, device_id={"line": mate}, device_id_type=MESH)

        greeted = greeted + jnp.where(
            jnp.logical_or(on(far, core_only), on(mate, core_only)), 1, 0
        )

    around = jnp.int32(0)
    for far, _, _, core_only in relays:
        around = around + jnp.where(on(far, core_only), 1, 0)
    held = jnp.logical_or(place == -1, place == -2)
    for mate in holders:
        held = jnp.logical_or(held, place == mate)

    upper = lax.broadcasted_iota(I32, (size, LANES), 1) >= cols
    upper_half = lax.broadcasted_iota(I32, (half, LANES), 1) >= cols
    upper_row = lax.broadcasted_iota(I32, (1, LANES), 1) >= cols
    eye = lax.broadcasted_iota(I32, (size, wide), 0) == lax.broadcasted_iota(
        I32, (size, wide), 1
    )

    def copies(d, slot):
        to = {"surf": lax.rem(me + d, n)}
        return (
            pltpu.make_async_remote_copy(
                src_ref=out_ref.at[slot], dst_ref=got_ref.at[slot],
                send_sem=send_sem.at[slot, 0], recv_sem=recv_sem.at[slot, 0],
                device_id=to, device_id_type=MESH,
            ),
            pltpu.make_async_remote_copy(
                src_ref=out_side_ref.at[slot], dst_ref=got_side_ref.at[slot],
                send_sem=send_sem.at[slot, 1], recv_sem=recv_sem.at[slot, 1],
                device_id=to, device_id_type=MESH,
            ),
        )

    def fill(slot):
        at = index_ref[slot]
        line, elem = index_ref[room + slot], index_ref[2 * room + slot]
        terms = dot(face_ref[at], adjoints_ref[line])
        terms = jnp.where(elem == 1, terms, pltpu.roll(terms, cols, 1))
        force = both_ref[at].astype(F32) - terms
        hi = force.astype(BF16).astype(F32)
        both = jnp.where(upper, hi, pltpu.roll(force - hi, cols, 1)).astype(BF16)
        moved = dot(inv_ref[at], both)
        moved = moved + pltpu.roll(moved, cols, 1)
        codes, scale = coded(moved)
        out_ref[slot, :, :body] = code_ref[at, :, :body]
        last = code_ref[at, :, body:].astype(I32)
        out_ref[slot, :, body:] = jnp.where(upper, codes, last).astype(I16)
        out_side_ref[slot, :, :body] = side_ref[at, :, :body]
        out_side_ref[slot, 0:1, body:] = jnp.where(upper_row, scale, side_ref[at, 0:1, body:])
        out_side_ref[slot, 1:2, body:] = side_ref[at, 1:2, body:]

    def decode(codes_at, sides_at, slot):
        value = codes_at[slot].astype(F32) * sides_at[slot, 0:1]
        value = value + jnp.where(eye, sides_at[slot, 1:2], 0.0)
        hi, lo = split(value)
        hi_ref[slot] = hi
        lo_ref[slot] = lo

    opposite = n // 2
    if n == 4:
        order = [(2, 1), (1, 2), (3, 3)]
    else:
        order = [(d, d) for d in sorted(range(1, n), key=lambda d: -min(d, n - d))]

    def pick(even, odd):
        return jnp.where(lax.rem(me, 2) == 0, even, odd)

    def first_leg(k, c):
        far, j, mate, _ = relays[k]
        part = pl.ds(c * half, half)
        return pltpu.make_async_remote_copy(
            src_ref=out_ref.at[opposite * cap + j, part], dst_ref=relay_ref.at[k, part],
            send_sem=leg_send.at[k, c], recv_sem=leg_recv.at[k, c],
            device_id={"surf": lax.rem(me + opposite, n), "line": mate}, device_id_type=MESH,
        )

    def second_leg(k, c):
        far, j, mate, _ = relays[k]
        part = pl.ds(c * half, half)
        return pltpu.make_async_remote_copy(
            src_ref=relay_ref.at[k, part], dst_ref=got_ref.at[opposite * cap + j, part],
            send_sem=on_send.at[k, c], recv_sem=on_recv.at[k, c],
            device_id={"line": far}, device_id_type=MESH,
        )

    def walk(offsets, visit):
        ends, total = [], 0
        for even, odd in offsets:
            total = total + pick(budgets[even], budgets[odd])
            ends.append(total)
        total = sum(budgets[even] for even, _ in offsets)

        def turn(i, _):
            d, start = pick(*offsets[-1]), ([0] + ends)[len(offsets) - 1]
            for p in reversed(range(len(offsets) - 1)):
                before = i < ends[p]
                d = jnp.where(before, pick(*offsets[p]), d)
                start = jnp.where(before, ([0] + ends)[p], start)
            visit(i, d, i - start)
            return 0

        lax.fori_loop(0, total, turn, 0)

    def direct(d, j):
        return jnp.logical_or(d != opposite, j >= around)

    def leave(i, d, j):
        slot = d * cap + j
        fill(slot)

        @pl.when(i == 0)
        def _():
            pl.semaphore_wait(barrier, greeted)

        @pl.when(d == 0)
        def _():
            decode(out_ref, out_side_ref, slot)

        @pl.when(jnp.logical_and(d > 0, jnp.logical_not(held)))
        def _():
            block, rows = copies(d, slot)
            rows.start()

            @pl.when(direct(d, j))
            def _():
                block.start()

            for k, (far, at, mate, core_only) in enumerate(relays):
                @pl.when(jnp.logical_and(on(far, core_only), slot == opposite * cap + at))
                def _():
                    first_leg(k, 0).start()
                    first_leg(k, 1).start()

    walk(order + [(0, 0)], leave)

    for c in range(2):
        for k, (far, j, mate, core_only) in enumerate(relays):
            @pl.when(on(mate, core_only))
            def _():
                first_leg(k, c).wait_recv()
                second_leg(k, c).start()

    if holders:
        @pl.when(held)
        def _():
            def release(_, d, j):
                for copy in copies(d, d * cap + j):
                    copy.start()

            walk(order, release)

    def arrive(_, d, j):
        slot = d * cap + j
        block, rows = copies(d, slot)
        rows.wait_recv()

        @pl.when(direct(d, j))
        def _():
            block.wait_recv()

        for k, (far, at, mate, core_only) in enumerate(relays):
            @pl.when(jnp.logical_and(on(far, core_only), slot == opposite * cap + at))
            def _():
                second_leg(k, 0).wait_recv()
                second_leg(k, 1).wait_recv()

        decode(got_ref, got_side_ref, slot)

    walk(order[::-1], arrive)

    def pass_on(l):
        return pltpu.make_async_remote_copy(
            src_ref=going.at[l], dst_ref=coming.at[l], send_sem=go_sem.at[l],
            recv_sem=come_sem.at[l], device_id={"line": inner}, device_id_type=MESH,
        )

    def carry(l, twice):
        packed = jnp.where(upper_half, twice[half:], twice[:half])
        most = jnp.maximum(jnp.max(jnp.abs(packed), axis=0, keepdims=True), TINY)
        power = jnp.ceil(jnp.log2(most) * 256.0)
        codes = jnp.round(packed * (CARRY_TOP * jnp.exp2(power * (-1.0 / 256.0))))
        going[l, :half] = codes.astype(I32).astype(I16)
        going[l, half:] = jnp.broadcast_to(power, (16, LANES)).astype(I32).astype(I16)

    def carried(l):
        power = coming[l, half:].astype(F32)[0:1]
        value = coming[l, :half].astype(F32) * (
            jnp.exp2(power * (1.0 / 256.0)) * (1.0 / CARRY_TOP)
        )
        hi = value.astype(BF16).astype(F32)
        lo = value - hi
        hi_turn, lo_turn = pltpu.roll(hi, cols, 1), pltpu.roll(lo, cols, 1)
        pair = jnp.concatenate(
            [jnp.where(upper_half, lo_turn, hi), jnp.where(upper_half, lo, hi_turn)], axis=0
        ).astype(BF16)
        same = jnp.concatenate(
            [jnp.where(upper_half, hi_turn, hi), jnp.where(upper_half, hi, hi_turn)], axis=0
        ).astype(BF16)
        return pair, same

    def applied(hi, lo, pair, same):
        first = dot(hi, pair)
        return first + (pltpu.roll(first, cols, 1) + dot(lo, same))

    def doubled(tile):
        return jnp.where(upper, tile, pltpu.roll(tile, cols, 1))

    def compose(l):
        inside = index_ref[3 * room + l * elems]
        outside = index_ref[3 * room + l * elems + 1]
        in_hi, in_lo = hi_ref[inside][:, :size], lo_ref[inside][:, :size]
        far_hi, far_lo = hi_ref[outside], lo_ref[outside]
        whole = dot(in_hi, far_hi) + (dot(in_hi, far_lo) + dot(in_lo, far_hi))
        tile = whole[:, body:] + (
            hi_ref[inside][:, body:].astype(F32) + lo_ref[inside][:, body:].astype(F32)
        )
        m_hi, m_lo = split(whole)
        map_hi[l] = m_hi
        map_lo[l] = m_lo
        twice = doubled(tile)
        shift[l] = twice

        @pl.when(place == top)
        def _():
            carry(l, twice)
            pass_on(l).start()

    @pl.when(place == top)
    def _():
        coming[...] = jnp.zeros_like(coming)

    def step(l):
        pass_on(l).wait_recv()
        pair, same = carried(l)
        twice = shift[l] + applied(map_hi[l][:, :size], map_lo[l][:, :size], pair, same)

        @pl.when(place > 0)
        def _():
            carry(l, twice)
            pass_on(l).start()

        shift[l] = twice

    def finish(l):
        pair, same = carried(l)
        outside = index_ref[3 * room + l * elems + 1]
        far_hi, far_lo = hi_ref[outside], lo_ref[outside]
        first = doubled(far_hi[:, body:].astype(F32) + far_lo[:, body:].astype(F32))
        first = first + applied(far_hi[:, :size], far_lo[:, :size], pair, same)
        result_ref[l] = jnp.where(upper, first, shift[l]).astype(BF16).T

    def turn(i, _):
        early, late = place == top - 1, place == 0
        pairs_from = jnp.where(early, 0, jnp.where(late, lines, 3 * lines))
        paired = jnp.logical_and(i >= pairs_from, i < pairs_from + 2 * lines)
        stage = jnp.where(paired, pairs_from // lines + lax.rem(i, 2), i // lines)
        l = jnp.where(paired, (i - pairs_from) // 2, lax.rem(i, lines))

        @pl.when(stage == 0)
        def _():
            compose(l)

        @pl.when(jnp.logical_and(stage == 1, place < top))
        def _():
            step(l)

        @pl.when(stage == 2)
        def _():
            finish(l)

        return 0

    lax.fori_loop(0, 3 * lines, turn, 0)

    @pl.when(place > 0)
    def _():
        def gone(l, _):
            pass_on(l).wait_send()
            return 0

        lax.fori_loop(0, lines, gone, 0)

    for k, (far, j, mate, core_only) in enumerate(relays):
        @pl.when(on(far, core_only))
        def _():
            first_leg(k, 0).wait_send()
            first_leg(k, 1).wait_send()

        @pl.when(on(mate, core_only))
        def _():
            second_leg(k, 0).wait_send()
            second_leg(k, 1).wait_send()

    def left(_, d, j):
        block, rows = copies(d, d * cap + j)
        rows.wait_send()

        @pl.when(direct(d, j))
        def _():
            block.wait_send()

    walk(order, left)


def relays_of(n, n_line, budgets):
    if n != 4 or n_line != 8:
        return (), ()
    crossing = 2 * budgets[2] + budgets[1] + budgets[3]
    if budgets[2] < 2 or crossing < 8:
        return (), ()
    relays = ((7, 0, 1, -1),)
    if crossing > 8:
        relays += ((7, 1, 3, 1), (6, 0, 0, -1), (5, 0, 2, 1))
    return relays, (0, 1) if crossing > 8 else (1,)


def swept(n, n_line, cap, lines, elems, plan, budgets, index, inv, face, both, adjoints,
          codes, sides):
    stored, size, wide = codes.shape
    cols = wide - size
    vmem = pl.BlockSpec(memory_space=pltpu.VMEM)
    room = n * cap
    coded_blocks = pltpu.VMEM((room, size, wide), I16)
    side_rows = pltpu.VMEM((room, 2, wide), F32)
    parts = pltpu.VMEM((room, size, wide), BF16)
    maps = pltpu.VMEM((lines, size, wide), BF16)
    message = pltpu.VMEM((lines, size // 2 + 16, LANES), I16)
    relays, holders = relays_of(n, n_line, budgets)
    legs = pltpu.SemaphoreType.DMA((max(len(relays), 1), 2))
    return pl.pallas_call(
        functools.partial(
            sweep_kernel, n, n_line, cap, lines, elems, budgets, relays, holders
        ),
        out_shape=jax.ShapeDtypeStruct((lines, elems * cols, size), BF16),
        in_specs=[pl.BlockSpec(memory_space=pltpu.SMEM)] + [vmem] * 6,
        out_specs=vmem,
        scratch_shapes=[
            coded_blocks, side_rows, coded_blocks, side_rows, parts, parts, maps, maps,
            pltpu.VMEM((lines, size, LANES), F32),
            message, message,
            pltpu.VMEM((max(len(relays), 1), size, wide), I16),
            pltpu.SemaphoreType.DMA((room, 2)),
            pltpu.SemaphoreType.DMA((room, 2)),
            pltpu.SemaphoreType.DMA((lines,)),
            pltpu.SemaphoreType.DMA((lines,)),
            legs, legs, legs, legs,
        ],
        compiler_params=pltpu.CompilerParams(
            collective_id=1 + plan, has_side_effects=True, vmem_limit_bytes=40 << 20
        ),
    )(index, inv, face, both, adjoints, codes, sides)


def plans_of(n, cap):
    plans = []
    if n == 4 and cap % 2 == 0:
        for empty in (0, 2, 3):
            for double in range(n):
                if double != empty:
                    plans.append(tuple(
                        cap if d == double else 0 if d == empty else cap // 2
                        for d in range(n)
                    ))
    return plans + [(cap,) * n]


def per_device(n_surf, n_line, inv_block, couple_block, face_block, rhs, adjoint_prev,
               nb_line, send_list, send_count, recv_list):
    lines, elems, size, _ = inv_block.shape
    cols = rhs.shape[3]
    cap = send_list.shape[2]
    plans = plans_of(n_surf, cap)
    index, plan, adjoints, both, codes, sides = gathered(
        n_surf, cap, plans, recv_list, nb_line, send_count, send_list,
        jnp.swapaxes(adjoint_prev, 2, 3), jnp.swapaxes(rhs, 2, 3), inv_block, couple_block,
    )
    inv = inv_block.reshape(lines * elems, size, size)
    face = face_block.reshape(lines * elems, size, size)

    def branch(p):
        return lambda: swept(
            n_surf, n_line, cap, lines, elems, p, plans[p], index, inv, face, both, adjoints,
            codes, sides,
        )

    if len(plans) > 1:
        result = lax.switch(plan[0], [branch(p) for p in range(len(plans))])
    else:
        result = branch(0)()
    return jnp.swapaxes(result.reshape(lines, elems, cols, size), 2, 3)


def solution(mesh):
    whole = P("surf", "line", None, None)
    in_specs = (
        whole, whole, whole, whole, whole,
        P("surf"), P("surf", None, None), P("surf", None), P("surf", None, None),
    )
    body = functools.partial(per_device, mesh.shape["surf"], mesh.shape["line"])
    return jax.shard_map(
        body, mesh=mesh, in_specs=in_specs, out_specs=whole, check_vma=False
    )
```

```python
import functools

import jax
import jax.numpy as jnp
from jax import lax
from jax.experimental import pallas as pl
from jax.experimental.pallas import tpu as pltpu
from jax.sharding import PartitionSpec as P

MESH = pl.DeviceIdType.MESH
F32 = jnp.float32
BF16 = jnp.bfloat16
I16 = jnp.int16
I32 = jnp.int32
LANES = 128
TOP = 32767.0
TINY = 1e-30
CARRY_TOP = 32700.0


def dot(a, b):
    return jnp.dot(a, b, preferred_element_type=F32)


def split(value):
    high = value.astype(BF16)
    return high, (value - high.astype(F32)).astype(BF16)


def diagonal(size):
    return lax.broadcasted_iota(I32, (size, size), 0) == lax.broadcasted_iota(
        I32, (size, size), 1
    )


def coded(value):
    most = jnp.maximum(jnp.max(jnp.abs(value), axis=0, keepdims=True), TINY)
    return jnp.round(value * (TOP / most)).astype(I32), most * (1.0 / TOP)


def gather_kernel(
    n, cap, plans, recv_list_hbm, nb_hbm, count_hbm, send_list_hbm, adjoint_hbm, rhs_hbm,
    inv_hbm, couple_hbm,
    index_ref, plan_ref, adjoints_ref, both_ref, code_ref, side_ref,
    recv_list_ref, nb_ref, count_ref, send_list_ref, adjoint_ref, rhs_ref,
    places_ref, nbs_ref, counts_ref, inv_ref, couple_ref,
    first_sem, load_sem, table_send, table_recv, send_sem, recv_sem,
):
    me = lax.axis_index("surf")
    lines, elems = adjoint_ref.shape[:2]
    size = inv_ref.shape[1]
    stored = lines * elems
    chips = n // 2
    core, chip = lax.rem(me, 2), me // 2
    partner = me + 1 - 2 * core

    def loads(b):
        at = (b // elems, b % elems)
        return (
            pltpu.make_async_copy(inv_hbm.at[at], inv_ref.at[b], load_sem.at[b, 0]),
            pltpu.make_async_copy(couple_hbm.at[at], couple_ref.at[b], load_sem.at[b, 1]),
        )

    first = [
        pltpu.make_async_copy(source, goal, first_sem.at[i])
        for i, (source, goal) in enumerate((
            (adjoint_hbm, adjoint_ref), (recv_list_hbm, recv_list_ref), (nb_hbm, nb_ref),
            (count_hbm, count_ref), (send_list_hbm, send_list_ref), (rhs_hbm, rhs_ref),
        ))
    ]
    for load in first:
        load.start()
    barrier = pltpu.get_barrier_semaphore()
    for d in range(1, n):
        pl.semaphore_signal(
            barrier, inc=1, device_id={"surf": lax.rem(me + d, n)}, device_id_type=MESH
        )
    for b in range(stored):
        for load in loads(b):
            load.start()
    for load in first:
        load.wait()

    for l in range(lines):
        stack = jnp.concatenate([adjoint_ref[l, e] for e in range(elems)], axis=0)
        adjoints_ref[me * lines + l] = stack.T

    pl.semaphore_wait(barrier, n - 1)

    def tables(d, owner):
        return [
            pltpu.make_async_remote_copy(
                src_ref=source, dst_ref=goal.at[owner], send_sem=table_send.at[d, i],
                recv_sem=table_recv.at[d, i], device_id={"surf": lax.rem(me + d, n)},
                device_id_type=MESH,
            )
            for i, (source, goal) in enumerate((
                (recv_list_ref.at[0], places_ref), (nb_ref, nbs_ref),
                (count_ref.at[0], counts_ref),
            ))
        ]

    def line_copy(owner, l, way, to):
        row = owner * lines + l
        return pltpu.make_async_remote_copy(
            src_ref=adjoints_ref.at[row], dst_ref=adjoints_ref.at[row],
            send_sem=send_sem.at[way, l], recv_sem=recv_sem.at[row],
            device_id={"surf": to}, device_id_type=MESH,
        )

    def across(k):
        return lax.rem(chip + k, chips) * 2 + core

    for d in range(1, n):
        for copy in tables(d, me):
            copy.start()
    for l in range(lines):
        for k in range(1, chips):
            line_copy(me, l, k, across(k)).start()
    for l in range(lines):
        line_copy(me, l, 0, partner).start()

    for s in range(n):
        for j in range(cap):
            places_ref[me, s, j] = recv_list_ref[0, s, j]
        counts_ref[me, s] = count_ref[0, s]
    for l in range(lines):
        nbs_ref[me, l] = nb_ref[l]

    eye = diagonal(size)

    def product(b):
        for load in loads(b):
            load.wait()
        value = -dot(inv_ref[b], couple_ref[b])
        main = jnp.sum(jnp.where(eye, value, 0.0), axis=0, keepdims=True)
        main = main.astype(BF16).astype(F32)
        codes, scale = coded(value - jnp.where(eye, main, 0.0))
        code_ref[b, :, :size] = codes.astype(I16)
        side_ref[b, 0:1, :size] = scale
        side_ref[b, 1:2, :size] = main
        rhs = rhs_ref[b // elems, b % elems]
        both_ref[b] = jnp.concatenate([rhs, rhs], axis=0).T

    def relay(l):
        for k in range(1, chips):
            source = across(k)
            line_copy(source, l, k, partner).wait_recv()
            line_copy(source, l, chips - 1 + k, partner).start()

    lax.fori_loop(0, stored, lambda b, _: (product(b), 0)[1], 0)

    for d in range(1, n):
        for copy in tables(d, lax.rem(me + n - d, n)):
            copy.wait_recv()
        for copy in tables(d, me):
            copy.wait_send()
    index_table(n, lines, elems, cap, plans, me, places_ref, nbs_ref, counts_ref,
                send_list_ref, index_ref, plan_ref)

    for l in range(lines):
        relay(l)
    for l in range(lines):
        line_copy(partner, l, 0, partner).wait_recv()
        for k in range(1, chips):
            other = across(k)
            line_copy(other + 1 - 2 * core, l, 0, partner).wait_recv()
            line_copy(me, l, k, other).wait_send()
            line_copy(other, l, chips - 1 + k, partner).wait_send()
        line_copy(me, l, 0, partner).wait_send()


def index_table(n, lines, elems, cap, plans, me, places, nbs, counts, sends, out_ref, plan_ref):
    stored = lines * elems
    room = n * cap
    for d in range(n):
        to = lax.rem(me + d, n)
        here = counts[me, to]
        for j in range(cap):
            used = j < here
            goal = jnp.where(used, places[to, me, j], 0)
            slot = d * cap + j
            out_ref[slot] = jnp.where(used, sends[0, to, j], 0)
            line = goal // elems
            out_ref[room + slot] = nbs[to, line]
            out_ref[2 * room + slot] = goal - line * elems
    for q in range(stored):
        value = jnp.int32(0)
        for d in range(n):
            source = lax.rem(me + n - d, n)
            for j in range(cap):
                hit = jnp.logical_and(j < counts[source, me], places[me, source, j] == q)
                value = jnp.where(hit, d * cap + j, value)
        out_ref[3 * room + q] = value

    best = jnp.int32(len(plans) - 1)
    most = []
    for d in range(n):
        value = counts[0, d]
        for s in range(1, n):
            value = jnp.maximum(value, counts[s, (s + d) % n])
        most.append(value)
    for p in reversed(range(len(plans) - 1)):
        fits = most[0] <= plans[p][0]
        for d in range(1, n):
            fits = jnp.logical_and(fits, most[d] <= plans[p][d])
        best = jnp.where(fits, p, best)
    plan_ref[0] = best


def gathered(n, cap, plans, recv_list, nb_line, send_count, send_list, adjoint_t, rhs_t,
             inv_block, couple_block):
    lines, elems, cols, size = adjoint_t.shape
    stored, wide = lines * elems, size + cols
    chips = n // 2
    vmem, hbm = pl.BlockSpec(memory_space=pltpu.VMEM), pl.BlockSpec(memory_space=pl.ANY)
    smem = pl.BlockSpec(memory_space=pltpu.SMEM)
    return pl.pallas_call(
        functools.partial(gather_kernel, n, cap, plans),
        out_shape=(
            jax.ShapeDtypeStruct((LANES,), I32),
            jax.ShapeDtypeStruct((1,), I32),
            jax.ShapeDtypeStruct((n * lines, size, elems * cols), BF16),
            jax.ShapeDtypeStruct((stored, size, 2 * cols), BF16),
            jax.ShapeDtypeStruct((stored, size, wide), I16),
            jax.ShapeDtypeStruct((stored, 2, wide), F32),
        ),
        in_specs=[hbm] * 8,
        out_specs=(smem, smem) + (vmem,) * 4,
        scratch_shapes=[
            pltpu.SMEM(recv_list.shape, I32),
            pltpu.SMEM(nb_line.shape, I32),
            pltpu.SMEM(send_count.shape, I32),
            pltpu.SMEM(send_list.shape, I32),
            pltpu.VMEM(adjoint_t.shape, BF16),
            pltpu.VMEM(rhs_t.shape, BF16),
            pltpu.SMEM((n, n, cap), I32),
            pltpu.SMEM((n, lines), I32),
            pltpu.SMEM((n, n), I32),
            pltpu.VMEM((stored, size, size), BF16),
            pltpu.VMEM((stored, size, size), BF16),
            pltpu.SemaphoreType.DMA((6,)),
            pltpu.SemaphoreType.DMA((stored, 2)),
            pltpu.SemaphoreType.DMA((n, 3)),
            pltpu.SemaphoreType.DMA((n, 3)),
            pltpu.SemaphoreType.DMA((2 * chips - 1, lines)),
            pltpu.SemaphoreType.DMA((n * lines,)),
        ],
        compiler_params=pltpu.CompilerParams(
            collective_id=0, has_side_effects=True, vmem_limit_bytes=54 << 20
        ),
    )(recv_list, nb_line, send_count, send_list, adjoint_t, rhs_t, inv_block, couple_block)


def sweep_kernel(
    n, n_line, cap, lines, elems, budgets, relays, holders,
    index_ref, inv_ref, face_ref, both_ref, adjoints_ref, code_ref, side_ref,
    result_hbm, result_ref, out_ref, out_side_ref, got_ref, got_side_ref, hi_ref, lo_ref,
    map_hi, map_lo, shift, going, coming, relay_ref,
    send_sem, recv_sem, go_sem, come_sem, leg_send, leg_recv, on_send, on_recv, done_sem,
):
    me, place = lax.axis_index("surf"), lax.axis_index("line")
    _, size, wide = code_ref.shape
    cols = wide - size
    room = n * cap
    body = wide - LANES
    half = size // 2
    inner, outer = jnp.maximum(place - 1, 0), jnp.minimum(place + 1, n_line - 1)
    top = n_line - 1

    barrier = pltpu.get_barrier_semaphore()
    for d in range(1, n):
        pl.semaphore_signal(
            barrier, inc=1, device_id={"surf": lax.rem(me + d, n)}, device_id_type=MESH
        )

    @pl.when(place < top)
    def _():
        pl.semaphore_signal(barrier, inc=1, device_id={"line": outer}, device_id_type=MESH)

    greeted = n - 1 + jnp.where(place > 0, 1, 0)
    core = lax.rem(me, 2)

    def on(at, core_only):
        here = place == at
        return here if core_only < 0 else jnp.logical_and(here, core == core_only)

    for far, mate, core_only in sorted({(far, mate, c) for far, _, mate, c in relays}):
        @pl.when(on(mate, core_only))
        def _():
            pl.semaphore_signal(
                barrier, inc=1, device_id={"surf": lax.rem(me + n // 2, n), "line": far},
                device_id_type=MESH,
            )

        @pl.when(on(far, core_only))
        def _():
            pl.semaphore_signal(barrier, inc=1, device_id={"line": mate}, device_id_type=MESH)

        greeted = greeted + jnp.where(
            jnp.logical_or(on(far, core_only), on(mate, core_only)), 1, 0
        )

    around = jnp.int32(0)
    for far, _, _, core_only in relays:
        around = around + jnp.where(on(far, core_only), 1, 0)
    held = jnp.logical_or(place == -1, place == -2)
    for mate in holders:
        held = jnp.logical_or(held, place == mate)

    upper = lax.broadcasted_iota(I32, (size, LANES), 1) >= cols
    upper_half = lax.broadcasted_iota(I32, (half, LANES), 1) >= cols
    upper_row = lax.broadcasted_iota(I32, (1, LANES), 1) >= cols
    eye = lax.broadcasted_iota(I32, (size, wide), 0) == lax.broadcasted_iota(
        I32, (size, wide), 1
    )

    def copies(d, slot):
        to = {"surf": lax.rem(me + d, n)}
        return (
            pltpu.make_async_remote_copy(
                src_ref=out_ref.at[slot], dst_ref=got_ref.at[slot],
                send_sem=send_sem.at[slot, 0], recv_sem=recv_sem.at[slot, 0],
                device_id=to, device_id_type=MESH,
            ),
            pltpu.make_async_remote_copy(
                src_ref=out_side_ref.at[slot], dst_ref=got_side_ref.at[slot],
                send_sem=send_sem.at[slot, 1], recv_sem=recv_sem.at[slot, 1],
                device_id=to, device_id_type=MESH,
            ),
        )

    def fill(slot):
        at = index_ref[slot]
        line, elem = index_ref[room + slot], index_ref[2 * room + slot]
        terms = dot(face_ref[at], adjoints_ref[line])
        terms = jnp.where(elem == 1, terms, pltpu.roll(terms, cols, 1))
        force = both_ref[at].astype(F32) - terms
        hi = force.astype(BF16).astype(F32)
        both = jnp.where(upper, hi, pltpu.roll(force - hi, cols, 1)).astype(BF16)
        moved = dot(inv_ref[at], both)
        moved = moved + pltpu.roll(moved, cols, 1)
        codes, scale = coded(moved)
        out_ref[slot, :, :body] = code_ref[at, :, :body]
        last = code_ref[at, :, body:].astype(I32)
        out_ref[slot, :, body:] = jnp.where(upper, codes, last).astype(I16)
        out_side_ref[slot, :, :body] = side_ref[at, :, :body]
        out_side_ref[slot, 0:1, body:] = jnp.where(upper_row, scale, side_ref[at, 0:1, body:])
        out_side_ref[slot, 1:2, body:] = side_ref[at, 1:2, body:]

    def decode(codes_at, sides_at, slot):
        value = codes_at[slot].astype(F32) * sides_at[slot, 0:1]
        value = value + jnp.where(eye, sides_at[slot, 1:2], 0.0)
        hi, lo = split(value)
        hi_ref[slot] = hi
        lo_ref[slot] = lo

    opposite = n // 2
    if n == 4:
        order = [(2, 1), (1, 2), (3, 3)]
    else:
        order = [(d, d) for d in sorted(range(1, n), key=lambda d: -min(d, n - d))]

    def pick(even, odd):
        return jnp.where(lax.rem(me, 2) == 0, even, odd)

    def first_leg(k, c):
        far, j, mate, _ = relays[k]
        part = pl.ds(c * half, half)
        return pltpu.make_async_remote_copy(
            src_ref=out_ref.at[opposite * cap + j, part], dst_ref=relay_ref.at[k, part],
            send_sem=leg_send.at[k, c], recv_sem=leg_recv.at[k, c],
            device_id={"surf": lax.rem(me + opposite, n), "line": mate}, device_id_type=MESH,
        )

    def second_leg(k, c):
        far, j, mate, _ = relays[k]
        part = pl.ds(c * half, half)
        return pltpu.make_async_remote_copy(
            src_ref=relay_ref.at[k, part], dst_ref=got_ref.at[opposite * cap + j, part],
            send_sem=on_send.at[k, c], recv_sem=on_recv.at[k, c],
            device_id={"line": far}, device_id_type=MESH,
        )

    def walk(offsets, visit):
        ends, total = [], 0
        for even, odd in offsets:
            total = total + pick(budgets[even], budgets[odd])
            ends.append(total)
        total = sum(budgets[even] for even, _ in offsets)

        def turn(i, _):
            d, start = pick(*offsets[-1]), ([0] + ends)[len(offsets) - 1]
            for p in reversed(range(len(offsets) - 1)):
                before = i < ends[p]
                d = jnp.where(before, pick(*offsets[p]), d)
                start = jnp.where(before, ([0] + ends)[p], start)
            visit(i, d, i - start)
            return 0

        lax.fori_loop(0, total, turn, 0)

    def direct(d, j):
        return jnp.logical_or(d != opposite, j >= around)

    def leave(i, d, j):
        slot = d * cap + j
        fill(slot)

        @pl.when(i == 0)
        def _():
            pl.semaphore_wait(barrier, greeted)

        @pl.when(d == 0)
        def _():
            decode(out_ref, out_side_ref, slot)

        @pl.when(jnp.logical_and(d > 0, jnp.logical_not(held)))
        def _():
            block, rows = copies(d, slot)
            rows.start()

            @pl.when(direct(d, j))
            def _():
                block.start()

            for k, (far, at, mate, core_only) in enumerate(relays):
                @pl.when(jnp.logical_and(on(far, core_only), slot == opposite * cap + at))
                def _():
                    first_leg(k, 0).start()
                    first_leg(k, 1).start()

    walk(order + [(0, 0)], leave)

    for c in range(2):
        for k, (far, j, mate, core_only) in enumerate(relays):
            @pl.when(on(mate, core_only))
            def _():
                first_leg(k, c).wait_recv()
                second_leg(k, c).start()

    if holders:
        @pl.when(held)
        def _():
            def release(_, d, j):
                for copy in copies(d, d * cap + j):
                    copy.start()

            walk(order, release)

    def arrive(_, d, j):
        slot = d * cap + j
        block, rows = copies(d, slot)
        rows.wait_recv()

        @pl.when(direct(d, j))
        def _():
            block.wait_recv()

        for k, (far, at, mate, core_only) in enumerate(relays):
            @pl.when(jnp.logical_and(on(far, core_only), slot == opposite * cap + at))
            def _():
                second_leg(k, 0).wait_recv()
                second_leg(k, 1).wait_recv()

        decode(got_ref, got_side_ref, slot)

    walk(order[::-1], arrive)

    def pass_on(l):
        return pltpu.make_async_remote_copy(
            src_ref=going.at[l], dst_ref=coming.at[l], send_sem=go_sem.at[l],
            recv_sem=come_sem.at[l], device_id={"line": inner}, device_id_type=MESH,
        )

    def carry(l, twice):
        packed = jnp.where(upper_half, twice[half:], twice[:half])
        most = jnp.maximum(jnp.max(jnp.abs(packed), axis=0, keepdims=True), TINY)
        power = jnp.ceil(jnp.log2(most) * 256.0)
        codes = jnp.round(packed * (CARRY_TOP * jnp.exp2(power * (-1.0 / 256.0))))
        going[l, :half] = codes.astype(I32).astype(I16)
        going[l, half:] = jnp.broadcast_to(power, (16, LANES)).astype(I32).astype(I16)

    def carried(l):
        power = coming[l, half:].astype(F32)[0:1]
        value = coming[l, :half].astype(F32) * (
            jnp.exp2(power * (1.0 / 256.0)) * (1.0 / CARRY_TOP)
        )
        hi = value.astype(BF16).astype(F32)
        lo = value - hi
        hi_turn, lo_turn = pltpu.roll(hi, cols, 1), pltpu.roll(lo, cols, 1)
        pair = jnp.concatenate(
            [jnp.where(upper_half, lo_turn, hi), jnp.where(upper_half, lo, hi_turn)], axis=0
        ).astype(BF16)
        same = jnp.concatenate(
            [jnp.where(upper_half, hi_turn, hi), jnp.where(upper_half, hi, hi_turn)], axis=0
        ).astype(BF16)
        return pair, same

    def applied(hi, lo, pair, same):
        first = dot(hi, pair)
        return first + (pltpu.roll(first, cols, 1) + dot(lo, same))

    def doubled(tile):
        return jnp.where(upper, tile, pltpu.roll(tile, cols, 1))

    def compose(l):
        inside = index_ref[3 * room + l * elems]
        outside = index_ref[3 * room + l * elems + 1]
        in_hi, in_lo = hi_ref[inside][:, :size], lo_ref[inside][:, :size]
        far_hi, far_lo = hi_ref[outside], lo_ref[outside]
        whole = dot(in_hi, far_hi) + (dot(in_hi, far_lo) + dot(in_lo, far_hi))
        tile = whole[:, body:] + (
            hi_ref[inside][:, body:].astype(F32) + lo_ref[inside][:, body:].astype(F32)
        )
        m_hi, m_lo = split(whole)
        map_hi[l] = m_hi
        map_lo[l] = m_lo
        twice = doubled(tile)
        shift[l] = twice

        @pl.when(place == top)
        def _():
            carry(l, twice)
            pass_on(l).start()

    @pl.when(place == top)
    def _():
        coming[...] = jnp.zeros_like(coming)

    def step(l):
        pass_on(l).wait_recv()
        pair, same = carried(l)
        twice = shift[l] + applied(map_hi[l][:, :size], map_lo[l][:, :size], pair, same)

        @pl.when(place > 0)
        def _():
            carry(l, twice)
            pass_on(l).start()

        shift[l] = twice

    def leaving(l):
        return pltpu.make_async_copy(result_ref.at[l], result_hbm.at[l], done_sem.at[l])

    def finish(l):
        pair, same = carried(l)
        outside = index_ref[3 * room + l * elems + 1]
        far_hi, far_lo = hi_ref[outside], lo_ref[outside]
        first = doubled(far_hi[:, body:].astype(F32) + far_lo[:, body:].astype(F32))
        first = first + applied(far_hi[:, :size], far_lo[:, :size], pair, same)
        result_ref[l] = jnp.where(upper, first, shift[l]).astype(BF16).T
        leaving(l).start()

    def turn(i, _):
        early, late = place == top - 1, place == 0
        pairs_from = jnp.where(early, 0, jnp.where(late, lines, 3 * lines))
        paired = jnp.logical_and(i >= pairs_from, i < pairs_from + 2 * lines)
        stage = jnp.where(paired, pairs_from // lines + lax.rem(i, 2), i // lines)
        l = jnp.where(paired, (i - pairs_from) // 2, lax.rem(i, lines))

        @pl.when(stage == 0)
        def _():
            compose(l)

        @pl.when(jnp.logical_and(stage == 1, place < top))
        def _():
            step(l)

        @pl.when(stage == 2)
        def _():
            finish(l)

        return 0

    lax.fori_loop(0, 3 * lines, turn, 0)

    def finished(l, _):
        leaving(l).wait()
        return 0

    lax.fori_loop(0, lines, finished, 0)

    @pl.when(place > 0)
    def _():
        def gone(l, _):
            pass_on(l).wait_send()
            return 0

        lax.fori_loop(0, lines, gone, 0)

    for k, (far, j, mate, core_only) in enumerate(relays):
        @pl.when(on(far, core_only))
        def _():
            first_leg(k, 0).wait_send()
            first_leg(k, 1).wait_send()

        @pl.when(on(mate, core_only))
        def _():
            second_leg(k, 0).wait_send()
            second_leg(k, 1).wait_send()

    def left(_, d, j):
        block, rows = copies(d, d * cap + j)
        rows.wait_send()

        @pl.when(direct(d, j))
        def _():
            block.wait_send()

    walk(order, left)


def relays_of(n, n_line, budgets):
    if n != 4 or n_line != 8:
        return (), ()
    crossing = 2 * budgets[2] + budgets[1] + budgets[3]
    if budgets[2] < 2 or crossing < 8:
        return (), ()
    relays = ((7, 0, 1, -1),)
    if crossing > 8:
        relays += ((7, 1, 3, -1 if budgets[1] > budgets[2] else 1), (6, 0, 0, -1), (5, 0, 2, -1))
    return relays, (0, 1) if crossing > 8 else (1,)


def swept(n, n_line, cap, lines, elems, plan, budgets, index, inv, face, both, adjoints,
          codes, sides):
    stored, size, wide = codes.shape
    cols = wide - size
    vmem = pl.BlockSpec(memory_space=pltpu.VMEM)
    room = n * cap
    coded_blocks = pltpu.VMEM((room, size, wide), I16)
    side_rows = pltpu.VMEM((room, 2, wide), F32)
    parts = pltpu.VMEM((room, size, wide), BF16)
    maps = pltpu.VMEM((lines, size, wide), BF16)
    message = pltpu.VMEM((lines, size // 2 + 16, LANES), I16)
    relays, holders = relays_of(n, n_line, budgets)
    legs = pltpu.SemaphoreType.DMA((max(len(relays), 1), 2))
    return pl.pallas_call(
        functools.partial(
            sweep_kernel, n, n_line, cap, lines, elems, budgets, relays, holders
        ),
        out_shape=jax.ShapeDtypeStruct((lines, elems * cols, size), BF16),
        in_specs=[pl.BlockSpec(memory_space=pltpu.SMEM)] + [vmem] * 6,
        out_specs=pl.BlockSpec(memory_space=pl.ANY),
        scratch_shapes=[
            pltpu.VMEM((lines, elems * cols, size), BF16),
            coded_blocks, side_rows, coded_blocks, side_rows, parts, parts, maps, maps,
            pltpu.VMEM((lines, size, LANES), F32),
            message, message,
            pltpu.VMEM((max(len(relays), 1), size, wide), I16),
            pltpu.SemaphoreType.DMA((room, 2)),
            pltpu.SemaphoreType.DMA((room, 2)),
            pltpu.SemaphoreType.DMA((lines,)),
            pltpu.SemaphoreType.DMA((lines,)),
            legs, legs, legs, legs, pltpu.SemaphoreType.DMA((lines,)),
        ],
        compiler_params=pltpu.CompilerParams(
            collective_id=1 + plan, has_side_effects=True, vmem_limit_bytes=40 << 20
        ),
    )(index, inv, face, both, adjoints, codes, sides)


def plans_of(n, cap):
    plans = []
    if n == 4 and cap % 2 == 0:
        for empty in (0, 2, 3):
            for double in range(n):
                if double != empty:
                    plans.append(tuple(
                        cap if d == double else 0 if d == empty else cap // 2
                        for d in range(n)
                    ))
    return plans + [(cap,) * n]


def per_device(n_surf, n_line, inv_block, couple_block, face_block, rhs, adjoint_prev,
               nb_line, send_list, send_count, recv_list):
    lines, elems, size, _ = inv_block.shape
    cols = rhs.shape[3]
    cap = send_list.shape[2]
    plans = plans_of(n_surf, cap)
    index, plan, adjoints, both, codes, sides = gathered(
        n_surf, cap, plans, recv_list, nb_line, send_count, send_list,
        jnp.swapaxes(adjoint_prev, 2, 3), jnp.swapaxes(rhs, 2, 3), inv_block, couple_block,
    )
    inv = inv_block.reshape(lines * elems, size, size)
    face = face_block.reshape(lines * elems, size, size)

    def branch(p):
        return lambda: swept(
            n_surf, n_line, cap, lines, elems, p, plans[p], index, inv, face, both, adjoints,
            codes, sides,
        )

    if len(plans) > 1:
        result = lax.switch(plan[0], [branch(p) for p in range(len(plans))])
    else:
        result = branch(0)()
    return jnp.swapaxes(result.reshape(lines, elems, cols, size), 2, 3)


def solution(mesh):
    whole = P("surf", "line", None, None)
    in_specs = (
        whole, whole, whole, whole, whole,
        P("surf"), P("surf", None, None), P("surf", None), P("surf", None, None),
    )
    body = functools.partial(per_device, mesh.shape["surf"], mesh.shape["line"])
    return jax.shard_map(
        body, mesh=mesh, in_specs=in_specs, out_specs=whole, check_vma=False
    )
```

```python
import functools

import jax
import jax.numpy as jnp
from jax import lax
from jax.experimental import pallas as pl
from jax.experimental.pallas import tpu as pltpu
from jax.sharding import PartitionSpec as P

MESH = pl.DeviceIdType.MESH
F32 = jnp.float32
BF16 = jnp.bfloat16
I16 = jnp.int16
I32 = jnp.int32
LANES = 128
TOP = 32767.0
TINY = 1e-33
CARRY_BITS = 14.99


def dot(a, b):
    return jnp.dot(a, b, preferred_element_type=F32)


def split(value):
    high = value.astype(BF16)
    return high, (value - high.astype(F32)).astype(BF16)


def diagonal(size):
    return lax.broadcasted_iota(I32, (size, size), 0) == lax.broadcasted_iota(
        I32, (size, size), 1
    )


def coded(value):
    most = jnp.maximum(jnp.max(jnp.abs(value), axis=0, keepdims=True), TINY)
    return jnp.round(value * (TOP / most)).astype(I32), most * (1.0 / TOP)


def gather_kernel(
    n, cap, plans, recv_list_hbm, nb_hbm, count_hbm, send_list_hbm, adjoint_hbm, rhs_hbm,
    inv_hbm, couple_hbm,
    index_ref, plan_ref, adjoints_ref, both_ref, code_ref, side_ref,
    recv_list_ref, nb_ref, count_ref, send_list_ref, adjoint_ref, rhs_ref,
    places_ref, nbs_ref, counts_ref, inv_ref, couple_ref,
    first_sem, load_sem, table_send, table_recv, send_sem, recv_sem,
):
    me = lax.axis_index("surf")
    lines, elems = adjoint_ref.shape[:2]
    size = inv_ref.shape[1]
    stored = lines * elems
    chips = n // 2
    core, chip = lax.rem(me, 2), me // 2
    partner = me + 1 - 2 * core

    def loads(b):
        at = (b // elems, b % elems)
        return (
            pltpu.make_async_copy(inv_hbm.at[at], inv_ref.at[b], load_sem.at[b, 0]),
            pltpu.make_async_copy(couple_hbm.at[at], couple_ref.at[b], load_sem.at[b, 1]),
        )

    first = [
        pltpu.make_async_copy(source, goal, first_sem.at[i])
        for i, (source, goal) in enumerate((
            (adjoint_hbm, adjoint_ref), (recv_list_hbm, recv_list_ref), (nb_hbm, nb_ref),
            (count_hbm, count_ref), (send_list_hbm, send_list_ref), (rhs_hbm, rhs_ref),
        ))
    ]
    for load in first:
        load.start()
    barrier = pltpu.get_barrier_semaphore()
    for d in range(1, n):
        pl.semaphore_signal(
            barrier, inc=1, device_id={"surf": lax.rem(me + d, n)}, device_id_type=MESH
        )
    for b in range(stored):
        for load in loads(b):
            load.start()
    for load in first:
        load.wait()

    for l in range(lines):
        stack = jnp.concatenate([adjoint_ref[l, e] for e in range(elems)], axis=0)
        adjoints_ref[me * lines + l] = stack.T

    pl.semaphore_wait(barrier, n - 1)

    def tables(d, owner):
        return [
            pltpu.make_async_remote_copy(
                src_ref=source, dst_ref=goal.at[owner], send_sem=table_send.at[d, i],
                recv_sem=table_recv.at[d, i], device_id={"surf": lax.rem(me + d, n)},
                device_id_type=MESH,
            )
            for i, (source, goal) in enumerate((
                (recv_list_ref.at[0], places_ref), (nb_ref, nbs_ref),
                (count_ref.at[0], counts_ref),
            ))
        ]

    def line_copy(owner, l, way, to):
        row = owner * lines + l
        return pltpu.make_async_remote_copy(
            src_ref=adjoints_ref.at[row], dst_ref=adjoints_ref.at[row],
            send_sem=send_sem.at[way, l], recv_sem=recv_sem.at[row],
            device_id={"surf": to}, device_id_type=MESH,
        )

    def across(k):
        return lax.rem(chip + k, chips) * 2 + core

    for d in range(1, n):
        for copy in tables(d, me):
            copy.start()
    for l in range(lines):
        for k in range(1, chips):
            line_copy(me, l, k, across(k)).start()
    for l in range(lines):
        line_copy(me, l, 0, partner).start()

    for s in range(n):
        for j in range(cap):
            places_ref[me, s, j] = recv_list_ref[0, s, j]
        counts_ref[me, s] = count_ref[0, s]
    for l in range(lines):
        nbs_ref[me, l] = nb_ref[l]

    eye = diagonal(size)

    def product(b):
        for load in loads(b):
            load.wait()
        value = -dot(inv_ref[b], couple_ref[b])
        main = jnp.sum(jnp.where(eye, value, 0.0), axis=0, keepdims=True)
        main = main.astype(BF16).astype(F32)
        codes, scale = coded(value - jnp.where(eye, main, 0.0))
        code_ref[b, :, :size] = codes.astype(I16)
        side_ref[b, 0:1, :size] = scale
        side_ref[b, 1:2, :size] = main
        rhs = rhs_ref[b // elems, b % elems]
        both_ref[b] = jnp.concatenate([rhs, rhs], axis=0).T

    def relay(l):
        for k in range(1, chips):
            source = across(k)
            line_copy(source, l, k, partner).wait_recv()
            line_copy(source, l, chips - 1 + k, partner).start()

    lax.fori_loop(0, stored, lambda b, _: (product(b), 0)[1], 0)

    for d in range(1, n):
        for copy in tables(d, lax.rem(me + n - d, n)):
            copy.wait_recv()
        for copy in tables(d, me):
            copy.wait_send()
    index_table(n, lines, elems, cap, plans, me, places_ref, nbs_ref, counts_ref,
                send_list_ref, index_ref, plan_ref)

    for l in range(lines):
        relay(l)
    for l in range(lines):
        line_copy(partner, l, 0, partner).wait_recv()
        for k in range(1, chips):
            other = across(k)
            line_copy(other + 1 - 2 * core, l, 0, partner).wait_recv()
            line_copy(me, l, k, other).wait_send()
            line_copy(other, l, chips - 1 + k, partner).wait_send()
        line_copy(me, l, 0, partner).wait_send()


def index_table(n, lines, elems, cap, plans, me, places, nbs, counts, sends, out_ref, plan_ref):
    stored = lines * elems
    room = n * cap
    for d in range(n):
        to = lax.rem(me + d, n)
        here = counts[me, to]
        for j in range(cap):
            used = j < here
            goal = jnp.where(used, places[to, me, j], 0)
            slot = d * cap + j
            out_ref[slot] = jnp.where(used, sends[0, to, j], 0)
            line = goal // elems
            out_ref[room + slot] = nbs[to, line]
            out_ref[2 * room + slot] = goal - line * elems
    for q in range(stored):
        value = jnp.int32(0)
        for d in range(n):
            source = lax.rem(me + n - d, n)
            for j in range(cap):
                hit = jnp.logical_and(j < counts[source, me], places[me, source, j] == q)
                value = jnp.where(hit, d * cap + j, value)
        out_ref[3 * room + q] = value

    best = jnp.int32(len(plans) - 1)
    most = []
    for d in range(n):
        value = counts[0, d]
        for s in range(1, n):
            value = jnp.maximum(value, counts[s, (s + d) % n])
        most.append(value)
    for p in reversed(range(len(plans) - 1)):
        fits = most[0] <= plans[p][0]
        for d in range(1, n):
            fits = jnp.logical_and(fits, most[d] <= plans[p][d])
        best = jnp.where(fits, p, best)
    plan_ref[0] = best


def gathered(n, cap, plans, recv_list, nb_line, send_count, send_list, adjoint_t, rhs_t,
             inv_block, couple_block):
    lines, elems, cols, size = adjoint_t.shape
    stored, wide = lines * elems, size + cols
    chips = n // 2
    vmem, hbm = pl.BlockSpec(memory_space=pltpu.VMEM), pl.BlockSpec(memory_space=pl.ANY)
    smem = pl.BlockSpec(memory_space=pltpu.SMEM)
    return pl.pallas_call(
        functools.partial(gather_kernel, n, cap, plans),
        out_shape=(
            jax.ShapeDtypeStruct((LANES,), I32),
            jax.ShapeDtypeStruct((1,), I32),
            jax.ShapeDtypeStruct((n * lines, size, elems * cols), BF16),
            jax.ShapeDtypeStruct((stored, size, 2 * cols), BF16),
            jax.ShapeDtypeStruct((stored, size, wide), I16),
            jax.ShapeDtypeStruct((stored, 2, wide), F32),
        ),
        in_specs=[hbm] * 8,
        out_specs=(smem, smem) + (vmem,) * 4,
        scratch_shapes=[
            pltpu.SMEM(recv_list.shape, I32),
            pltpu.SMEM(nb_line.shape, I32),
            pltpu.SMEM(send_count.shape, I32),
            pltpu.SMEM(send_list.shape, I32),
            pltpu.VMEM(adjoint_t.shape, BF16),
            pltpu.VMEM(rhs_t.shape, BF16),
            pltpu.SMEM((n, n, cap), I32),
            pltpu.SMEM((n, lines), I32),
            pltpu.SMEM((n, n), I32),
            pltpu.VMEM((stored, size, size), BF16),
            pltpu.VMEM((stored, size, size), BF16),
            pltpu.SemaphoreType.DMA((6,)),
            pltpu.SemaphoreType.DMA((stored, 2)),
            pltpu.SemaphoreType.DMA((n, 3)),
            pltpu.SemaphoreType.DMA((n, 3)),
            pltpu.SemaphoreType.DMA((2 * chips - 1, lines)),
            pltpu.SemaphoreType.DMA((n * lines,)),
        ],
        compiler_params=pltpu.CompilerParams(
            collective_id=0, has_side_effects=True, vmem_limit_bytes=54 << 20
        ),
    )(recv_list, nb_line, send_count, send_list, adjoint_t, rhs_t, inv_block, couple_block)


def sweep_kernel(
    n, n_line, cap, lines, elems, budgets, relays, holders,
    index_ref, inv_ref, face_ref, both_ref, adjoints_ref, code_ref, side_ref,
    result_hbm, result_ref, out_ref, out_side_ref, got_ref, got_side_ref, hi_ref, lo_ref,
    map_hi, map_lo, shift, going, coming, relay_ref,
    send_sem, recv_sem, go_sem, come_sem, leg_send, leg_recv, on_send, on_recv, done_sem,
):
    me, place = lax.axis_index("surf"), lax.axis_index("line")
    _, size, wide = code_ref.shape
    cols = wide - size
    room = n * cap
    body = wide - LANES
    half = size // 2
    inner, outer = jnp.maximum(place - 1, 0), jnp.minimum(place + 1, n_line - 1)
    top = n_line - 1

    barrier = pltpu.get_barrier_semaphore()
    for d in range(1, n):
        pl.semaphore_signal(
            barrier, inc=1, device_id={"surf": lax.rem(me + d, n)}, device_id_type=MESH
        )

    @pl.when(place < top)
    def _():
        pl.semaphore_signal(barrier, inc=1, device_id={"line": outer}, device_id_type=MESH)

    greeted = n - 1 + jnp.where(place > 0, 1, 0)
    core = lax.rem(me, 2)

    def on(at, core_only):
        here = place == at
        return here if core_only < 0 else jnp.logical_and(here, core == core_only)

    for far, mate, core_only in sorted({(far, mate, c) for far, _, mate, c in relays}):
        @pl.when(on(mate, core_only))
        def _():
            pl.semaphore_signal(
                barrier, inc=1, device_id={"surf": lax.rem(me + n // 2, n), "line": far},
                device_id_type=MESH,
            )

        @pl.when(on(far, core_only))
        def _():
            pl.semaphore_signal(barrier, inc=1, device_id={"line": mate}, device_id_type=MESH)

        greeted = greeted + jnp.where(
            jnp.logical_or(on(far, core_only), on(mate, core_only)), 1, 0
        )

    around = jnp.int32(0)
    for far, _, _, core_only in relays:
        around = around + jnp.where(on(far, core_only), 1, 0)
    held = jnp.logical_or(place == -1, place == -2)
    for mate in holders:
        held = jnp.logical_or(held, place == mate)

    upper = lax.broadcasted_iota(I32, (size, LANES), 1) >= cols
    upper_half = lax.broadcasted_iota(I32, (half, LANES), 1) >= cols
    upper_row = lax.broadcasted_iota(I32, (1, LANES), 1) >= cols
    eye = lax.broadcasted_iota(I32, (size, wide), 0) == lax.broadcasted_iota(
        I32, (size, wide), 1
    )

    def copies(d, slot):
        to = {"surf": lax.rem(me + d, n)}
        return (
            pltpu.make_async_remote_copy(
                src_ref=out_ref.at[slot], dst_ref=got_ref.at[slot],
                send_sem=send_sem.at[slot, 0], recv_sem=recv_sem.at[slot, 0],
                device_id=to, device_id_type=MESH,
            ),
            pltpu.make_async_remote_copy(
                src_ref=out_side_ref.at[slot], dst_ref=got_side_ref.at[slot],
                send_sem=send_sem.at[slot, 1], recv_sem=recv_sem.at[slot, 1],
                device_id=to, device_id_type=MESH,
            ),
        )

    def fill(slot):
        at = index_ref[slot]
        line, elem = index_ref[room + slot], index_ref[2 * room + slot]
        terms = dot(face_ref[at], adjoints_ref[line])
        terms = jnp.where(elem == 1, terms, pltpu.roll(terms, cols, 1))
        force = both_ref[at].astype(F32) - terms
        hi = force.astype(BF16).astype(F32)
        both = jnp.where(upper, hi, pltpu.roll(force - hi, cols, 1)).astype(BF16)
        moved = dot(inv_ref[at], both)
        moved = moved + pltpu.roll(moved, cols, 1)
        codes, scale = coded(moved)
        out_ref[slot, :, :body] = code_ref[at, :, :body]
        last = code_ref[at, :, body:].astype(I32)
        out_ref[slot, :, body:] = jnp.where(upper, codes, last).astype(I16)
        out_side_ref[slot, :, :body] = side_ref[at, :, :body]
        out_side_ref[slot, 0:1, body:] = jnp.where(upper_row, scale, side_ref[at, 0:1, body:])
        out_side_ref[slot, 1:2, body:] = side_ref[at, 1:2, body:]

    def decode(codes_at, sides_at, slot):
        value = codes_at[slot].astype(F32) * sides_at[slot, 0:1]
        value = value + jnp.where(eye, sides_at[slot, 1:2], 0.0)
        hi, lo = split(value)
        hi_ref[slot] = hi
        lo_ref[slot] = lo

    opposite = n // 2
    if n == 4:
        order = [(2, 1), (1, 2), (3, 3)]
    else:
        order = [(d, d) for d in sorted(range(1, n), key=lambda d: -min(d, n - d))]

    def pick(even, odd):
        return jnp.where(lax.rem(me, 2) == 0, even, odd)

    def first_leg(k, c):
        far, j, mate, _ = relays[k]
        part = pl.ds(c * half, half)
        return pltpu.make_async_remote_copy(
            src_ref=out_ref.at[opposite * cap + j, part], dst_ref=relay_ref.at[k, part],
            send_sem=leg_send.at[k, c], recv_sem=leg_recv.at[k, c],
            device_id={"surf": lax.rem(me + opposite, n), "line": mate}, device_id_type=MESH,
        )

    def second_leg(k, c):
        far, j, mate, _ = relays[k]
        part = pl.ds(c * half, half)
        return pltpu.make_async_remote_copy(
            src_ref=relay_ref.at[k, part], dst_ref=got_ref.at[opposite * cap + j, part],
            send_sem=on_send.at[k, c], recv_sem=on_recv.at[k, c],
            device_id={"line": far}, device_id_type=MESH,
        )

    def walk(offsets, visit):
        ends, total = [], 0
        for even, odd in offsets:
            total = total + pick(budgets[even], budgets[odd])
            ends.append(total)
        total = sum(budgets[even] for even, _ in offsets)

        def turn(i, _):
            d, start = pick(*offsets[-1]), ([0] + ends)[len(offsets) - 1]
            for p in reversed(range(len(offsets) - 1)):
                before = i < ends[p]
                d = jnp.where(before, pick(*offsets[p]), d)
                start = jnp.where(before, ([0] + ends)[p], start)
            visit(i, d, i - start)
            return 0

        lax.fori_loop(0, total, turn, 0)

    def direct(d, j):
        return jnp.logical_or(d != opposite, j >= around)

    def leave(i, d, j):
        slot = d * cap + j
        fill(slot)

        @pl.when(i == 0)
        def _():
            pl.semaphore_wait(barrier, greeted)

        @pl.when(d == 0)
        def _():
            decode(out_ref, out_side_ref, slot)

        @pl.when(jnp.logical_and(d > 0, jnp.logical_not(held)))
        def _():
            block, rows = copies(d, slot)
            rows.start()

            @pl.when(direct(d, j))
            def _():
                block.start()

            for k, (far, at, mate, core_only) in enumerate(relays):
                @pl.when(jnp.logical_and(on(far, core_only), slot == opposite * cap + at))
                def _():
                    first_leg(k, 0).start()
                    first_leg(k, 1).start()

    walk(order + [(0, 0)], leave)

    for c in range(2):
        for k, (far, j, mate, core_only) in enumerate(relays):
            @pl.when(on(mate, core_only))
            def _():
                first_leg(k, c).wait_recv()
                second_leg(k, c).start()

    if holders:
        @pl.when(held)
        def _():
            def release(_, d, j):
                for copy in copies(d, d * cap + j):
                    copy.start()

            walk(order, release)

    def arrive(_, d, j):
        slot = d * cap + j
        block, rows = copies(d, slot)
        rows.wait_recv()

        @pl.when(direct(d, j))
        def _():
            block.wait_recv()

        for k, (far, at, mate, core_only) in enumerate(relays):
            @pl.when(jnp.logical_and(on(far, core_only), slot == opposite * cap + at))
            def _():
                second_leg(k, 0).wait_recv()
                second_leg(k, 1).wait_recv()

        decode(got_ref, got_side_ref, slot)

    walk(order[::-1], arrive)

    def pass_on(l):
        return pltpu.make_async_remote_copy(
            src_ref=going.at[l], dst_ref=coming.at[l], send_sem=go_sem.at[l],
            recv_sem=come_sem.at[l], device_id={"line": inner}, device_id_type=MESH,
        )

    def carry(l, twice):
        packed = jnp.where(upper_half, twice[half:], twice[:half])
        most = jnp.maximum(jnp.max(jnp.abs(packed), axis=0, keepdims=True), TINY)
        power = jnp.minimum(jnp.ceil(jnp.log2(most) * 256.0), 32767.0)
        codes = jnp.round(packed * jnp.exp2(CARRY_BITS - power * (1.0 / 256.0)))
        going[l, :half] = codes.astype(I32).astype(I16)
        going[l, half:] = jnp.broadcast_to(power, (16, LANES)).astype(I32).astype(I16)

    def carried(l):
        power = coming[l, half:].astype(F32)[0:1]
        value = coming[l, :half].astype(F32) * jnp.exp2(power * (1.0 / 256.0) - CARRY_BITS)
        hi = value.astype(BF16).astype(F32)
        lo = value - hi
        hi_turn, lo_turn = pltpu.roll(hi, cols, 1), pltpu.roll(lo, cols, 1)
        pair = jnp.concatenate(
            [jnp.where(upper_half, lo_turn, hi), jnp.where(upper_half, lo, hi_turn)], axis=0
        ).astype(BF16)
        same = jnp.concatenate(
            [jnp.where(upper_half, hi_turn, hi), jnp.where(upper_half, hi, hi_turn)], axis=0
        ).astype(BF16)
        return pair, same

    def applied(hi, lo, pair, same):
        first = dot(hi, pair)
        return first + (pltpu.roll(first, cols, 1) + dot(lo, same))

    def doubled(tile):
        return jnp.where(upper, tile, pltpu.roll(tile, cols, 1))

    def compose(l):
        inside = index_ref[3 * room + l * elems]
        outside = index_ref[3 * room + l * elems + 1]
        in_hi, in_lo = hi_ref[inside][:, :size], lo_ref[inside][:, :size]
        far_hi, far_lo = hi_ref[outside], lo_ref[outside]
        whole = dot(in_hi, far_hi) + (dot(in_hi, far_lo) + dot(in_lo, far_hi))
        tile = whole[:, body:] + (
            hi_ref[inside][:, body:].astype(F32) + lo_ref[inside][:, body:].astype(F32)
        )
        m_hi, m_lo = split(whole)
        map_hi[l] = m_hi
        map_lo[l] = m_lo
        twice = doubled(tile)
        shift[l] = twice

        @pl.when(place == top)
        def _():
            carry(l, twice)
            pass_on(l).start()

    @pl.when(place == top)
    def _():
        coming[...] = jnp.zeros_like(coming)

    def step(l):
        pass_on(l).wait_recv()
        pair, same = carried(l)
        twice = shift[l] + applied(map_hi[l][:, :size], map_lo[l][:, :size], pair, same)

        @pl.when(place > 0)
        def _():
            carry(l, twice)
            pass_on(l).start()

        shift[l] = twice

    def leaving(l):
        return pltpu.make_async_copy(result_ref.at[l], result_hbm.at[l], done_sem.at[l])

    def finish(l):
        pair, same = carried(l)
        outside = index_ref[3 * room + l * elems + 1]
        far_hi, far_lo = hi_ref[outside], lo_ref[outside]
        first = doubled(far_hi[:, body:].astype(F32) + far_lo[:, body:].astype(F32))
        first = first + applied(far_hi[:, :size], far_lo[:, :size], pair, same)
        result_ref[l] = jnp.where(upper, first, shift[l]).astype(BF16).T
        leaving(l).start()

    def turn(i, _):
        early, late = place == top - 1, place == 0
        pairs_from = jnp.where(early, 0, jnp.where(late, lines, 3 * lines))
        paired = jnp.logical_and(i >= pairs_from, i < pairs_from + 2 * lines)
        stage = jnp.where(paired, pairs_from // lines + lax.rem(i, 2), i // lines)
        l = jnp.where(paired, (i - pairs_from) // 2, lax.rem(i, lines))

        @pl.when(stage == 0)
        def _():
            compose(l)

        @pl.when(jnp.logical_and(stage == 1, place < top))
        def _():
            step(l)

        @pl.when(stage == 2)
        def _():
            finish(l)

        return 0

    lax.fori_loop(0, 3 * lines, turn, 0)

    def finished(l, _):
        leaving(l).wait()
        return 0

    lax.fori_loop(0, lines, finished, 0)

    @pl.when(place > 0)
    def _():
        def gone(l, _):
            pass_on(l).wait_send()
            return 0

        lax.fori_loop(0, lines, gone, 0)

    for k, (far, j, mate, core_only) in enumerate(relays):
        @pl.when(on(far, core_only))
        def _():
            first_leg(k, 0).wait_send()
            first_leg(k, 1).wait_send()

        @pl.when(on(mate, core_only))
        def _():
            second_leg(k, 0).wait_send()
            second_leg(k, 1).wait_send()

    def left(_, d, j):
        block, rows = copies(d, d * cap + j)
        rows.wait_send()

        @pl.when(direct(d, j))
        def _():
            block.wait_send()

    walk(order, left)


def relays_of(n, n_line, budgets):
    if n != 4 or n_line != 8:
        return (), ()
    crossing = 2 * budgets[2] + budgets[1] + budgets[3]
    if budgets[2] < 2 or crossing < 8:
        return (), ()
    relays = ((7, 0, 1, -1),)
    if crossing > 8:
        relays += ((7, 1, 3, -1 if budgets[1] > budgets[2] else 1), (6, 0, 0, -1), (5, 0, 2, -1))
    return relays, (0, 1) if crossing > 8 else (1,)


def swept(n, n_line, cap, lines, elems, plan, budgets, index, inv, face, both, adjoints,
          codes, sides):
    stored, size, wide = codes.shape
    cols = wide - size
    vmem = pl.BlockSpec(memory_space=pltpu.VMEM)
    room = n * cap
    coded_blocks = pltpu.VMEM((room, size, wide), I16)
    side_rows = pltpu.VMEM((room, 2, wide), F32)
    parts = pltpu.VMEM((room, size, wide), BF16)
    maps = pltpu.VMEM((lines, size, wide), BF16)
    message = pltpu.VMEM((lines, size // 2 + 16, LANES), I16)
    relays, holders = relays_of(n, n_line, budgets)
    legs = pltpu.SemaphoreType.DMA((max(len(relays), 1), 2))
    return pl.pallas_call(
        functools.partial(
            sweep_kernel, n, n_line, cap, lines, elems, budgets, relays, holders
        ),
        out_shape=jax.ShapeDtypeStruct((lines, elems * cols, size), BF16),
        in_specs=[pl.BlockSpec(memory_space=pltpu.SMEM)] + [vmem] * 6,
        out_specs=pl.BlockSpec(memory_space=pl.ANY),
        scratch_shapes=[
            pltpu.VMEM((lines, elems * cols, size), BF16),
            coded_blocks, side_rows, coded_blocks, side_rows, parts, parts, maps, maps,
            pltpu.VMEM((lines, size, LANES), F32),
            message, message,
            pltpu.VMEM((max(len(relays), 1), size, wide), I16),
            pltpu.SemaphoreType.DMA((room, 2)),
            pltpu.SemaphoreType.DMA((room, 2)),
            pltpu.SemaphoreType.DMA((lines,)),
            pltpu.SemaphoreType.DMA((lines,)),
            legs, legs, legs, legs, pltpu.SemaphoreType.DMA((lines,)),
        ],
        compiler_params=pltpu.CompilerParams(
            collective_id=1 + plan, has_side_effects=True, vmem_limit_bytes=40 << 20
        ),
    )(index, inv, face, both, adjoints, codes, sides)


def plans_of(n, cap):
    plans = []
    if n == 4 and cap % 2 == 0:
        for empty in (0, 2, 3):
            for double in range(n):
                if double != empty:
                    plans.append(tuple(
                        cap if d == double else 0 if d == empty else cap // 2
                        for d in range(n)
                    ))
    return plans + [(cap,) * n]


def per_device(n_surf, n_line, inv_block, couple_block, face_block, rhs, adjoint_prev,
               nb_line, send_list, send_count, recv_list):
    lines, elems, size, _ = inv_block.shape
    cols = rhs.shape[3]
    cap = send_list.shape[2]
    plans = plans_of(n_surf, cap)
    index, plan, adjoints, both, codes, sides = gathered(
        n_surf, cap, plans, recv_list, nb_line, send_count, send_list,
        jnp.swapaxes(adjoint_prev, 2, 3), jnp.swapaxes(rhs, 2, 3), inv_block, couple_block,
    )
    inv = inv_block.reshape(lines * elems, size, size)
    face = face_block.reshape(lines * elems, size, size)

    def branch(p):
        return lambda: swept(
            n_surf, n_line, cap, lines, elems, p, plans[p], index, inv, face, both, adjoints,
            codes, sides,
        )

    if len(plans) > 1:
        result = lax.switch(plan[0], [branch(p) for p in range(len(plans))])
    else:
        result = branch(0)()
    return jnp.swapaxes(result.reshape(lines, elems, cols, size), 2, 3)


def solution(mesh):
    whole = P("surf", "line", None, None)
    in_specs = (
        whole, whole, whole, whole, whole,
        P("surf"), P("surf", None, None), P("surf", None), P("surf", None, None),
    )
    body = functools.partial(per_device, mesh.shape["surf"], mesh.shape["line"])
    return jax.shard_map(
        body, mesh=mesh, in_specs=in_specs, out_specs=whole, check_vma=False
    )
```
